32 devices in a mesh: groups: 2 (over y), adapter: 8 (over z, x), tensor: 2 (over core).
Axes of the slice: x: 2, y: 2, z: 4, core: 2. Of those that a mesh axis runs over, the one named last changes fastest.
Arguments:
- tokens: bfloat16 [2048, 5120], P(('groups', 'adapter'), 'tensor'), parts along dimension 0, may hold values from -6 to 6
- cotangent: bfloat16 [2048, 5120], P(('groups', 'adapter'), 'tensor'), parts along dimension 0, may hold values from -3 to 3
- down_adapter: bfloat16 [8, 64, 5120], P('adapter', None, 'tensor'), may hold values from -0.078125 to 0.078125
- up_adapter: bfloat16 [8, 64, 5120], P('adapter', None, 'tensor'), may hold values from -0.75 to 0.75
- token_lists: int32 [16, 256], P('groups'), parts along dimension 0, may hold values from 0 to 1023, as said below
- gating: float32 [16, 256], P(('groups', 'adapter')), parts along dimension 0, may hold values from 0.25 to 1
Outputs:
- branch_out: bfloat16 [2048, 5120], P(('groups', 'adapter'), 'tensor'), parts along dimension 0
- input_grad: bfloat16 [2048, 5120], P(('groups', 'adapter'), 'tensor'), parts along dimension 0
- down_grad: bfloat16 [16, 64, 5120], P(('groups', 'adapter'), None, 'tensor'), parts along dimension 0
- up_grad: bfloat16 [16, 64, 5120], P(('groups', 'adapter'), None, 'tensor'), parts along dimension 0
The draws below stay inside these ranges and needn't reach their ends.
There are 2 independent parts, one for each index of `groups`. The reference program is written for one: setup_inputs(seed, part) draws one part's arguments, and reference() takes and returns one part's arrays. A program takes and returns all parts, laid end to end along the dimension named above; an argument that names none is the same for every part. Nothing has to cross between parts.
Inputs may be any that keep to these rules, and one draw needn't show every extreme that they name: `token_lists`: row e holds 256 distinct tokens, grouped by the index of adapter that holds them (tokens t with t // 128 equal), in increasing order of that index; every index supplies between 16 and 48 tokens to every expert, and for every expert some index supplies exactly 48.
All inputs are finite; a program needn't handle non-finite values.
Results may differ from the reference program's by a relative error of at most 0.0064.
Values may be sent and summed in bfloat16 or wider, within the bound.
No kernel may reach another device: no remote copies, remote signals or barrier semaphores. Data moves between devices by JAX's collectives and lax.ppermute only.
A program may use at most 64 MiB of HBM per device.

```python
import math
import jax
import jax.numpy as jnp
from jax import lax

D = 5120
R = 64
TOK_DEV = 128
EXPERTS = 8
TOKENS = 1024
CAP = 256
SLOT = 48
N_ADAPTER = 8


def draw_token_lists(key, part):
    key = jax.random.fold_in(key, 7)
    pair_key, spread_key, selection_key = jax.random.split(key, 3)
    owners = N_ADAPTER
    mean_rows = CAP // owners
    half_rows = mean_rows // 2
    order_scores = jax.random.randint(pair_key, (EXPERTS, owners), 0, 1 << 20) * owners + jnp.arange(owners)[None, :]
    ranking = jnp.argsort(order_scores, axis=1)
    spread = jax.random.randint(spread_key, (EXPERTS, owners // 2), 0, half_rows + 1)
    spread = spread.at[:, 0].set(half_rows)
    by_rank = jnp.stack([spread, -spread], axis=2).reshape(EXPERTS, owners)
    inverse = jnp.argsort(ranking, axis=1)
    counts = mean_rows + jnp.take_along_axis(by_rank, inverse, axis=1)
    pick_scores = jax.random.randint(selection_key, (EXPERTS, owners, TOK_DEV), 0, 1 << 16) * TOK_DEV + jnp.arange(TOK_DEV)[None, None, :]
    chosen = jnp.argsort(pick_scores, axis=2)[:, :, :SLOT]
    global_rows = chosen + (jnp.arange(owners) * TOK_DEV)[None, :, None]
    live_slot = jnp.arange(SLOT)[None, None, :] < counts[:, :, None]
    flat_rows = global_rows.reshape(EXPERTS, owners * SLOT)
    flat_live = live_slot.reshape(EXPERTS, owners * SLOT)
    sort_keys = jnp.where(flat_live, 0, owners * SLOT) + jnp.arange(owners * SLOT)[None, :]
    keep_order = jnp.argsort(sort_keys, axis=1)[:, :CAP]
    return jnp.take_along_axis(flat_rows, keep_order, axis=1).astype(jnp.int32)


def shard_levels(rng, dims, cuts, smallest, largest):
    level = 1.0
    for position, blocks in cuts:
        heights = jax.random.uniform(jax.random.fold_in(jax.random.fold_in(rng, 6), position), (blocks,), jnp.float32, smallest / len(cuts), largest / len(cuts))
        level = level * jnp.repeat(jnp.exp(heights), dims[position] // blocks).reshape((-1,) + (1,) * (len(dims) - 1 - position))
    return level


def bell_draw(key, extent, deviation, limit, cuts=(), held_as=jnp.bfloat16):
    entries = jax.random.normal(key, extent, jnp.float32) * deviation
    if len(cuts) > 0:
        entries = shard_levels(key, extent, cuts, -0.22, 0.18) * entries
    return jnp.clip(entries, min=-limit, max=limit).astype(held_as)


def setup_inputs(seed: int = 0, part: int = 0) -> dict:
    key_list = jax.random.split(jax.random.key(seed), 7)
    part_keys = jax.random.split(jax.random.fold_in(key_list[6], part), 7)
    tokens = bell_draw(part_keys[0], (TOKENS, D), 1.0, 6.0, ((0, 8), (1, 2)))
    cotangent = bell_draw(part_keys[1], (TOKENS, D), 0.5, 3.0, ((0, 8), (1, 2)))
    down_adapter = bell_draw(key_list[2], (EXPERTS, R, D), D ** -0.5, 0.078125, ((0, 8), (2, 2)))
    up_adapter = bell_draw(key_list[3], (EXPERTS, R, D), R ** -0.5, 0.75, ((0, 8), (2, 2)))
    token_lists = draw_token_lists(jax.random.fold_in(jax.random.fold_in(key_list[6], part), 71), part)
    gating = jnp.clip(jnp.exp(math.log(1.0) - 1.3862944 * jax.random.uniform(part_keys[5], (EXPERTS, CAP), jnp.float32) ** shard_levels(part_keys[5], (EXPERTS, CAP), ((0, 8),), -0.2, 0.2)), 0.25, 1.0)
    return {"tokens": tokens, "cotangent": cotangent, "down_adapter": down_adapter, "up_adapter": up_adapter, "token_lists": token_lists, "gating": gating}


adapter_scale_factor = 2.0


def contract_last(left_op, right_op):
    return lax.dot_general(left_op, right_op, (((1,), (1,)), ((), ())), preferred_element_type=jnp.float32)


def contract_first(left_op, right_op):
    return lax.dot_general(left_op, right_op, (((0,), (0,)), ((), ())), preferred_element_type=jnp.float32)


def reference(tokens, cotangent, down_adapter, up_adapter, token_lists, gating):
    def expert(carry, item):
        branch, grad_in = carry
        row_index, router_gate_row, down_matrix, up_matrix = item
        gathered = jnp.take(tokens, row_index, axis=0)
        cot_rows = jnp.take(cotangent, row_index, axis=0)
        low_rank = contract_last(gathered, down_matrix).astype(jnp.bfloat16)
        scale_factors = (adapter_scale_factor * router_gate_row)[:, None]
        weighted = (scale_factors * cot_rows.astype(jnp.float32)).astype(jnp.bfloat16)
        out_rows = (scale_factors * jnp.dot(low_rank, up_matrix, preferred_element_type=jnp.float32)).astype(jnp.bfloat16)
        out_rows = lax.optimization_barrier(out_rows)
        low_grad = contract_last(weighted, up_matrix).astype(jnp.bfloat16)
        back_rows = jnp.dot(low_grad, down_matrix, preferred_element_type=jnp.float32).astype(jnp.bfloat16)
        back_rows = lax.optimization_barrier(back_rows)
        branch = branch.at[row_index].add(out_rows.astype(jnp.float32))
        grad_in = grad_in.at[row_index].add(back_rows.astype(jnp.float32))
        down_term = (contract_first(low_grad, gathered) / CAP).astype(jnp.bfloat16)
        up_term = (contract_first(low_rank, weighted) / CAP).astype(jnp.bfloat16)
        return (branch, grad_in), (down_term, up_term)

    start = (jnp.zeros((TOKENS, D), jnp.float32), jnp.zeros((TOKENS, D), jnp.float32))
    (branch, grad_in), (down_grad, up_grad) = lax.scan(expert, start, (token_lists, gating, down_adapter, up_adapter))
    return branch.astype(jnp.bfloat16), grad_in.astype(jnp.bfloat16), down_grad, up_grad
```

```python
import jax
import jax.numpy as jnp
from jax import lax
from jax.sharding import PartitionSpec as P

adapter_scale_factor = 2.0


def contract_last(left_op, right_op):
    return lax.dot_general(
        left_op, right_op, (((1,), (1,)), ((), ())), preferred_element_type=jnp.float32
    )


def contract_first(left_op, right_op):
    return lax.dot_general(
        left_op, right_op, (((0,), (0,)), ((), ())), preferred_element_type=jnp.float32
    )


def gather_rows(source_rows, local_index, live_slot):
    taken_rows = jnp.take(source_rows, local_index.reshape(-1), axis=0)
    taken_rows = taken_rows.reshape(local_index.shape + (source_rows.shape[1],))
    return jnp.where(live_slot[:, :, None], taken_rows, jnp.zeros_like(taken_rows))


def combine(onehot, returned):
    flat_rows = returned.reshape(-1, returned.shape[-1])
    return jnp.dot(onehot, flat_rows, preferred_element_type=jnp.float32).astype(jnp.bfloat16)


def by_rows(tokens, cotangent, down_adapter, up_adapter, token_lists, gating):
    owners = lax.axis_size("adapter")
    my_index = lax.axis_index("adapter")
    tok_local = tokens.shape[0]
    half_width = tokens.shape[1]
    capacity = gating.shape[1]
    slot_count = 3 * capacity // (2 * owners)
    slot_ids = jnp.arange(slot_count, dtype=jnp.int32)
    source = token_lists // tok_local
    sent_count = jnp.sum((source == my_index).astype(jnp.int32), axis=1)
    sent_start = jnp.sum((source < my_index).astype(jnp.int32), axis=1)
    live_send = slot_ids[None, :] < sent_count[:, None]
    position = jnp.minimum(sent_start[:, None] + slot_ids[None, :], capacity - 1)
    local_index = jnp.take_along_axis(token_lists, position, axis=1) - my_index * tok_local
    local_index = jnp.where(live_send, local_index, 0)
    outgoing_rows = gather_rows(tokens, local_index, live_send)
    cot_send = gather_rows(cotangent, local_index, live_send)
    token_ids = jnp.arange(tok_local, dtype=jnp.int32)
    onehot = ((token_ids[:, None] == local_index.reshape(1, -1)) & live_send.reshape(1, -1)).astype(
        jnp.bfloat16
    )
    own_list = lax.dynamic_slice_in_dim(token_lists, my_index, 1, 0)[0]
    own_source = own_list // tok_local
    peer_ids = jnp.arange(owners, dtype=jnp.int32)
    recv_count = jnp.sum((own_source[None, :] == peer_ids[:, None]).astype(jnp.int32), axis=1)
    received_offset = jnp.sum((own_source[None, :] < peer_ids[:, None]).astype(jnp.int32), axis=1)
    active_received = slot_ids[None, :] < recv_count[:, None]
    gate_pos = jnp.minimum(received_offset[:, None] + slot_ids[None, :], capacity - 1)
    gate_slot_values = jnp.take(gating[0], gate_pos.reshape(-1)).reshape(gate_pos.shape)
    scale_factors = (
        adapter_scale_factor * jnp.where(active_received, gate_slot_values, 0.0)
    ).reshape(-1, 1)
    down_matrix = down_adapter[0]
    up_matrix = up_adapter[0]
    flat_shape = (owners * slot_count, half_width)
    block_shape = (owners, slot_count, half_width)
    row_recv = lax.all_to_all(outgoing_rows, "adapter", split_axis=0, concat_axis=0, tiled=True)
    rows_in = row_recv.reshape(flat_shape)
    low_rank = lax.psum(contract_last(rows_in, down_matrix), "tensor").astype(jnp.bfloat16)
    out_rows = (
        scale_factors * jnp.dot(low_rank, up_matrix, preferred_element_type=jnp.float32)
    ).astype(jnp.bfloat16)
    out_back = lax.all_to_all(
        out_rows.reshape(block_shape), "adapter", split_axis=0, concat_axis=0, tiled=True
    )
    cot_recv = lax.all_to_all(cot_send, "adapter", split_axis=0, concat_axis=0, tiled=True)
    weighted = (scale_factors * cot_recv.reshape(flat_shape)).astype(jnp.bfloat16)
    low_grad = lax.psum(contract_last(weighted, up_matrix), "tensor").astype(jnp.bfloat16)
    back_rows = jnp.dot(low_grad, down_matrix, preferred_element_type=jnp.float32).astype(
        jnp.bfloat16
    )
    grad_back = lax.all_to_all(
        back_rows.reshape(block_shape), "adapter", split_axis=0, concat_axis=0, tiled=True
    )
    branch_out = combine(onehot, out_back)
    input_grad = combine(onehot, grad_back)
    down_grad = (contract_first(low_grad, rows_in) / capacity).astype(jnp.bfloat16)[None]
    up_grad = (contract_first(low_rank, weighted) / capacity).astype(jnp.bfloat16)[None]
    return (branch_out, input_grad, down_grad, up_grad)


PLACES = 4


def on_line(pairs):
    return [(2 * a + side, 2 * b + side) for a, b in pairs for side in (0, 1)]


RISE = on_line([(0, 1), (1, 2), (2, 3)])
FALL = on_line([(1, 0), (2, 1), (3, 2)])
RISE_OUT = on_line([(1, 2), (2, 3)])
FALL_OUT = on_line([(2, 1), (1, 0)])
TO_ENDS = on_line([(2, 3), (1, 0)])
FROM_ENDS = on_line([(3, 2), (0, 1)])
RISE_IN = on_line([(0, 1), (1, 2)])
FALL_IN = on_line([(3, 2), (2, 1)])
TWO_APART = on_line([(0, 2), (1, 3), (2, 0), (3, 1)])
END_TO_END = on_line([(0, 3), (3, 0)])
PARTNER = [(2 * a + side, 2 * a + 1 - side) for a in range(PLACES) for side in (0, 1)]


def move(value, pairs):
    return lax.ppermute(value, "adapter", pairs)


def spread(matrix, high):
    below = move(matrix, RISE)
    above = move(matrix, FALL)
    rising = move(below, RISE_OUT)
    falling = move(above, FALL_OUT)
    second = jnp.where(high, rising, falling)
    third = move(second, TO_ENDS)
    return matrix, below, above, second, third


def collect(parts):
    own, below, above, second, third = parts
    half = jnp.bfloat16
    back = move(third.astype(half), FROM_ENDS)
    second = (second + back.astype(jnp.float32)).astype(half)
    falling = move(second, FALL_IN)
    rising = move(second, RISE_IN)
    below = move((below + falling.astype(jnp.float32)).astype(half), FALL)
    above = move((above + rising.astype(jnp.float32)).astype(half), RISE)
    return own + below.astype(jnp.float32) + above.astype(jnp.float32)


def both_cores(partial):
    return partial + lax.ppermute(partial, "tensor", [(0, 1), (1, 0)])


def by_pairs(tokens, cotangent, down_adapter, up_adapter, token_lists, gating):
    me = lax.axis_index("adapter")
    place = me // 2
    high = place >= 2
    tok_local = tokens.shape[0]
    capacity = gating.shape[1]
    down_matrix = down_adapter[0]
    up_matrix = up_adapter[0]
    rank = down_matrix.shape[0]

    gates = (
        gating,
        move(gating, RISE),
        move(gating, FALL),
        move(gating, TWO_APART),
        move(gating, END_TO_END),
    )
    experts = jnp.stack(
        [
            me,
            jnp.maximum(me - 2, 0),
            jnp.minimum(me + 2, 2 * PLACES - 1),
            jnp.where(high, me - 4, me + 4),
            2 * (PLACES - 1) - 2 * place + me % 2,
        ]
    )
    lists = jnp.take(token_lists, experts, axis=0)
    gate_rows = adapter_scale_factor * jnp.concatenate(gates, axis=0)
    token_ids = jnp.arange(tok_local, dtype=jnp.int32)
    ids = jnp.concatenate([me * tok_local + token_ids, (me ^ 1) * tok_local + token_ids])
    taken = ids[:, None, None] == lists[None, :, :]
    scale = jnp.sum(jnp.where(taken, gate_rows[None, :, :], 0.0), axis=2)
    scale = jnp.repeat(scale, rank, axis=1)

    tokens2 = jnp.concatenate([tokens, move(tokens, PARTNER)], axis=0)
    downs = spread(down_matrix, high)
    cot2 = jnp.concatenate([cotangent, move(cotangent, PARTNER)], axis=0)
    ups = spread(up_matrix, high)

    down_all = jnp.concatenate(downs, axis=0)
    up_all = jnp.concatenate(ups, axis=0)
    low = (scale * both_cores(contract_last(tokens2, down_all))).astype(jnp.bfloat16)
    low_back = (scale * both_cores(contract_last(cot2, up_all))).astype(jnp.bfloat16)

    def parts(weights, rows):
        return tuple(
            contract_first(weights[:, k * rank : (k + 1) * rank], rows) for k in range(5)
        )

    up_grad = collect(parts(low, cot2))
    down_grad = collect(parts(low_back, tokens2))

    def outward(weights, matrix):
        theirs = jnp.dot(weights[tok_local:], matrix, preferred_element_type=jnp.float32)
        back = move(theirs.astype(jnp.bfloat16), PARTNER)
        mine = jnp.dot(weights[:tok_local], matrix, preferred_element_type=jnp.float32)
        return (mine + back.astype(jnp.float32)).astype(jnp.bfloat16)

    branch_out = outward(low, up_all)
    input_grad = outward(low_back, down_all)
    down_grad = (down_grad / capacity).astype(jnp.bfloat16)[None]
    up_grad = (up_grad / capacity).astype(jnp.bfloat16)[None]
    return (branch_out, input_grad, down_grad, up_grad)


def local(*args):
    plan = by_pairs if lax.axis_size("adapter") == 2 * PLACES else by_rows
    return plan(*args)


def solution(mesh):
    in_specs = (
        P(("groups", "adapter"), "tensor"),
        P(("groups", "adapter"), "tensor"),
        P("adapter", None, "tensor"),
        P("adapter", None, "tensor"),
        P("groups", None),
        P(("groups", "adapter"), None),
    )
    out_specs = (
        P(("groups", "adapter"), "tensor"),
        P(("groups", "adapter"), "tensor"),
        P(("groups", "adapter"), None, "tensor"),
        P(("groups", "adapter"), None, "tensor"),
    )
    return jax.shard_map(local, mesh=mesh, in_specs=in_specs, out_specs=out_specs, check_vma=False)
```

```python
import jax
import jax.numpy as jnp
from jax import lax
from jax.sharding import PartitionSpec as P

adapter_scale_factor = 2.0


def contract_last(left_op, right_op):
    return lax.dot_general(
        left_op, right_op, (((1,), (1,)), ((), ())), preferred_element_type=jnp.float32
    )


def contract_first(left_op, right_op):
    return lax.dot_general(
        left_op, right_op, (((0,), (0,)), ((), ())), preferred_element_type=jnp.float32
    )


def gather_rows(source_rows, local_index, live_slot):
    taken_rows = jnp.take(source_rows, local_index.reshape(-1), axis=0)
    taken_rows = taken_rows.reshape(local_index.shape + (source_rows.shape[1],))
    return jnp.where(live_slot[:, :, None], taken_rows, jnp.zeros_like(taken_rows))


def combine(onehot, returned):
    flat_rows = returned.reshape(-1, returned.shape[-1])
    return jnp.dot(onehot, flat_rows, preferred_element_type=jnp.float32).astype(jnp.bfloat16)


def by_rows(tokens, cotangent, down_adapter, up_adapter, token_lists, gating):
    owners = lax.axis_size("adapter")
    my_index = lax.axis_index("adapter")
    tok_local = tokens.shape[0]
    half_width = tokens.shape[1]
    capacity = gating.shape[1]
    slot_count = 3 * capacity // (2 * owners)
    slot_ids = jnp.arange(slot_count, dtype=jnp.int32)
    source = token_lists // tok_local
    sent_count = jnp.sum((source == my_index).astype(jnp.int32), axis=1)
    sent_start = jnp.sum((source < my_index).astype(jnp.int32), axis=1)
    live_send = slot_ids[None, :] < sent_count[:, None]
    position = jnp.minimum(sent_start[:, None] + slot_ids[None, :], capacity - 1)
    local_index = jnp.take_along_axis(token_lists, position, axis=1) - my_index * tok_local
    local_index = jnp.where(live_send, local_index, 0)
    outgoing_rows = gather_rows(tokens, local_index, live_send)
    cot_send = gather_rows(cotangent, local_index, live_send)
    token_ids = jnp.arange(tok_local, dtype=jnp.int32)
    onehot = ((token_ids[:, None] == local_index.reshape(1, -1)) & live_send.reshape(1, -1)).astype(
        jnp.bfloat16
    )
    own_list = lax.dynamic_slice_in_dim(token_lists, my_index, 1, 0)[0]
    own_source = own_list // tok_local
    peer_ids = jnp.arange(owners, dtype=jnp.int32)
    recv_count = jnp.sum((own_source[None, :] == peer_ids[:, None]).astype(jnp.int32), axis=1)
    received_offset = jnp.sum((own_source[None, :] < peer_ids[:, None]).astype(jnp.int32), axis=1)
    active_received = slot_ids[None, :] < recv_count[:, None]
    gate_pos = jnp.minimum(received_offset[:, None] + slot_ids[None, :], capacity - 1)
    gate_slot_values = jnp.take(gating[0], gate_pos.reshape(-1)).reshape(gate_pos.shape)
    scale_factors = (
        adapter_scale_factor * jnp.where(active_received, gate_slot_values, 0.0)
    ).reshape(-1, 1)
    down_matrix = down_adapter[0]
    up_matrix = up_adapter[0]
    flat_shape = (owners * slot_count, half_width)
    block_shape = (owners, slot_count, half_width)
    row_recv = lax.all_to_all(outgoing_rows, "adapter", split_axis=0, concat_axis=0, tiled=True)
    rows_in = row_recv.reshape(flat_shape)
    low_rank = lax.psum(contract_last(rows_in, down_matrix), "tensor").astype(jnp.bfloat16)
    out_rows = (
        scale_factors * jnp.dot(low_rank, up_matrix, preferred_element_type=jnp.float32)
    ).astype(jnp.bfloat16)
    out_back = lax.all_to_all(
        out_rows.reshape(block_shape), "adapter", split_axis=0, concat_axis=0, tiled=True
    )
    cot_recv = lax.all_to_all(cot_send, "adapter", split_axis=0, concat_axis=0, tiled=True)
    weighted = (scale_factors * cot_recv.reshape(flat_shape)).astype(jnp.bfloat16)
    low_grad = lax.psum(contract_last(weighted, up_matrix), "tensor").astype(jnp.bfloat16)
    back_rows = jnp.dot(low_grad, down_matrix, preferred_element_type=jnp.float32).astype(
        jnp.bfloat16
    )
    grad_back = lax.all_to_all(
        back_rows.reshape(block_shape), "adapter", split_axis=0, concat_axis=0, tiled=True
    )
    branch_out = combine(onehot, out_back)
    input_grad = combine(onehot, grad_back)
    down_grad = (contract_first(low_grad, rows_in) / capacity).astype(jnp.bfloat16)[None]
    up_grad = (contract_first(low_rank, weighted) / capacity).astype(jnp.bfloat16)[None]
    return (branch_out, input_grad, down_grad, up_grad)


PLACES = 4


def on_line(pairs):
    return [(2 * a + side, 2 * b + side) for a, b in pairs for side in (0, 1)]


def xor_line(bit):
    return on_line([(a, a ^ bit) for a in range(PLACES)])


RISE = on_line([(0, 1), (1, 2), (2, 3)])
FALL = on_line([(1, 0), (2, 1), (3, 2)])
FROM_ENDS = on_line([(3, 2), (0, 1)])
RISE_IN = on_line([(0, 1), (1, 2)])
FALL_IN = on_line([(3, 2), (2, 1)])
PARTNER = [(2 * a + side, 2 * a + 1 - side) for a in range(PLACES) for side in (0, 1)]
SWAP = [(0, 1), (1, 0)]
OWNERS = 2 * PLACES
FAR = xor_line(2) + [(OWNERS + a, OWNERS + b) for a, b in xor_line(3)]


def move(value, pairs):
    return lax.ppermute(value, "adapter", pairs)


def after(value, earlier):
    return lax.optimization_barrier((value, earlier))[0]


def collect(weights, rows):
    own, third, second, below, above = weights
    half = jnp.bfloat16
    back = move(contract_first(third, rows).astype(half), FROM_ENDS)
    second = (contract_first(second, rows) + back.astype(jnp.float32)).astype(half)
    falling = move(second, FALL_IN)
    rising = move(second, RISE_IN)
    below = move((contract_first(below, rows) + falling.astype(jnp.float32)).astype(half), FALL)
    above = move((contract_first(above, rows) + rising.astype(jnp.float32)).astype(half), RISE)
    return contract_first(own, rows) + below.astype(jnp.float32) + above.astype(jnp.float32)


def both_cores(partial):
    return partial + lax.ppermute(partial, "tensor", SWAP)


def by_pairs(tokens, cotangent, down_adapter, up_adapter, token_lists, gating):
    me = lax.axis_index("adapter")
    first_group = lax.axis_index("groups") == 0
    place = me // 2
    odd = place % 2 == 1
    tok_local = tokens.shape[0]
    capacity = gating.shape[1]
    down_matrix = down_adapter[0]
    up_matrix = up_adapter[0]
    rank = down_matrix.shape[0]

    far_down = lax.ppermute(down_matrix, ("groups", "adapter"), FAR)
    near_down = move(down_matrix, xor_line(1))
    tokens2 = move(tokens, PARTNER)
    far_up = lax.ppermute(after(up_matrix, far_down), ("groups", "adapter"), FAR)
    cross_down = lax.ppermute(far_down, "groups", SWAP)
    near_up = move(after(up_matrix, near_down), xor_line(1))
    cot2 = move(after(cotangent, tokens2), PARTNER)
    later = after(gating, far_down)
    gates = [gating, move(later, xor_line(1)), move(later, xor_line(2)), move(later, xor_line(3))]
    cross_up = lax.ppermute(far_up, "groups", SWAP)

    far_bit = jnp.where(first_group, 2, 3)
    experts = jnp.stack([me, me ^ 2, me ^ (2 * far_bit), me ^ (2 * (far_bit ^ 1))])
    lists = jnp.take(token_lists, experts, axis=0)
    far_gate = jnp.where(first_group, gates[2], gates[3])
    cross_gate = jnp.where(first_group, gates[3], gates[2])
    gate_rows = adapter_scale_factor * jnp.concatenate([gates[0], gates[1], far_gate, cross_gate])
    token_ids = jnp.arange(tok_local, dtype=jnp.int32)
    ids = jnp.concatenate([me * tok_local + token_ids, (me ^ 1) * tok_local + token_ids])
    taken = ids[:, None, None] == lists[None, :, :]
    scale = jnp.sum(jnp.where(taken, gate_rows[None, :, :], 0.0), axis=2)
    scale = jnp.repeat(scale, rank, axis=1)

    tokens2 = jnp.concatenate([tokens, tokens2], axis=0)
    cot2 = jnp.concatenate([cotangent, cot2], axis=0)
    down_all = jnp.concatenate([down_matrix, near_down, far_down, cross_down], axis=0)
    up_all = jnp.concatenate([up_matrix, near_up, far_up, cross_up], axis=0)

    def low_rank(rows, matrices):
        return (scale * both_cores(contract_last(rows, matrices))).astype(jnp.bfloat16)

    def for_line(low):
        own, near, far, cross = (low[:, k * rank : (k + 1) * rank] for k in range(4))
        second = jnp.where(first_group, far, cross)
        third = jnp.where(first_group, cross, far)
        below = jnp.where(odd, near, third)
        above = jnp.where(odd, third, near)
        return own, third, second, below, above

    def outward(weights, matrix):
        theirs = jnp.dot(weights[tok_local:], matrix, preferred_element_type=jnp.float32)
        back = move(theirs.astype(jnp.bfloat16), PARTNER)
        mine = jnp.dot(weights[:tok_local], matrix, preferred_element_type=jnp.float32)
        return (mine + back.astype(jnp.float32)).astype(jnp.bfloat16)

    low = low_rank(tokens2, down_all)
    up_grad = collect(for_line(low), cot2)
    low_back = low_rank(cot2, up_all)
    down_grad = collect(for_line(low_back), tokens2)
    branch_out = outward(low, up_all)
    input_grad = outward(low_back, down_all)
    down_grad = (down_grad / capacity).astype(jnp.bfloat16)[None]
    up_grad = (up_grad / capacity).astype(jnp.bfloat16)[None]
    return (branch_out, input_grad, down_grad, up_grad)


def local(*args):
    fits = lax.axis_size("adapter") == OWNERS and lax.axis_size("groups") == 2
    plan = by_pairs if fits else by_rows
    return plan(*args)


def solution(mesh):
    in_specs = (
        P(("groups", "adapter"), "tensor"),
        P(("groups", "adapter"), "tensor"),
        P("adapter", None, "tensor"),
        P("adapter", None, "tensor"),
        P("groups", None),
        P(("groups", "adapter"), None),
    )
    out_specs = (
        P(("groups", "adapter"), "tensor"),
        P(("groups", "adapter"), "tensor"),
        P(("groups", "adapter"), None, "tensor"),
        P(("groups", "adapter"), None, "tensor"),
    )
    return jax.shard_map(local, mesh=mesh, in_specs=in_specs, out_specs=out_specs, check_vma=False)
```

```python
import jax
import jax.numpy as jnp
from jax import lax
from jax.sharding import PartitionSpec as P

adapter_scale_factor = 2.0


def contract_last(left_op, right_op):
    return lax.dot_general(
        left_op, right_op, (((1,), (1,)), ((), ())), preferred_element_type=jnp.float32
    )


def contract_first(left_op, right_op):
    return lax.dot_general(
        left_op, right_op, (((0,), (0,)), ((), ())), preferred_element_type=jnp.float32
    )


def gather_rows(source_rows, local_index, live_slot):
    taken_rows = jnp.take(source_rows, local_index.reshape(-1), axis=0)
    taken_rows = taken_rows.reshape(local_index.shape + (source_rows.shape[1],))
    return jnp.where(live_slot[:, :, None], taken_rows, jnp.zeros_like(taken_rows))


def combine(onehot, returned):
    flat_rows = returned.reshape(-1, returned.shape[-1])
    return jnp.dot(onehot, flat_rows, preferred_element_type=jnp.float32).astype(jnp.bfloat16)


def by_rows(tokens, cotangent, down_adapter, up_adapter, token_lists, gating):
    owners = lax.axis_size("adapter")
    my_index = lax.axis_index("adapter")
    tok_local = tokens.shape[0]
    half_width = tokens.shape[1]
    capacity = gating.shape[1]
    slot_count = 3 * capacity // (2 * owners)
    slot_ids = jnp.arange(slot_count, dtype=jnp.int32)
    source = token_lists // tok_local
    sent_count = jnp.sum((source == my_index).astype(jnp.int32), axis=1)
    sent_start = jnp.sum((source < my_index).astype(jnp.int32), axis=1)
    live_send = slot_ids[None, :] < sent_count[:, None]
    position = jnp.minimum(sent_start[:, None] + slot_ids[None, :], capacity - 1)
    local_index = jnp.take_along_axis(token_lists, position, axis=1) - my_index * tok_local
    local_index = jnp.where(live_send, local_index, 0)
    outgoing_rows = gather_rows(tokens, local_index, live_send)
    cot_send = gather_rows(cotangent, local_index, live_send)
    token_ids = jnp.arange(tok_local, dtype=jnp.int32)
    onehot = ((token_ids[:, None] == local_index.reshape(1, -1)) & live_send.reshape(1, -1)).astype(
        jnp.bfloat16
    )
    own_list = lax.dynamic_slice_in_dim(token_lists, my_index, 1, 0)[0]
    own_source = own_list // tok_local
    peer_ids = jnp.arange(owners, dtype=jnp.int32)
    recv_count = jnp.sum((own_source[None, :] == peer_ids[:, None]).astype(jnp.int32), axis=1)
    received_offset = jnp.sum((own_source[None, :] < peer_ids[:, None]).astype(jnp.int32), axis=1)
    active_received = slot_ids[None, :] < recv_count[:, None]
    gate_pos = jnp.minimum(received_offset[:, None] + slot_ids[None, :], capacity - 1)
    gate_slot_values = jnp.take(gating[0], gate_pos.reshape(-1)).reshape(gate_pos.shape)
    scale_factors = (
        adapter_scale_factor * jnp.where(active_received, gate_slot_values, 0.0)
    ).reshape(-1, 1)
    down_matrix = down_adapter[0]
    up_matrix = up_adapter[0]
    flat_shape = (owners * slot_count, half_width)
    block_shape = (owners, slot_count, half_width)
    row_recv = lax.all_to_all(outgoing_rows, "adapter", split_axis=0, concat_axis=0, tiled=True)
    rows_in = row_recv.reshape(flat_shape)
    low_rank = lax.psum(contract_last(rows_in, down_matrix), "tensor").astype(jnp.bfloat16)
    out_rows = (
        scale_factors * jnp.dot(low_rank, up_matrix, preferred_element_type=jnp.float32)
    ).astype(jnp.bfloat16)
    out_back = lax.all_to_all(
        out_rows.reshape(block_shape), "adapter", split_axis=0, concat_axis=0, tiled=True
    )
    cot_recv = lax.all_to_all(cot_send, "adapter", split_axis=0, concat_axis=0, tiled=True)
    weighted = (scale_factors * cot_recv.reshape(flat_shape)).astype(jnp.bfloat16)
    low_grad = lax.psum(contract_last(weighted, up_matrix), "tensor").astype(jnp.bfloat16)
    back_rows = jnp.dot(low_grad, down_matrix, preferred_element_type=jnp.float32).astype(
        jnp.bfloat16
    )
    grad_back = lax.all_to_all(
        back_rows.reshape(block_shape), "adapter", split_axis=0, concat_axis=0, tiled=True
    )
    branch_out = combine(onehot, out_back)
    input_grad = combine(onehot, grad_back)
    down_grad = (contract_first(low_grad, rows_in) / capacity).astype(jnp.bfloat16)[None]
    up_grad = (contract_first(low_rank, weighted) / capacity).astype(jnp.bfloat16)[None]
    return (branch_out, input_grad, down_grad, up_grad)


PLACES = 4


def on_line(pairs):
    return [(2 * a + side, 2 * b + side) for a, b in pairs for side in (0, 1)]


def xor_line(bit):
    return on_line([(a, a ^ bit) for a in range(PLACES)])


ENDS_IN = on_line([(0, 1), (3, 2)])
MIDDLE = on_line([(1, 2), (2, 1)])
ENDS_OUT = on_line([(1, 0), (2, 3)])
PARTNER = [(2 * a + side, 2 * a + 1 - side) for a in range(PLACES) for side in (0, 1)]
SWAP = [(0, 1), (1, 0)]
OWNERS = 2 * PLACES
FAR = xor_line(2) + [(OWNERS + a, OWNERS + b) for a, b in xor_line(3)]


def move(value, pairs):
    return lax.ppermute(value, "adapter", pairs)


def after(value, earlier):
    return lax.optimization_barrier((value, earlier))[0]


def narrow(value):
    return value.astype(jnp.bfloat16)


def add_up(*values):
    total = values[0]
    for value in values[1:]:
        total = total + value.astype(jnp.float32)
    return total


def collect_start(weights, rows):
    parts = [contract_first(weight, rows) for weight in weights]
    for_end = move(narrow(parts[3]), ENDS_IN)
    rest = move(narrow(jnp.concatenate([parts[2], parts[1]])), ENDS_IN)
    return parts, for_end, rest


def collect_end(started):
    (own, first, second, third), for_end, rest = started
    for_middle, for_near = jnp.split(rest, 2)
    for_end = move(narrow(add_up(second, for_end)), MIDDLE)
    for_middle = move(narrow(add_up(third, for_middle)), MIDDLE)
    for_end = move(narrow(add_up(first, for_end)), ENDS_OUT)
    return add_up(own, for_near, for_middle, for_end)


def both_cores(partial):
    return partial + lax.ppermute(partial, "tensor", SWAP)


def by_pairs(tokens, cotangent, down_adapter, up_adapter, token_lists, gating):
    me = lax.axis_index("adapter")
    first_group = lax.axis_index("groups") == 0
    tok_local = tokens.shape[0]
    capacity = gating.shape[1]
    down_matrix = down_adapter[0]
    up_matrix = up_adapter[0]
    rank = down_matrix.shape[0]

    far_down = lax.ppermute(down_matrix, ("groups", "adapter"), FAR)
    tokens2 = move(tokens, PARTNER)
    near_down = move(down_matrix, xor_line(1))
    cross_down = lax.ppermute(far_down, "groups", SWAP)
    far_up = lax.ppermute(after(up_matrix, far_down), ("groups", "adapter"), FAR)
    cot2 = move(after(cotangent, (tokens2, far_down)), PARTNER)
    near_up = move(after(up_matrix, near_down), xor_line(1))
    cross_up = lax.ppermute(far_up, "groups", SWAP)
    later = after(gating, (far_down, near_down, tokens2))
    gates = [gating, move(later, xor_line(1)), move(later, xor_line(2)), move(later, xor_line(3))]

    far_bit = jnp.where(first_group, 2, 3)
    experts = jnp.stack([me, me ^ 2, me ^ (2 * far_bit), me ^ (2 * (far_bit ^ 1))])
    lists = jnp.take(token_lists, experts, axis=0)
    far_gate = jnp.where(first_group, gates[2], gates[3])
    cross_gate = jnp.where(first_group, gates[3], gates[2])
    gate_rows = adapter_scale_factor * jnp.concatenate([gates[0], gates[1], far_gate, cross_gate])
    token_ids = jnp.arange(tok_local, dtype=jnp.int32)
    ids = jnp.concatenate([me * tok_local + token_ids, (me ^ 1) * tok_local + token_ids])
    taken = ids[:, None, None] == lists[None, :, :]
    scale = jnp.sum(jnp.where(taken, gate_rows[None, :, :], 0.0), axis=2)
    scale = jnp.repeat(scale, rank, axis=1)

    tokens2 = jnp.concatenate([tokens, tokens2], axis=0)
    cot2 = jnp.concatenate([cotangent, cot2], axis=0)
    down_all = jnp.concatenate([down_matrix, near_down, far_down, cross_down], axis=0)

    def low_rank(rows, matrices):
        return (scale * both_cores(contract_last(rows, matrices))).astype(jnp.bfloat16)

    def for_line(low):
        own, near, far, cross = (low[:, k * rank : (k + 1) * rank] for k in range(4))
        second = jnp.where(first_group, far, cross)
        third = jnp.where(first_group, cross, far)
        return own, near, second, third

    def outward_start(weights, matrix):
        theirs = jnp.dot(weights[tok_local:], matrix, preferred_element_type=jnp.float32)
        return move(narrow(theirs), PARTNER)

    def outward_end(weights, matrix, back):
        mine = jnp.dot(weights[:tok_local], matrix, preferred_element_type=jnp.float32)
        return narrow(mine + back.astype(jnp.float32))

    low = low_rank(tokens2, down_all)
    up_parts = collect_start(for_line(low), cot2)
    cross_up = after(cross_up, low)
    up_all = jnp.concatenate([up_matrix, near_up, far_up, cross_up], axis=0)
    low_back = low_rank(cot2, up_all)
    branch_back = outward_start(low, up_all)
    down_parts = collect_start(for_line(low_back), tokens2)
    input_back = outward_start(low_back, down_all)
    up_grad = collect_end(up_parts)
    branch_out = outward_end(low, up_all, branch_back)
    input_grad = outward_end(low_back, down_all, input_back)
    down_grad = collect_end(down_parts)
    down_grad = (down_grad / capacity).astype(jnp.bfloat16)[None]
    up_grad = (up_grad / capacity).astype(jnp.bfloat16)[None]
    return (branch_out, input_grad, down_grad, up_grad)


def local(*args):
    fits = lax.axis_size("adapter") == OWNERS and lax.axis_size("groups") == 2
    plan = by_pairs if fits else by_rows
    return plan(*args)


def solution(mesh):
    in_specs = (
        P(("groups", "adapter"), "tensor"),
        P(("groups", "adapter"), "tensor"),
        P("adapter", None, "tensor"),
        P("adapter", None, "tensor"),
        P("groups", None),
        P(("groups", "adapter"), None),
    )
    out_specs = (
        P(("groups", "adapter"), "tensor"),
        P(("groups", "adapter"), "tensor"),
        P(("groups", "adapter"), None, "tensor"),
        P(("groups", "adapter"), None, "tensor"),
    )
    return jax.shard_map(local, mesh=mesh, in_specs=in_specs, out_specs=out_specs, check_vma=False)
```

```python
import jax
import jax.numpy as jnp
from jax import lax
from jax.sharding import PartitionSpec as P

adapter_scale_factor = 2.0


def contract_last(left_op, right_op):
    return lax.dot_general(
        left_op, right_op, (((1,), (1,)), ((), ())), preferred_element_type=jnp.float32
    )


def contract_first(left_op, right_op):
    return lax.dot_general(
        left_op, right_op, (((0,), (0,)), ((), ())), preferred_element_type=jnp.float32
    )


def gather_rows(source_rows, local_index, live_slot):
    taken_rows = jnp.take(source_rows, local_index.reshape(-1), axis=0)
    taken_rows = taken_rows.reshape(local_index.shape + (source_rows.shape[1],))
    return jnp.where(live_slot[:, :, None], taken_rows, jnp.zeros_like(taken_rows))


def combine(onehot, returned):
    flat_rows = returned.reshape(-1, returned.shape[-1])
    return jnp.dot(onehot, flat_rows, preferred_element_type=jnp.float32).astype(jnp.bfloat16)


def by_rows(tokens, cotangent, down_adapter, up_adapter, token_lists, gating):
    owners = lax.axis_size("adapter")
    my_index = lax.axis_index("adapter")
    tok_local = tokens.shape[0]
    half_width = tokens.shape[1]
    capacity = gating.shape[1]
    slot_count = 3 * capacity // (2 * owners)
    slot_ids = jnp.arange(slot_count, dtype=jnp.int32)
    source = token_lists // tok_local
    sent_count = jnp.sum((source == my_index).astype(jnp.int32), axis=1)
    sent_start = jnp.sum((source < my_index).astype(jnp.int32), axis=1)
    live_send = slot_ids[None, :] < sent_count[:, None]
    position = jnp.minimum(sent_start[:, None] + slot_ids[None, :], capacity - 1)
    local_index = jnp.take_along_axis(token_lists, position, axis=1) - my_index * tok_local
    local_index = jnp.where(live_send, local_index, 0)
    outgoing_rows = gather_rows(tokens, local_index, live_send)
    cot_send = gather_rows(cotangent, local_index, live_send)
    token_ids = jnp.arange(tok_local, dtype=jnp.int32)
    onehot = ((token_ids[:, None] == local_index.reshape(1, -1)) & live_send.reshape(1, -1)).astype(
        jnp.bfloat16
    )
    own_list = lax.dynamic_slice_in_dim(token_lists, my_index, 1, 0)[0]
    own_source = own_list // tok_local
    peer_ids = jnp.arange(owners, dtype=jnp.int32)
    recv_count = jnp.sum((own_source[None, :] == peer_ids[:, None]).astype(jnp.int32), axis=1)
    received_offset = jnp.sum((own_source[None, :] < peer_ids[:, None]).astype(jnp.int32), axis=1)
    active_received = slot_ids[None, :] < recv_count[:, None]
    gate_pos = jnp.minimum(received_offset[:, None] + slot_ids[None, :], capacity - 1)
    gate_slot_values = jnp.take(gating[0], gate_pos.reshape(-1)).reshape(gate_pos.shape)
    scale_factors = (
        adapter_scale_factor * jnp.where(active_received, gate_slot_values, 0.0)
    ).reshape(-1, 1)
    down_matrix = down_adapter[0]
    up_matrix = up_adapter[0]
    flat_shape = (owners * slot_count, half_width)
    block_shape = (owners, slot_count, half_width)
    row_recv = lax.all_to_all(outgoing_rows, "adapter", split_axis=0, concat_axis=0, tiled=True)
    rows_in = row_recv.reshape(flat_shape)
    low_rank = lax.psum(contract_last(rows_in, down_matrix), "tensor").astype(jnp.bfloat16)
    out_rows = (
        scale_factors * jnp.dot(low_rank, up_matrix, preferred_element_type=jnp.float32)
    ).astype(jnp.bfloat16)
    out_back = lax.all_to_all(
        out_rows.reshape(block_shape), "adapter", split_axis=0, concat_axis=0, tiled=True
    )
    cot_recv = lax.all_to_all(cot_send, "adapter", split_axis=0, concat_axis=0, tiled=True)
    weighted = (scale_factors * cot_recv.reshape(flat_shape)).astype(jnp.bfloat16)
    low_grad = lax.psum(contract_last(weighted, up_matrix), "tensor").astype(jnp.bfloat16)
    back_rows = jnp.dot(low_grad, down_matrix, preferred_element_type=jnp.float32).astype(
        jnp.bfloat16
    )
    grad_back = lax.all_to_all(
        back_rows.reshape(block_shape), "adapter", split_axis=0, concat_axis=0, tiled=True
    )
    branch_out = combine(onehot, out_back)
    input_grad = combine(onehot, grad_back)
    down_grad = (contract_first(low_grad, rows_in) / capacity).astype(jnp.bfloat16)[None]
    up_grad = (contract_first(low_rank, weighted) / capacity).astype(jnp.bfloat16)[None]
    return (branch_out, input_grad, down_grad, up_grad)


PLACES = 4


def on_line(pairs):
    return [(2 * a + side, 2 * b + side) for a, b in pairs for side in (0, 1)]


def xor_line(bit):
    return on_line([(a, a ^ bit) for a in range(PLACES)])


ENDS_IN = on_line([(0, 1), (3, 2)])
MIDDLE = on_line([(1, 2), (2, 1)])
ENDS_OUT = on_line([(1, 0), (2, 3)])
PARTNER = [(2 * a + side, 2 * a + 1 - side) for a in range(PLACES) for side in (0, 1)]
SWAP = [(0, 1), (1, 0)]
OWNERS = 2 * PLACES
FAR = xor_line(2) + [(OWNERS + a, OWNERS + b) for a, b in xor_line(3)]


def move(value, pairs):
    return lax.ppermute(value, "adapter", pairs)


def after(value, earlier):
    return lax.optimization_barrier((value, earlier))[0]


def narrow(value):
    return value.astype(jnp.bfloat16)


def add_up(*values):
    total = values[0]
    for value in values[1:]:
        total = total + value.astype(jnp.float32)
    return total


def partial_sums(weights, rows):
    parts = [contract_first(weight, rows) for weight in weights]
    return lax.optimization_barrier((parts, [narrow(part) for part in parts[1:]]))


def both_cores(partial):
    return partial + lax.ppermute(partial, "tensor", SWAP)


def by_pairs(tokens, cotangent, down_adapter, up_adapter, token_lists, gating):
    me = lax.axis_index("adapter")
    first_group = lax.axis_index("groups") == 0
    tok_local = tokens.shape[0]
    capacity = gating.shape[1]
    down_matrix = down_adapter[0]
    up_matrix = up_adapter[0]
    rank = down_matrix.shape[0]

    far_down = lax.ppermute(down_matrix, ("groups", "adapter"), FAR)
    tokens2 = move(tokens, PARTNER)
    near_down = move(down_matrix, xor_line(1))
    cot2 = move(cotangent, PARTNER)
    cross_down = lax.ppermute(far_down, "groups", SWAP)
    far_up = lax.ppermute(after(up_matrix, far_down), ("groups", "adapter"), FAR)
    near_up = move(after(up_matrix, near_down), xor_line(1))
    cross_up = lax.ppermute(far_up, "groups", SWAP)
    later = after(gating, (far_down, near_up))
    gates = [gating, move(later, xor_line(1)), move(later, xor_line(2)), move(later, xor_line(3))]
    tokens2, cot2, near_up = lax.optimization_barrier((tokens2, cot2, near_up))

    far_bit = jnp.where(first_group, 2, 3)
    experts = jnp.stack([me, me ^ 2, me ^ (2 * far_bit), me ^ (2 * (far_bit ^ 1))])
    lists = jnp.take(token_lists, experts, axis=0)
    far_gate = jnp.where(first_group, gates[2], gates[3])
    cross_gate = jnp.where(first_group, gates[3], gates[2])
    gate_rows = adapter_scale_factor * jnp.concatenate([gates[0], gates[1], far_gate, cross_gate])
    token_ids = jnp.arange(tok_local, dtype=jnp.int32)
    ids = jnp.concatenate([me * tok_local + token_ids, (me ^ 1) * tok_local + token_ids])
    taken = ids[:, None, None] == lists[None, :, :]
    scale = jnp.sum(jnp.where(taken, gate_rows[None, :, :], 0.0), axis=2)
    scale = jnp.repeat(scale, rank, axis=1)

    tokens2 = jnp.concatenate([tokens, tokens2], axis=0)
    cot2 = jnp.concatenate([cotangent, cot2], axis=0)
    down_all = jnp.concatenate([down_matrix, near_down, far_down, cross_down], axis=0)

    def low_rank(rows, matrices, *earlier):
        product = both_cores(contract_last(rows, matrices))
        return narrow(scale * after(product, earlier))

    def for_line(low):
        own, near, far, cross = (low[:, k * rank : (k + 1) * rank] for k in range(4))
        second = jnp.where(first_group, far, cross)
        third = jnp.where(first_group, cross, far)
        return own, near, second, third

    def outward_start(weights, matrix):
        theirs = jnp.dot(weights[tok_local:], matrix, preferred_element_type=jnp.float32)
        return move(narrow(theirs), PARTNER)

    def outward_end(weights, matrix, back):
        mine = jnp.dot(weights[:tok_local], matrix, preferred_element_type=jnp.float32)
        return narrow(mine + back.astype(jnp.float32))

    low = low_rank(tokens2, down_all, far_up)
    (own, first, second, third), up_send = partial_sums(for_line(low), cot2)
    up_1a = move(up_send[2], ENDS_IN)
    up_1b = move(up_send[1], ENDS_IN)
    up_1c = move(up_send[0], ENDS_IN)

    cross_up = after(cross_up, (up_1a, up_1b))
    up_all = jnp.concatenate([up_matrix, near_up, far_up, cross_up], axis=0)
    low_back = low_rank(cot2, up_all)
    branch_back = outward_start(low, up_all)
    up_2a = move(narrow(add_up(second, up_1a)), MIDDLE)
    up_2b = move(narrow(add_up(third, up_1b)), MIDDLE)
    low_back = after(low_back, (up_1c, up_2a))
    (own_b, first_b, second_b, third_b), down_send = partial_sums(for_line(low_back), tokens2)
    down_1a = move(down_send[2], ENDS_IN)
    down_1b = move(down_send[1], ENDS_IN)
    down_1c = move(down_send[0], ENDS_IN)
    up_3 = move(narrow(add_up(first, up_2a)), ENDS_OUT)
    input_back = outward_start(low_back, down_all)
    down_2a = move(narrow(add_up(second_b, down_1a)), MIDDLE)
    down_2b = move(narrow(add_up(third_b, down_1b)), MIDDLE)
    up_grad = add_up(own, up_1c, up_2b, up_3)
    branch_out = outward_end(low, up_all, branch_back)
    down_3 = move(narrow(add_up(first_b, down_2a)), ENDS_OUT)
    input_grad = outward_end(low_back, down_all, input_back)
    down_grad = add_up(own_b, down_1c, down_2b, down_3)
    down_grad = (down_grad / capacity).astype(jnp.bfloat16)[None]
    up_grad = (up_grad / capacity).astype(jnp.bfloat16)[None]
    return (branch_out, input_grad, down_grad, up_grad)


def local(*args):
    fits = lax.axis_size("adapter") == OWNERS and lax.axis_size("groups") == 2
    plan = by_pairs if fits else by_rows
    return plan(*args)


def solution(mesh):
    in_specs = (
        P(("groups", "adapter"), "tensor"),
        P(("groups", "adapter"), "tensor"),
        P("adapter", None, "tensor"),
        P("adapter", None, "tensor"),
        P("groups", None),
        P(("groups", "adapter"), None),
    )
    out_specs = (
        P(("groups", "adapter"), "tensor"),
        P(("groups", "adapter"), "tensor"),
        P(("groups", "adapter"), None, "tensor"),
        P(("groups", "adapter"), None, "tensor"),
    )
    return jax.shard_map(local, mesh=mesh, in_specs=in_specs, out_specs=out_specs, check_vma=False)
```

```python
import jax
import jax.numpy as jnp
from jax import lax
from jax.sharding import PartitionSpec as P

adapter_scale_factor = 2.0


def contract_last(left_op, right_op):
    return lax.dot_general(
        left_op, right_op, (((1,), (1,)), ((), ())), preferred_element_type=jnp.float32
    )


def contract_first(left_op, right_op):
    return lax.dot_general(
        left_op, right_op, (((0,), (0,)), ((), ())), preferred_element_type=jnp.float32
    )


def gather_rows(source_rows, local_index, live_slot):
    taken_rows = jnp.take(source_rows, local_index.reshape(-1), axis=0)
    taken_rows = taken_rows.reshape(local_index.shape + (source_rows.shape[1],))
    return jnp.where(live_slot[:, :, None], taken_rows, jnp.zeros_like(taken_rows))


def combine(onehot, returned):
    flat_rows = returned.reshape(-1, returned.shape[-1])
    return jnp.dot(onehot, flat_rows, preferred_element_type=jnp.float32).astype(jnp.bfloat16)


def by_rows(tokens, cotangent, down_adapter, up_adapter, token_lists, gating):
    owners = lax.axis_size("adapter")
    my_index = lax.axis_index("adapter")
    tok_local = tokens.shape[0]
    half_width = tokens.shape[1]
    capacity = gating.shape[1]
    slot_count = 3 * capacity // (2 * owners)
    slot_ids = jnp.arange(slot_count, dtype=jnp.int32)
    source = token_lists // tok_local
    sent_count = jnp.sum((source == my_index).astype(jnp.int32), axis=1)
    sent_start = jnp.sum((source < my_index).astype(jnp.int32), axis=1)
    live_send = slot_ids[None, :] < sent_count[:, None]
    position = jnp.minimum(sent_start[:, None] + slot_ids[None, :], capacity - 1)
    local_index = jnp.take_along_axis(token_lists, position, axis=1) - my_index * tok_local
    local_index = jnp.where(live_send, local_index, 0)
    outgoing_rows = gather_rows(tokens, local_index, live_send)
    cot_send = gather_rows(cotangent, local_index, live_send)
    token_ids = jnp.arange(tok_local, dtype=jnp.int32)
    onehot = ((token_ids[:, None] == local_index.reshape(1, -1)) & live_send.reshape(1, -1)).astype(
        jnp.bfloat16
    )
    own_list = lax.dynamic_slice_in_dim(token_lists, my_index, 1, 0)[0]
    own_source = own_list // tok_local
    peer_ids = jnp.arange(owners, dtype=jnp.int32)
    recv_count = jnp.sum((own_source[None, :] == peer_ids[:, None]).astype(jnp.int32), axis=1)
    received_offset = jnp.sum((own_source[None, :] < peer_ids[:, None]).astype(jnp.int32), axis=1)
    active_received = slot_ids[None, :] < recv_count[:, None]
    gate_pos = jnp.minimum(received_offset[:, None] + slot_ids[None, :], capacity - 1)
    gate_slot_values = jnp.take(gating[0], gate_pos.reshape(-1)).reshape(gate_pos.shape)
    scale_factors = (
        adapter_scale_factor * jnp.where(active_received, gate_slot_values, 0.0)
    ).reshape(-1, 1)
    down_matrix = down_adapter[0]
    up_matrix = up_adapter[0]
    flat_shape = (owners * slot_count, half_width)
    block_shape = (owners, slot_count, half_width)
    row_recv = lax.all_to_all(outgoing_rows, "adapter", split_axis=0, concat_axis=0, tiled=True)
    rows_in = row_recv.reshape(flat_shape)
    low_rank = lax.psum(contract_last(rows_in, down_matrix), "tensor").astype(jnp.bfloat16)
    out_rows = (
        scale_factors * jnp.dot(low_rank, up_matrix, preferred_element_type=jnp.float32)
    ).astype(jnp.bfloat16)
    out_back = lax.all_to_all(
        out_rows.reshape(block_shape), "adapter", split_axis=0, concat_axis=0, tiled=True
    )
    cot_recv = lax.all_to_all(cot_send, "adapter", split_axis=0, concat_axis=0, tiled=True)
    weighted = (scale_factors * cot_recv.reshape(flat_shape)).astype(jnp.bfloat16)
    low_grad = lax.psum(contract_last(weighted, up_matrix), "tensor").astype(jnp.bfloat16)
    back_rows = jnp.dot(low_grad, down_matrix, preferred_element_type=jnp.float32).astype(
        jnp.bfloat16
    )
    grad_back = lax.all_to_all(
        back_rows.reshape(block_shape), "adapter", split_axis=0, concat_axis=0, tiled=True
    )
    branch_out = combine(onehot, out_back)
    input_grad = combine(onehot, grad_back)
    down_grad = (contract_first(low_grad, rows_in) / capacity).astype(jnp.bfloat16)[None]
    up_grad = (contract_first(low_rank, weighted) / capacity).astype(jnp.bfloat16)[None]
    return (branch_out, input_grad, down_grad, up_grad)


PLACES = 4


def on_line(pairs):
    return [(2 * a + side, 2 * b + side) for a, b in pairs for side in (0, 1)]


def xor_line(bit):
    return on_line([(a, a ^ bit) for a in range(PLACES)])


PARTNER = [(2 * a + side, 2 * a + 1 - side) for a in range(PLACES) for side in (0, 1)]
SWAP = [(0, 1), (1, 0)]
OWNERS = 2 * PLACES
FAR = xor_line(2) + [(OWNERS + a, OWNERS + b) for a, b in xor_line(3)]


def move(value, pairs):
    return lax.ppermute(value, "adapter", pairs)


def after(value, earlier):
    return lax.optimization_barrier((value, earlier))[0]


def narrow(value):
    return value.astype(jnp.bfloat16)


def add_up(*values):
    total = values[0]
    for value in values[1:]:
        total = total + value.astype(jnp.float32)
    return total


def partial_sums(weights, rows):
    parts = [contract_first(weight, rows) for weight in weights]
    return lax.optimization_barrier((parts, [narrow(part) for part in parts[1:]]))


def both_cores(partial):
    return partial + lax.ppermute(partial, "tensor", SWAP)


def gather_gates(gating, earlier):
    later = after(gating, earlier)
    return [gating] + [move(later, xor_line(bit)) for bit in (1, 2, 3)]


def by_pairs(tokens, cotangent, down_adapter, up_adapter, token_lists, gating):
    me = lax.axis_index("adapter")
    first_group = lax.axis_index("groups") == 0
    tok_local = tokens.shape[0]
    capacity = gating.shape[1]
    down_matrix = down_adapter[0]
    up_matrix = up_adapter[0]
    rank = down_matrix.shape[0]

    far_down = lax.ppermute(down_matrix, ("groups", "adapter"), FAR)
    tokens2 = move(tokens, PARTNER)
    near_down = move(down_matrix, xor_line(1))
    cot2 = move(after(cotangent, far_down), PARTNER)
    cross_down = lax.ppermute(far_down, "groups", SWAP)
    far_up = lax.ppermute(after(up_matrix, far_down), ("groups", "adapter"), FAR)
    near_up = move(after(up_matrix, near_down), xor_line(1))
    cross_up = lax.ppermute(far_up, "groups", SWAP)
    gates = gather_gates(gating, (far_down, tokens2))

    far_bit = jnp.where(first_group, 2, 3)
    experts = jnp.stack([me, me ^ 2, me ^ (2 * far_bit), me ^ (2 * (far_bit ^ 1))])
    lists = jnp.take(token_lists, experts, axis=0)
    far_gate = jnp.where(first_group, gates[2], gates[3])
    cross_gate = jnp.where(first_group, gates[3], gates[2])
    gate_rows = adapter_scale_factor * jnp.concatenate([gates[0], gates[1], far_gate, cross_gate])
    token_ids = jnp.arange(tok_local, dtype=jnp.int32)
    ids = jnp.concatenate([me * tok_local + token_ids, (me ^ 1) * tok_local + token_ids])
    taken = ids[:, None, None] == lists[None, :, :]
    scale = jnp.sum(jnp.where(taken, gate_rows[None, :, :], 0.0), axis=2)
    scale = jnp.repeat(scale, rank, axis=1)

    tokens2 = jnp.concatenate([tokens, tokens2], axis=0)
    cot2 = jnp.concatenate([cotangent, cot2], axis=0)
    down_all = jnp.concatenate([down_matrix, near_down, far_down, cross_down], axis=0)

    def low_rank(rows, matrices, *earlier):
        product = both_cores(contract_last(rows, matrices))
        return narrow(scale * after(product, earlier))

    def for_line(low):
        own, near, far, cross = (low[:, k * rank : (k + 1) * rank] for k in range(4))
        second = jnp.where(first_group, far, cross)
        third = jnp.where(first_group, cross, far)
        return own, near, second, third

    def outward_start(weights, matrix):
        theirs = jnp.dot(weights[tok_local:], matrix, preferred_element_type=jnp.float32)
        return move(narrow(theirs), PARTNER)

    def outward_end(weights, matrix, back):
        mine = jnp.dot(weights[:tok_local], matrix, preferred_element_type=jnp.float32)
        return narrow(mine + back.astype(jnp.float32))

    low = low_rank(tokens2, down_all, far_up)
    (own, first, second, third), up_send = partial_sums(for_line(low), cot2)
    up_near = move(jnp.concatenate([up_send[0], up_send[2]]), xor_line(1))

    cross_up = after(cross_up, up_send)
    up_all = jnp.concatenate([up_matrix, near_up, far_up, cross_up], axis=0)
    low_back = low_rank(cot2, up_all, up_near)
    branch_back = outward_start(low, up_all)
    (own_b, first_b, second_b, third_b), down_send = partial_sums(for_line(low_back), tokens2)
    down_third = move(down_send[2], xor_line(1))
    down_first = move(down_send[0], xor_line(1))
    input_back = outward_start(low_back, down_all)
    up_first, up_third = jnp.split(up_near, 2)
    up_far = move(narrow(add_up(second, up_third)), xor_line(2))
    down_far = move(narrow(add_up(second_b, down_third)), xor_line(2))
    branch_out = outward_end(low, up_all, branch_back)
    up_grad = add_up(own, up_first, up_far)
    input_grad = outward_end(low_back, down_all, input_back)
    down_grad = add_up(own_b, down_first, down_far)
    down_grad = (down_grad / capacity).astype(jnp.bfloat16)[None]
    up_grad = (up_grad / capacity).astype(jnp.bfloat16)[None]
    return (branch_out, input_grad, down_grad, up_grad)


def local(*args):
    fits = lax.axis_size("adapter") == OWNERS and lax.axis_size("groups") == 2
    plan = by_pairs if fits else by_rows
    return plan(*args)


def solution(mesh):
    in_specs = (
        P(("groups", "adapter"), "tensor"),
        P(("groups", "adapter"), "tensor"),
        P("adapter", None, "tensor"),
        P("adapter", None, "tensor"),
        P("groups", None),
        P(("groups", "adapter"), None),
    )
    out_specs = (
        P(("groups", "adapter"), "tensor"),
        P(("groups", "adapter"), "tensor"),
        P(("groups", "adapter"), None, "tensor"),
        P(("groups", "adapter"), None, "tensor"),
    )
    return jax.shard_map(local, mesh=mesh, in_specs=in_specs, out_specs=out_specs, check_vma=False)
```

```python
import jax
import jax.numpy as jnp
from jax import lax
from jax.sharding import PartitionSpec as P

adapter_scale_factor = 2.0


def contract_last(left_op, right_op):
    return lax.dot_general(
        left_op, right_op, (((1,), (1,)), ((), ())), preferred_element_type=jnp.float32
    )


def contract_first(left_op, right_op):
    return lax.dot_general(
        left_op, right_op, (((0,), (0,)), ((), ())), preferred_element_type=jnp.float32
    )


def gather_rows(source_rows, local_index, live_slot):
    taken_rows = jnp.take(source_rows, local_index.reshape(-1), axis=0)
    taken_rows = taken_rows.reshape(local_index.shape + (source_rows.shape[1],))
    return jnp.where(live_slot[:, :, None], taken_rows, jnp.zeros_like(taken_rows))


def combine(onehot, returned):
    flat_rows = returned.reshape(-1, returned.shape[-1])
    return jnp.dot(onehot, flat_rows, preferred_element_type=jnp.float32).astype(jnp.bfloat16)


def by_rows(tokens, cotangent, down_adapter, up_adapter, token_lists, gating):
    owners = lax.axis_size("adapter")
    my_index = lax.axis_index("adapter")
    tok_local = tokens.shape[0]
    half_width = tokens.shape[1]
    capacity = gating.shape[1]
    slot_count = 3 * capacity // (2 * owners)
    slot_ids = jnp.arange(slot_count, dtype=jnp.int32)
    source = token_lists // tok_local
    sent_count = jnp.sum((source == my_index).astype(jnp.int32), axis=1)
    sent_start = jnp.sum((source < my_index).astype(jnp.int32), axis=1)
    live_send = slot_ids[None, :] < sent_count[:, None]
    position = jnp.minimum(sent_start[:, None] + slot_ids[None, :], capacity - 1)
    local_index = jnp.take_along_axis(token_lists, position, axis=1) - my_index * tok_local
    local_index = jnp.where(live_send, local_index, 0)
    outgoing_rows = gather_rows(tokens, local_index, live_send)
    cot_send = gather_rows(cotangent, local_index, live_send)
    token_ids = jnp.arange(tok_local, dtype=jnp.int32)
    onehot = ((token_ids[:, None] == local_index.reshape(1, -1)) & live_send.reshape(1, -1)).astype(
        jnp.bfloat16
    )
    own_list = lax.dynamic_slice_in_dim(token_lists, my_index, 1, 0)[0]
    own_source = own_list // tok_local
    peer_ids = jnp.arange(owners, dtype=jnp.int32)
    recv_count = jnp.sum((own_source[None, :] == peer_ids[:, None]).astype(jnp.int32), axis=1)
    received_offset = jnp.sum((own_source[None, :] < peer_ids[:, None]).astype(jnp.int32), axis=1)
    active_received = slot_ids[None, :] < recv_count[:, None]
    gate_pos = jnp.minimum(received_offset[:, None] + slot_ids[None, :], capacity - 1)
    gate_slot_values = jnp.take(gating[0], gate_pos.reshape(-1)).reshape(gate_pos.shape)
    scale_factors = (
        adapter_scale_factor * jnp.where(active_received, gate_slot_values, 0.0)
    ).reshape(-1, 1)
    down_matrix = down_adapter[0]
    up_matrix = up_adapter[0]
    flat_shape = (owners * slot_count, half_width)
    block_shape = (owners, slot_count, half_width)
    row_recv = lax.all_to_all(outgoing_rows, "adapter", split_axis=0, concat_axis=0, tiled=True)
    rows_in = row_recv.reshape(flat_shape)
    low_rank = lax.psum(contract_last(rows_in, down_matrix), "tensor").astype(jnp.bfloat16)
    out_rows = (
        scale_factors * jnp.dot(low_rank, up_matrix, preferred_element_type=jnp.float32)
    ).astype(jnp.bfloat16)
    out_back = lax.all_to_all(
        out_rows.reshape(block_shape), "adapter", split_axis=0, concat_axis=0, tiled=True
    )
    cot_recv = lax.all_to_all(cot_send, "adapter", split_axis=0, concat_axis=0, tiled=True)
    weighted = (scale_factors * cot_recv.reshape(flat_shape)).astype(jnp.bfloat16)
    low_grad = lax.psum(contract_last(weighted, up_matrix), "tensor").astype(jnp.bfloat16)
    back_rows = jnp.dot(low_grad, down_matrix, preferred_element_type=jnp.float32).astype(
        jnp.bfloat16
    )
    grad_back = lax.all_to_all(
        back_rows.reshape(block_shape), "adapter", split_axis=0, concat_axis=0, tiled=True
    )
    branch_out = combine(onehot, out_back)
    input_grad = combine(onehot, grad_back)
    down_grad = (contract_first(low_grad, rows_in) / capacity).astype(jnp.bfloat16)[None]
    up_grad = (contract_first(low_rank, weighted) / capacity).astype(jnp.bfloat16)[None]
    return (branch_out, input_grad, down_grad, up_grad)


PLACES = 4


def on_line(pairs):
    return [(2 * a + side, 2 * b + side) for a, b in pairs for side in (0, 1)]


def xor_line(bit):
    return on_line([(a, a ^ bit) for a in range(PLACES)])


PARTNER = [(2 * a + side, 2 * a + 1 - side) for a in range(PLACES) for side in (0, 1)]
SWAP = [(0, 1), (1, 0)]
OWNERS = 2 * PLACES
FAR = xor_line(2) + [(OWNERS + a, OWNERS + b) for a, b in xor_line(3)]


def move(value, pairs):
    return lax.ppermute(value, "adapter", pairs)


def after(value, earlier):
    return lax.optimization_barrier((value, earlier))[0]


def narrow(value):
    return value.astype(jnp.bfloat16)


def add_up(*values):
    total = values[0]
    for value in values[1:]:
        total = total + value.astype(jnp.float32)
    return total


def partial_sums(weights, rows):
    parts = [contract_first(weight, rows) for weight in weights]
    return lax.optimization_barrier((parts, [narrow(part) for part in parts[1:]]))


def both_cores(partial):
    return partial + lax.ppermute(partial, "tensor", SWAP)


def gather_gates(gating, earlier):
    later = after(gating, earlier)
    return [gating] + [move(later, xor_line(bit)) for bit in (1, 2, 3)]


def by_pairs(tokens, cotangent, down_adapter, up_adapter, token_lists, gating):
    me = lax.axis_index("adapter")
    first_group = lax.axis_index("groups") == 0
    tok_local = tokens.shape[0]
    capacity = gating.shape[1]
    down_matrix = down_adapter[0]
    up_matrix = up_adapter[0]
    rank = down_matrix.shape[0]

    far_down = lax.ppermute(down_matrix, ("groups", "adapter"), FAR)
    tokens2 = move(tokens, PARTNER)
    near_down = move(down_matrix, xor_line(1))
    cot2 = move(after(cotangent, far_down), PARTNER)
    cross_down = lax.ppermute(far_down, "groups", SWAP)
    far_up = lax.ppermute(after(up_matrix, far_down), ("groups", "adapter"), FAR)
    near_up = move(after(up_matrix, near_down), xor_line(1))
    cot2, near_up, far_up = lax.optimization_barrier((cot2, near_up, far_up))
    cross_up = lax.ppermute(far_up, "groups", SWAP)
    gates = gather_gates(gating, (far_down, tokens2))

    far_bit = jnp.where(first_group, 2, 3)
    experts = jnp.stack([me, me ^ 2, me ^ (2 * far_bit), me ^ (2 * (far_bit ^ 1))])
    lists = jnp.take(token_lists, experts, axis=0)
    far_gate = jnp.where(first_group, gates[2], gates[3])
    cross_gate = jnp.where(first_group, gates[3], gates[2])
    gate_rows = adapter_scale_factor * jnp.concatenate([gates[0], gates[1], far_gate, cross_gate])
    token_ids = jnp.arange(tok_local, dtype=jnp.int32)
    ids = jnp.concatenate([me * tok_local + token_ids, (me ^ 1) * tok_local + token_ids])
    taken = ids[:, None, None] == lists[None, :, :]
    scale = jnp.sum(jnp.where(taken, gate_rows[None, :, :], 0.0), axis=2)
    scale = jnp.repeat(scale, rank, axis=1)

    tokens2 = jnp.concatenate([tokens, tokens2], axis=0)
    cot2 = jnp.concatenate([cotangent, cot2], axis=0)
    down_all = jnp.concatenate([down_matrix, near_down, far_down, cross_down], axis=0)

    def low_rank(rows, matrices, *earlier):
        product = both_cores(contract_last(rows, matrices))
        return narrow(scale * after(product, earlier))

    def for_line(low):
        own, near, far, cross = (low[:, k * rank : (k + 1) * rank] for k in range(4))
        second = jnp.where(first_group, far, cross)
        third = jnp.where(first_group, cross, far)
        return own, near, second, third

    def outward_start(weights, matrix):
        theirs = jnp.dot(weights[tok_local:], matrix, preferred_element_type=jnp.float32)
        return move(narrow(theirs), PARTNER)

    def outward_end(weights, matrix, back):
        mine = jnp.dot(weights[:tok_local], matrix, preferred_element_type=jnp.float32)
        return narrow(mine + back.astype(jnp.float32))

    low = low_rank(tokens2, down_all)
    (own, first, second, third), up_send = partial_sums(for_line(low), cot2)
    up_third = move(up_send[2], xor_line(1))
    up_first = move(up_send[0], xor_line(1))

    cross_up = after(cross_up, up_third)
    up_all = jnp.concatenate([up_matrix, near_up, far_up, cross_up], axis=0)
    low_back = low_rank(cot2, up_all)
    branch_back = outward_start(low, up_all)
    (own_b, first_b, second_b, third_b), down_send = partial_sums(for_line(low_back), tokens2)
    down_third = move(down_send[2], xor_line(1))
    down_first = move(after(down_send[0], (up_first, down_third)), xor_line(1))
    input_back = outward_start(low_back, down_all)
    up_far = move(narrow(add_up(second, up_third)), xor_line(2))
    down_far = move(narrow(add_up(second_b, down_third)), xor_line(2))
    branch_out = outward_end(low, up_all, branch_back)
    up_grad = add_up(own, up_first, up_far)
    input_grad = outward_end(low_back, down_all, input_back)
    down_grad = add_up(own_b, down_first, down_far)
    down_grad = (down_grad / capacity).astype(jnp.bfloat16)[None]
    up_grad = (up_grad / capacity).astype(jnp.bfloat16)[None]
    return (branch_out, input_grad, down_grad, up_grad)


def local(*args):
    fits = lax.axis_size("adapter") == OWNERS and lax.axis_size("groups") == 2
    plan = by_pairs if fits else by_rows
    return plan(*args)


def solution(mesh):
    in_specs = (
        P(("groups", "adapter"), "tensor"),
        P(("groups", "adapter"), "tensor"),
        P("adapter", None, "tensor"),
        P("adapter", None, "tensor"),
        P("groups", None),
        P(("groups", "adapter"), None),
    )
    out_specs = (
        P(("groups", "adapter"), "tensor"),
        P(("groups", "adapter"), "tensor"),
        P(("groups", "adapter"), None, "tensor"),
        P(("groups", "adapter"), None, "tensor"),
    )
    return jax.shard_map(local, mesh=mesh, in_specs=in_specs, out_specs=out_specs, check_vma=False)
```

```python
import jax
import jax.numpy as jnp
from jax import lax
from jax.sharding import PartitionSpec as P

adapter_scale_factor = 2.0


def contract_last(left_op, right_op):
    return lax.dot_general(
        left_op, right_op, (((1,), (1,)), ((), ())), preferred_element_type=jnp.float32
    )


def contract_first(left_op, right_op):
    return lax.dot_general(
        left_op, right_op, (((0,), (0,)), ((), ())), preferred_element_type=jnp.float32
    )


def gather_rows(source_rows, local_index, live_slot):
    taken_rows = jnp.take(source_rows, local_index.reshape(-1), axis=0)
    taken_rows = taken_rows.reshape(local_index.shape + (source_rows.shape[1],))
    return jnp.where(live_slot[:, :, None], taken_rows, jnp.zeros_like(taken_rows))


def combine(onehot, returned):
    flat_rows = returned.reshape(-1, returned.shape[-1])
    return jnp.dot(onehot, flat_rows, preferred_element_type=jnp.float32).astype(jnp.bfloat16)


def by_rows(tokens, cotangent, down_adapter, up_adapter, token_lists, gating):
    owners = lax.axis_size("adapter")
    my_index = lax.axis_index("adapter")
    tok_local = tokens.shape[0]
    half_width = tokens.shape[1]
    capacity = gating.shape[1]
    slot_count = 3 * capacity // (2 * owners)
    slot_ids = jnp.arange(slot_count, dtype=jnp.int32)
    source = token_lists // tok_local
    sent_count = jnp.sum((source == my_index).astype(jnp.int32), axis=1)
    sent_start = jnp.sum((source < my_index).astype(jnp.int32), axis=1)
    live_send = slot_ids[None, :] < sent_count[:, None]
    position = jnp.minimum(sent_start[:, None] + slot_ids[None, :], capacity - 1)
    local_index = jnp.take_along_axis(token_lists, position, axis=1) - my_index * tok_local
    local_index = jnp.where(live_send, local_index, 0)
    outgoing_rows = gather_rows(tokens, local_index, live_send)
    cot_send = gather_rows(cotangent, local_index, live_send)
    token_ids = jnp.arange(tok_local, dtype=jnp.int32)
    onehot = ((token_ids[:, None] == local_index.reshape(1, -1)) & live_send.reshape(1, -1)).astype(
        jnp.bfloat16
    )
    own_list = lax.dynamic_slice_in_dim(token_lists, my_index, 1, 0)[0]
    own_source = own_list // tok_local
    peer_ids = jnp.arange(owners, dtype=jnp.int32)
    recv_count = jnp.sum((own_source[None, :] == peer_ids[:, None]).astype(jnp.int32), axis=1)
    received_offset = jnp.sum((own_source[None, :] < peer_ids[:, None]).astype(jnp.int32), axis=1)
    active_received = slot_ids[None, :] < recv_count[:, None]
    gate_pos = jnp.minimum(received_offset[:, None] + slot_ids[None, :], capacity - 1)
    gate_slot_values = jnp.take(gating[0], gate_pos.reshape(-1)).reshape(gate_pos.shape)
    scale_factors = (
        adapter_scale_factor * jnp.where(active_received, gate_slot_values, 0.0)
    ).reshape(-1, 1)
    down_matrix = down_adapter[0]
    up_matrix = up_adapter[0]
    flat_shape = (owners * slot_count, half_width)
    block_shape = (owners, slot_count, half_width)
    row_recv = lax.all_to_all(outgoing_rows, "adapter", split_axis=0, concat_axis=0, tiled=True)
    rows_in = row_recv.reshape(flat_shape)
    low_rank = lax.psum(contract_last(rows_in, down_matrix), "tensor").astype(jnp.bfloat16)
    out_rows = (
        scale_factors * jnp.dot(low_rank, up_matrix, preferred_element_type=jnp.float32)
    ).astype(jnp.bfloat16)
    out_back = lax.all_to_all(
        out_rows.reshape(block_shape), "adapter", split_axis=0, concat_axis=0, tiled=True
    )
    cot_recv = lax.all_to_all(cot_send, "adapter", split_axis=0, concat_axis=0, tiled=True)
    weighted = (scale_factors * cot_recv.reshape(flat_shape)).astype(jnp.bfloat16)
    low_grad = lax.psum(contract_last(weighted, up_matrix), "tensor").astype(jnp.bfloat16)
    back_rows = jnp.dot(low_grad, down_matrix, preferred_element_type=jnp.float32).astype(
        jnp.bfloat16
    )
    grad_back = lax.all_to_all(
        back_rows.reshape(block_shape), "adapter", split_axis=0, concat_axis=0, tiled=True
    )
    branch_out = combine(onehot, out_back)
    input_grad = combine(onehot, grad_back)
    down_grad = (contract_first(low_grad, rows_in) / capacity).astype(jnp.bfloat16)[None]
    up_grad = (contract_first(low_rank, weighted) / capacity).astype(jnp.bfloat16)[None]
    return (branch_out, input_grad, down_grad, up_grad)


PLACES = 4


def on_line(pairs):
    return [(2 * a + side, 2 * b + side) for a, b in pairs for side in (0, 1)]


def xor_line(bit):
    return on_line([(a, a ^ bit) for a in range(PLACES)])


PARTNER = [(2 * a + side, 2 * a + 1 - side) for a in range(PLACES) for side in (0, 1)]
SWAP = [(0, 1), (1, 0)]
OWNERS = 2 * PLACES
FAR = xor_line(2) + [(OWNERS + a, OWNERS + b) for a, b in xor_line(3)]


def move(value, pairs):
    return lax.ppermute(value, "adapter", pairs)


def after(value, earlier):
    return lax.optimization_barrier((value, earlier))[0]


def narrow(value):
    return value.astype(jnp.bfloat16)


def add_up(*values):
    total = values[0]
    for value in values[1:]:
        total = total + value.astype(jnp.float32)
    return total


def partial_sums(weights, rows):
    parts = [jnp.dot(weight, rows, preferred_element_type=jnp.float32) for weight in weights]
    return lax.optimization_barrier((parts, [narrow(part) for part in parts[1:]]))


def both_cores(partial):
    return partial + lax.ppermute(partial, "tensor", SWAP)


LANES = 128


def gate_columns(gating, rows):
    pieces, rest = [], gating
    for _ in range(3):
        piece = lax.reduce_precision(rest, exponent_bits=8, mantissa_bits=7)
        pieces.append(narrow(piece).reshape(-1, LANES))
        rest = rest - piece
    columns = jnp.concatenate(pieces)
    return jnp.pad(columns, ((0, rows - columns.shape[0]), (0, 0)))


def gates_of(columns, capacity):
    pieces = columns[: 3 * capacity // LANES].reshape(3, 1, capacity)
    return jnp.sum(pieces.astype(jnp.float32), axis=0)


def by_pairs(tokens, cotangent, down_adapter, up_adapter, token_lists, gating):
    me = lax.axis_index("adapter")
    first_group = lax.axis_index("groups") == 0
    tok_local, width = tokens.shape
    capacity = gating.shape[1]
    down_matrix = down_adapter[0]
    up_matrix = up_adapter[0]
    rank = down_matrix.shape[0]

    message = jnp.concatenate([down_matrix, gate_columns(gating, rank)], axis=1)
    far_down = lax.ppermute(message, ("groups", "adapter"), FAR)
    tokens2 = move(tokens, PARTNER)
    near_down = move(message, xor_line(1))
    cot2 = move(cotangent, PARTNER)
    far_up = lax.ppermute(up_matrix, ("groups", "adapter"), FAR)
    cross_down = lax.ppermute(far_down, "groups", SWAP)
    near_up = move(jnp.concatenate([up_matrix, far_down[:, width:]], axis=1), xor_line(1))

    gates = [gating] + [gates_of(m[:, width:], capacity) for m in (near_down, far_down, near_up)]
    near_down, far_down, cross_down, near_up = (
        m[:, :width] for m in (near_down, far_down, cross_down, near_up)
    )
    far_bit = jnp.where(first_group, 2, 3)
    experts = jnp.stack([me, me ^ 2, me ^ (2 * far_bit), me ^ (2 * (far_bit ^ 1))])
    lists = jnp.take(token_lists, experts, axis=0)
    gate_rows = adapter_scale_factor * jnp.concatenate(gates)
    token_ids = jnp.arange(tok_local, dtype=jnp.int32)
    ids = jnp.concatenate([me * tok_local + token_ids, (me ^ 1) * tok_local + token_ids])
    taken = lists[:, :, None] == ids[None, None, :]
    scale = jnp.sum(jnp.where(taken, gate_rows[:, :, None], 0.0), axis=1)

    tokens2 = jnp.concatenate([tokens, tokens2], axis=0)
    down_all = jnp.concatenate([down_matrix, near_down, far_down, cross_down], axis=0)

    def low_rank(rows, matrices):
        product = both_cores(contract_last(matrices, rows))
        return narrow(scale[:, None, :] * product.reshape(-1, rank, 2 * tok_local))

    def for_line(low):
        second = jnp.where(first_group, low[2], low[3])
        third = jnp.where(first_group, low[3], low[2])
        return low[0], low[1], second, third

    def outward_start(low, matrix):
        weights = low[:, :, tok_local:].reshape(-1, tok_local)
        return move(narrow(contract_first(weights, matrix)), PARTNER)

    def outward_end(low, matrix, back):
        weights = low[:, :, :tok_local].reshape(-1, tok_local)
        return narrow(contract_first(weights, matrix) + back.astype(jnp.float32))

    low = low_rank(tokens2, down_all)
    cot2, far_up, low = lax.optimization_barrier((cot2, far_up, low))
    cross_up = lax.ppermute(far_up, "groups", SWAP)
    cot2 = jnp.concatenate([cotangent, cot2], axis=0)
    (own, first, second, third), up_send = partial_sums(for_line(low), cot2)
    up_third = move(up_send[2], xor_line(1))
    up_first = move(up_send[0], xor_line(1))

    cross_up = after(cross_up, up_third)
    up_all = jnp.concatenate([up_matrix, near_up, far_up, cross_up], axis=0)
    low_back = low_rank(cot2, up_all)
    branch_back = outward_start(low, up_all)
    (own_b, first_b, second_b, third_b), down_send = partial_sums(for_line(low_back), tokens2)
    down_third = move(down_send[2], xor_line(1))
    down_first = move(after(down_send[0], (up_first, down_third)), xor_line(1))
    input_back = outward_start(low_back, down_all)
    up_far = move(narrow(add_up(second, up_third)), xor_line(2))
    down_far = move(narrow(add_up(second_b, down_third)), xor_line(2))
    branch_out = outward_end(low, up_all, branch_back)
    up_grad = add_up(own, up_first, up_far)
    input_grad = outward_end(low_back, down_all, input_back)
    down_grad = add_up(own_b, down_first, down_far)
    down_grad = (down_grad / capacity).astype(jnp.bfloat16)[None]
    up_grad = (up_grad / capacity).astype(jnp.bfloat16)[None]
    return (branch_out, input_grad, down_grad, up_grad)


def local(*args):
    fits = lax.axis_size("adapter") == OWNERS and lax.axis_size("groups") == 2
    plan = by_pairs if fits else by_rows
    return plan(*args)


def solution(mesh):
    in_specs = (
        P(("groups", "adapter"), "tensor"),
        P(("groups", "adapter"), "tensor"),
        P("adapter", None, "tensor"),
        P("adapter", None, "tensor"),
        P("groups", None),
        P(("groups", "adapter"), None),
    )
    out_specs = (
        P(("groups", "adapter"), "tensor"),
        P(("groups", "adapter"), "tensor"),
        P(("groups", "adapter"), None, "tensor"),
        P(("groups", "adapter"), None, "tensor"),
    )
    return jax.shard_map(local, mesh=mesh, in_specs=in_specs, out_specs=out_specs, check_vma=False)
```

```python
import jax
import jax.numpy as jnp
from jax import lax
from jax.sharding import PartitionSpec as P

adapter_scale_factor = 2.0


def contract_last(left_op, right_op):
    return lax.dot_general(
        left_op, right_op, (((1,), (1,)), ((), ())), preferred_element_type=jnp.float32
    )


def contract_first(left_op, right_op):
    return lax.dot_general(
        left_op, right_op, (((0,), (0,)), ((), ())), preferred_element_type=jnp.float32
    )


def gather_rows(source_rows, local_index, live_slot):
    taken_rows = jnp.take(source_rows, local_index.reshape(-1), axis=0)
    taken_rows = taken_rows.reshape(local_index.shape + (source_rows.shape[1],))
    return jnp.where(live_slot[:, :, None], taken_rows, jnp.zeros_like(taken_rows))


def combine(onehot, returned):
    flat_rows = returned.reshape(-1, returned.shape[-1])
    return jnp.dot(onehot, flat_rows, preferred_element_type=jnp.float32).astype(jnp.bfloat16)


def by_rows(tokens, cotangent, down_adapter, up_adapter, token_lists, gating):
    owners = lax.axis_size("adapter")
    my_index = lax.axis_index("adapter")
    tok_local = tokens.shape[0]
    half_width = tokens.shape[1]
    capacity = gating.shape[1]
    slot_count = 3 * capacity // (2 * owners)
    slot_ids = jnp.arange(slot_count, dtype=jnp.int32)
    source = token_lists // tok_local
    sent_count = jnp.sum((source == my_index).astype(jnp.int32), axis=1)
    sent_start = jnp.sum((source < my_index).astype(jnp.int32), axis=1)
    live_send = slot_ids[None, :] < sent_count[:, None]
    position = jnp.minimum(sent_start[:, None] + slot_ids[None, :], capacity - 1)
    local_index = jnp.take_along_axis(token_lists, position, axis=1) - my_index * tok_local
    local_index = jnp.where(live_send, local_index, 0)
    outgoing_rows = gather_rows(tokens, local_index, live_send)
    cot_send = gather_rows(cotangent, local_index, live_send)
    token_ids = jnp.arange(tok_local, dtype=jnp.int32)
    onehot = ((token_ids[:, None] == local_index.reshape(1, -1)) & live_send.reshape(1, -1)).astype(
        jnp.bfloat16
    )
    own_list = lax.dynamic_slice_in_dim(token_lists, my_index, 1, 0)[0]
    own_source = own_list // tok_local
    peer_ids = jnp.arange(owners, dtype=jnp.int32)
    recv_count = jnp.sum((own_source[None, :] == peer_ids[:, None]).astype(jnp.int32), axis=1)
    received_offset = jnp.sum((own_source[None, :] < peer_ids[:, None]).astype(jnp.int32), axis=1)
    active_received = slot_ids[None, :] < recv_count[:, None]
    gate_pos = jnp.minimum(received_offset[:, None] + slot_ids[None, :], capacity - 1)
    gate_slot_values = jnp.take(gating[0], gate_pos.reshape(-1)).reshape(gate_pos.shape)
    scale_factors = (
        adapter_scale_factor * jnp.where(active_received, gate_slot_values, 0.0)
    ).reshape(-1, 1)
    down_matrix = down_adapter[0]
    up_matrix = up_adapter[0]
    flat_shape = (owners * slot_count, half_width)
    block_shape = (owners, slot_count, half_width)
    row_recv = lax.all_to_all(outgoing_rows, "adapter", split_axis=0, concat_axis=0, tiled=True)
    rows_in = row_recv.reshape(flat_shape)
    low_rank = lax.psum(contract_last(rows_in, down_matrix), "tensor").astype(jnp.bfloat16)
    out_rows = (
        scale_factors * jnp.dot(low_rank, up_matrix, preferred_element_type=jnp.float32)
    ).astype(jnp.bfloat16)
    out_back = lax.all_to_all(
        out_rows.reshape(block_shape), "adapter", split_axis=0, concat_axis=0, tiled=True
    )
    cot_recv = lax.all_to_all(cot_send, "adapter", split_axis=0, concat_axis=0, tiled=True)
    weighted = (scale_factors * cot_recv.reshape(flat_shape)).astype(jnp.bfloat16)
    low_grad = lax.psum(contract_last(weighted, up_matrix), "tensor").astype(jnp.bfloat16)
    back_rows = jnp.dot(low_grad, down_matrix, preferred_element_type=jnp.float32).astype(
        jnp.bfloat16
    )
    grad_back = lax.all_to_all(
        back_rows.reshape(block_shape), "adapter", split_axis=0, concat_axis=0, tiled=True
    )
    branch_out = combine(onehot, out_back)
    input_grad = combine(onehot, grad_back)
    down_grad = (contract_first(low_grad, rows_in) / capacity).astype(jnp.bfloat16)[None]
    up_grad = (contract_first(low_rank, weighted) / capacity).astype(jnp.bfloat16)[None]
    return (branch_out, input_grad, down_grad, up_grad)


PLACES = 4


def on_line(pairs):
    return [(2 * a + side, 2 * b + side) for a, b in pairs for side in (0, 1)]


def xor_line(bit):
    return on_line([(a, a ^ bit) for a in range(PLACES)])


PARTNER = [(2 * a + side, 2 * a + 1 - side) for a in range(PLACES) for side in (0, 1)]
SWAP = [(0, 1), (1, 0)]
OWNERS = 2 * PLACES
FAR = xor_line(2) + [(OWNERS + a, OWNERS + b) for a, b in xor_line(3)]


def move(value, pairs):
    return lax.ppermute(value, "adapter", pairs)


def after(value, earlier):
    return lax.optimization_barrier((value, earlier))[0]


def narrow(value):
    return value.astype(jnp.bfloat16)


def add_up(*values):
    total = values[0]
    for value in values[1:]:
        total = total + value.astype(jnp.float32)
    return total


def partial_sums(weights, rows):
    parts = [jnp.dot(weight, rows, preferred_element_type=jnp.float32) for weight in weights]
    return lax.optimization_barrier((parts, [narrow(part) for part in parts[1:]]))


def both_cores(partial):
    return partial + lax.ppermute(partial, "tensor", SWAP)


def gather_gates(gating):
    pair = jnp.concatenate([gating, move(gating, xor_line(1))])
    return jnp.concatenate([pair, move(pair, xor_line(2))])


def by_pairs(tokens, cotangent, down_adapter, up_adapter, token_lists, gating):
    me = lax.axis_index("adapter")
    first_group = lax.axis_index("groups") == 0
    tok_local = tokens.shape[0]
    capacity = gating.shape[1]
    down_matrix = down_adapter[0]
    up_matrix = up_adapter[0]
    rank = down_matrix.shape[0]

    far_down = lax.ppermute(down_matrix, ("groups", "adapter"), FAR)
    tokens2 = move(tokens, PARTNER)
    near_down = move(down_matrix, xor_line(1))
    cot2 = move(cotangent, PARTNER)
    near_up = move(up_matrix, xor_line(1))
    gates = gather_gates(gating)

    far_bit = jnp.where(first_group, 2, 3)
    experts = jnp.stack([me, me ^ 2, me ^ (2 * far_bit), me ^ (2 * (far_bit ^ 1))])
    lists = jnp.take(token_lists, experts, axis=0)
    crossed = jnp.concatenate([gates[:2], gates[3:], gates[2:3]])
    gate_rows = adapter_scale_factor * jnp.where(first_group, gates, crossed)
    token_ids = jnp.arange(tok_local, dtype=jnp.int32)
    ids = jnp.concatenate([me * tok_local + token_ids, (me ^ 1) * tok_local + token_ids])
    taken = lists[:, :, None] == ids[None, None, :]
    scale = jnp.sum(jnp.where(taken, gate_rows[:, :, None], 0.0), axis=1)

    tokens2 = jnp.concatenate([tokens, tokens2], axis=0)
    up_later, scale = lax.optimization_barrier((up_matrix, scale))
    far_up = lax.ppermute(up_later, ("groups", "adapter"), FAR)
    ready, scale = lax.optimization_barrier((far_down, scale))
    cross_down = lax.ppermute(ready, "groups", SWAP)
    down_all = jnp.concatenate([down_matrix, near_down, far_down, cross_down], axis=0)

    def low_rank(rows, matrices):
        product = both_cores(contract_last(matrices, rows))
        return narrow(scale[:, None, :] * product.reshape(-1, rank, 2 * tok_local))

    def for_line(low):
        second = jnp.where(first_group, low[2], low[3])
        third = jnp.where(first_group, low[3], low[2])
        return low[0], low[1], second, third

    def outward_start(low, matrix):
        weights = low[:, :, tok_local:].reshape(-1, tok_local)
        return move(narrow(contract_first(weights, matrix)), PARTNER)

    def outward_end(low, matrix, back):
        weights = low[:, :, :tok_local].reshape(-1, tok_local)
        return narrow(contract_first(weights, matrix) + back.astype(jnp.float32))

    low = low_rank(tokens2, down_all)
    cot2, far_up, near_up, low = lax.optimization_barrier((cot2, far_up, near_up, low))
    cross_up = lax.ppermute(far_up, "groups", SWAP)
    cot2 = jnp.concatenate([cotangent, cot2], axis=0)
    (own, first, second, third), up_send = partial_sums(for_line(low), cot2)
    up_third = move(up_send[2], xor_line(1))
    up_first = move(up_send[0], xor_line(1))

    cross_up = after(cross_up, up_third)
    up_all = jnp.concatenate([up_matrix, near_up, far_up, cross_up], axis=0)
    low_back = low_rank(cot2, up_all)
    (own_b, first_b, second_b, third_b), down_send = partial_sums(for_line(low_back), tokens2)
    down_third = move(down_send[2], xor_line(1))
    branch_back = outward_start(after(low, down_send), up_all)
    input_back = outward_start(low_back, down_all)
    up_far = move(narrow(add_up(second, up_third)), xor_line(2))
    down_sum = narrow(add_up(second_b, down_third))
    down_far = move(down_sum, xor_line(2))
    down_first = move(after(down_send[0], (up_first, down_sum)), xor_line(1))
    branch_out = outward_end(low, up_all, branch_back)
    up_grad = add_up(own, up_first, up_far)
    input_grad = outward_end(low_back, down_all, input_back)
    down_grad = add_up(own_b, down_first, down_far)
    down_grad = (down_grad / capacity).astype(jnp.bfloat16)[None]
    up_grad = (up_grad / capacity).astype(jnp.bfloat16)[None]
    return (branch_out, input_grad, down_grad, up_grad)


def local(*args):
    fits = lax.axis_size("adapter") == OWNERS and lax.axis_size("groups") == 2
    plan = by_pairs if fits else by_rows
    return plan(*args)


def solution(mesh):
    in_specs = (
        P(("groups", "adapter"), "tensor"),
        P(("groups", "adapter"), "tensor"),
        P("adapter", None, "tensor"),
        P("adapter", None, "tensor"),
        P("groups", None),
        P(("groups", "adapter"), None),
    )
    out_specs = (
        P(("groups", "adapter"), "tensor"),
        P(("groups", "adapter"), "tensor"),
        P(("groups", "adapter"), None, "tensor"),
        P(("groups", "adapter"), None, "tensor"),
    )
    return jax.shard_map(local, mesh=mesh, in_specs=in_specs, out_specs=out_specs, check_vma=False)
```

```python
import jax
import jax.numpy as jnp
from jax import lax
from jax.sharding import PartitionSpec as P

adapter_scale_factor = 2.0


def contract_last(left_op, right_op):
    return lax.dot_general(
        left_op, right_op, (((1,), (1,)), ((), ())), preferred_element_type=jnp.float32
    )


def contract_first(left_op, right_op):
    return lax.dot_general(
        left_op, right_op, (((0,), (0,)), ((), ())), preferred_element_type=jnp.float32
    )


def gather_rows(source_rows, local_index, live_slot):
    taken_rows = jnp.take(source_rows, local_index.reshape(-1), axis=0)
    taken_rows = taken_rows.reshape(local_index.shape + (source_rows.shape[1],))
    return jnp.where(live_slot[:, :, None], taken_rows, jnp.zeros_like(taken_rows))


def combine(onehot, returned):
    flat_rows = returned.reshape(-1, returned.shape[-1])
    return jnp.dot(onehot, flat_rows, preferred_element_type=jnp.float32).astype(jnp.bfloat16)


def by_rows(tokens, cotangent, down_adapter, up_adapter, token_lists, gating):
    owners = lax.axis_size("adapter")
    my_index = lax.axis_index("adapter")
    tok_local = tokens.shape[0]
    half_width = tokens.shape[1]
    capacity = gating.shape[1]
    slot_count = 3 * capacity // (2 * owners)
    slot_ids = jnp.arange(slot_count, dtype=jnp.int32)
    source = token_lists // tok_local
    sent_count = jnp.sum((source == my_index).astype(jnp.int32), axis=1)
    sent_start = jnp.sum((source < my_index).astype(jnp.int32), axis=1)
    live_send = slot_ids[None, :] < sent_count[:, None]
    position = jnp.minimum(sent_start[:, None] + slot_ids[None, :], capacity - 1)
    local_index = jnp.take_along_axis(token_lists, position, axis=1) - my_index * tok_local
    local_index = jnp.where(live_send, local_index, 0)
    outgoing_rows = gather_rows(tokens, local_index, live_send)
    cot_send = gather_rows(cotangent, local_index, live_send)
    token_ids = jnp.arange(tok_local, dtype=jnp.int32)
    onehot = ((token_ids[:, None] == local_index.reshape(1, -1)) & live_send.reshape(1, -1)).astype(
        jnp.bfloat16
    )
    own_list = lax.dynamic_slice_in_dim(token_lists, my_index, 1, 0)[0]
    own_source = own_list // tok_local
    peer_ids = jnp.arange(owners, dtype=jnp.int32)
    recv_count = jnp.sum((own_source[None, :] == peer_ids[:, None]).astype(jnp.int32), axis=1)
    received_offset = jnp.sum((own_source[None, :] < peer_ids[:, None]).astype(jnp.int32), axis=1)
    active_received = slot_ids[None, :] < recv_count[:, None]
    gate_pos = jnp.minimum(received_offset[:, None] + slot_ids[None, :], capacity - 1)
    gate_slot_values = jnp.take(gating[0], gate_pos.reshape(-1)).reshape(gate_pos.shape)
    scale_factors = (
        adapter_scale_factor * jnp.where(active_received, gate_slot_values, 0.0)
    ).reshape(-1, 1)
    down_matrix = down_adapter[0]
    up_matrix = up_adapter[0]
    flat_shape = (owners * slot_count, half_width)
    block_shape = (owners, slot_count, half_width)
    row_recv = lax.all_to_all(outgoing_rows, "adapter", split_axis=0, concat_axis=0, tiled=True)
    rows_in = row_recv.reshape(flat_shape)
    low_rank = lax.psum(contract_last(rows_in, down_matrix), "tensor").astype(jnp.bfloat16)
    out_rows = (
        scale_factors * jnp.dot(low_rank, up_matrix, preferred_element_type=jnp.float32)
    ).astype(jnp.bfloat16)
    out_back = lax.all_to_all(
        out_rows.reshape(block_shape), "adapter", split_axis=0, concat_axis=0, tiled=True
    )
    cot_recv = lax.all_to_all(cot_send, "adapter", split_axis=0, concat_axis=0, tiled=True)
    weighted = (scale_factors * cot_recv.reshape(flat_shape)).astype(jnp.bfloat16)
    low_grad = lax.psum(contract_last(weighted, up_matrix), "tensor").astype(jnp.bfloat16)
    back_rows = jnp.dot(low_grad, down_matrix, preferred_element_type=jnp.float32).astype(
        jnp.bfloat16
    )
    grad_back = lax.all_to_all(
        back_rows.reshape(block_shape), "adapter", split_axis=0, concat_axis=0, tiled=True
    )
    branch_out = combine(onehot, out_back)
    input_grad = combine(onehot, grad_back)
    down_grad = (contract_first(low_grad, rows_in) / capacity).astype(jnp.bfloat16)[None]
    up_grad = (contract_first(low_rank, weighted) / capacity).astype(jnp.bfloat16)[None]
    return (branch_out, input_grad, down_grad, up_grad)


PLACES = 4


def on_line(pairs):
    return [(2 * a + side, 2 * b + side) for a, b in pairs for side in (0, 1)]


def xor_line(bit):
    return on_line([(a, a ^ bit) for a in range(PLACES)])


PARTNER = [(2 * a + side, 2 * a + 1 - side) for a in range(PLACES) for side in (0, 1)]
SWAP = [(0, 1), (1, 0)]
OWNERS = 2 * PLACES
FAR = xor_line(2) + [(OWNERS + a, OWNERS + b) for a, b in xor_line(3)]


def move(value, pairs):
    return lax.ppermute(value, "adapter", pairs)


def after(value, earlier):
    return lax.optimization_barrier((value, earlier))[0]


def narrow(value):
    return value.astype(jnp.bfloat16)


def add_up(*values):
    total = values[0]
    for value in values[1:]:
        total = total + value.astype(jnp.float32)
    return total


def partial_sums(weights, rows):
    parts = [jnp.dot(weight, rows, preferred_element_type=jnp.float32) for weight in weights]
    return lax.optimization_barrier((parts, [narrow(part) for part in parts[1:]]))


def both_cores(partial):
    return partial + lax.ppermute(partial, "tensor", SWAP)


def by_pairs(tokens, cotangent, down_adapter, up_adapter, token_lists, gating):
    me = lax.axis_index("adapter")
    first_group = lax.axis_index("groups") == 0
    tok_local = tokens.shape[0]
    capacity = gating.shape[1]
    down_matrix = down_adapter[0]
    up_matrix = up_adapter[0]
    rank = down_matrix.shape[0]

    far_down = lax.ppermute(down_matrix, ("groups", "adapter"), FAR)
    tokens2 = move(tokens, PARTNER)
    near_gate, down_later = lax.optimization_barrier((move(gating, xor_line(1)), down_matrix))
    near_down = move(down_later, xor_line(1))
    cot2 = move(cotangent, PARTNER)
    near_up = move(up_matrix, xor_line(1))
    gates = jnp.concatenate([gating, near_gate])
    gates = jnp.concatenate([gates, move(gates, xor_line(2))])

    far_bit = jnp.where(first_group, 2, 3)
    experts = jnp.stack([me, me ^ 2, me ^ (2 * far_bit), me ^ (2 * (far_bit ^ 1))])
    lists = jnp.take(token_lists, experts, axis=0)
    crossed = jnp.concatenate([gates[:2], gates[3:], gates[2:3]])
    gate_rows = adapter_scale_factor * jnp.where(first_group, gates, crossed)
    token_ids = jnp.arange(tok_local, dtype=jnp.int32)
    ids = jnp.concatenate([me * tok_local + token_ids, (me ^ 1) * tok_local + token_ids])
    taken = lists[:, :, None] == ids[None, None, :]
    scale = jnp.sum(jnp.where(taken, gate_rows[:, :, None], 0.0), axis=1)

    tokens2 = jnp.concatenate([tokens, tokens2], axis=0)
    up_later, scale = lax.optimization_barrier((up_matrix, scale))
    far_up = lax.ppermute(up_later, ("groups", "adapter"), FAR)
    ready, scale = lax.optimization_barrier((far_down, scale))
    cross_down = lax.ppermute(ready, "groups", SWAP)
    down_all = jnp.concatenate([down_matrix, near_down, far_down, cross_down], axis=0)

    def low_rank(rows, matrices):
        product = both_cores(contract_last(matrices, rows))
        return narrow(scale[:, None, :] * product.reshape(-1, rank, 2 * tok_local))

    def for_line(low):
        second = jnp.where(first_group, low[2], low[3])
        third = jnp.where(first_group, low[3], low[2])
        return low[0], low[1], second, third

    def outward_start(low, matrix):
        weights = low[:, :, tok_local:].reshape(-1, tok_local)
        return move(narrow(contract_first(weights, matrix)), PARTNER)

    def outward_end(low, matrix, back):
        weights = low[:, :, :tok_local].reshape(-1, tok_local)
        return narrow(contract_first(weights, matrix) + back.astype(jnp.float32))

    low = low_rank(tokens2, down_all)
    cot2, far_up, near_up, low = lax.optimization_barrier((cot2, far_up, near_up, low))
    cross_up = lax.ppermute(far_up, "groups", SWAP)
    cot2 = jnp.concatenate([cotangent, cot2], axis=0)
    (own, first, second, third), up_send = partial_sums(for_line(low), cot2)
    up_third = move(up_send[2], xor_line(1))
    up_first = move(up_send[0], xor_line(1))

    cross_up = after(cross_up, up_third)
    up_all = jnp.concatenate([up_matrix, near_up, far_up, cross_up], axis=0)
    low_back = low_rank(cot2, up_all)
    (own_b, first_b, second_b, third_b), down_send = partial_sums(for_line(low_back), tokens2)
    down_third = move(down_send[2], xor_line(1))
    branch_back = outward_start(low, up_all)
    input_back = outward_start(low_back, down_all)
    up_far = move(narrow(add_up(second, up_third)), xor_line(2))
    down_sum = narrow(add_up(second_b, down_third))
    down_far = move(down_sum, xor_line(2))
    down_first = move(after(down_send[0], (up_first, down_sum)), xor_line(1))
    branch_out = outward_end(low, up_all, branch_back)
    up_grad = add_up(own, up_first, up_far)
    input_grad = outward_end(low_back, down_all, input_back)
    down_grad = add_up(own_b, down_first, down_far)
    down_grad = (down_grad / capacity).astype(jnp.bfloat16)[None]
    up_grad = (up_grad / capacity).astype(jnp.bfloat16)[None]
    return (branch_out, input_grad, down_grad, up_grad)


def local(*args):
    fits = lax.axis_size("adapter") == OWNERS and lax.axis_size("groups") == 2
    plan = by_pairs if fits else by_rows
    return plan(*args)


def solution(mesh):
    in_specs = (
        P(("groups", "adapter"), "tensor"),
        P(("groups", "adapter"), "tensor"),
        P("adapter", None, "tensor"),
        P("adapter", None, "tensor"),
        P("groups", None),
        P(("groups", "adapter"), None),
    )
    out_specs = (
        P(("groups", "adapter"), "tensor"),
        P(("groups", "adapter"), "tensor"),
        P(("groups", "adapter"), None, "tensor"),
        P(("groups", "adapter"), None, "tensor"),
    )
    return jax.shard_map(local, mesh=mesh, in_specs=in_specs, out_specs=out_specs, check_vma=False)
```

```python
import jax
import jax.numpy as jnp
from jax import lax
from jax.sharding import PartitionSpec as P

adapter_scale_factor = 2.0


def contract_last(left_op, right_op):
    return lax.dot_general(
        left_op, right_op, (((1,), (1,)), ((), ())), preferred_element_type=jnp.float32
    )


def contract_first(left_op, right_op):
    return lax.dot_general(
        left_op, right_op, (((0,), (0,)), ((), ())), preferred_element_type=jnp.float32
    )


def gather_rows(source_rows, local_index, live_slot):
    taken_rows = jnp.take(source_rows, local_index.reshape(-1), axis=0)
    taken_rows = taken_rows.reshape(local_index.shape + (source_rows.shape[1],))
    return jnp.where(live_slot[:, :, None], taken_rows, jnp.zeros_like(taken_rows))


def combine(onehot, returned):
    flat_rows = returned.reshape(-1, returned.shape[-1])
    return jnp.dot(onehot, flat_rows, preferred_element_type=jnp.float32).astype(jnp.bfloat16)


def by_rows(tokens, cotangent, down_adapter, up_adapter, token_lists, gating):
    owners = lax.axis_size("adapter")
    my_index = lax.axis_index("adapter")
    tok_local = tokens.shape[0]
    half_width = tokens.shape[1]
    capacity = gating.shape[1]
    slot_count = 3 * capacity // (2 * owners)
    slot_ids = jnp.arange(slot_count, dtype=jnp.int32)
    source = token_lists // tok_local
    sent_count = jnp.sum((source == my_index).astype(jnp.int32), axis=1)
    sent_start = jnp.sum((source < my_index).astype(jnp.int32), axis=1)
    live_send = slot_ids[None, :] < sent_count[:, None]
    position = jnp.minimum(sent_start[:, None] + slot_ids[None, :], capacity - 1)
    local_index = jnp.take_along_axis(token_lists, position, axis=1) - my_index * tok_local
    local_index = jnp.where(live_send, local_index, 0)
    outgoing_rows = gather_rows(tokens, local_index, live_send)
    cot_send = gather_rows(cotangent, local_index, live_send)
    token_ids = jnp.arange(tok_local, dtype=jnp.int32)
    onehot = ((token_ids[:, None] == local_index.reshape(1, -1)) & live_send.reshape(1, -1)).astype(
        jnp.bfloat16
    )
    own_list = lax.dynamic_slice_in_dim(token_lists, my_index, 1, 0)[0]
    own_source = own_list // tok_local
    peer_ids = jnp.arange(owners, dtype=jnp.int32)
    recv_count = jnp.sum((own_source[None, :] == peer_ids[:, None]).astype(jnp.int32), axis=1)
    received_offset = jnp.sum((own_source[None, :] < peer_ids[:, None]).astype(jnp.int32), axis=1)
    active_received = slot_ids[None, :] < recv_count[:, None]
    gate_pos = jnp.minimum(received_offset[:, None] + slot_ids[None, :], capacity - 1)
    gate_slot_values = jnp.take(gating[0], gate_pos.reshape(-1)).reshape(gate_pos.shape)
    scale_factors = (
        adapter_scale_factor * jnp.where(active_received, gate_slot_values, 0.0)
    ).reshape(-1, 1)
    down_matrix = down_adapter[0]
    up_matrix = up_adapter[0]
    flat_shape = (owners * slot_count, half_width)
    block_shape = (owners, slot_count, half_width)
    row_recv = lax.all_to_all(outgoing_rows, "adapter", split_axis=0, concat_axis=0, tiled=True)
    rows_in = row_recv.reshape(flat_shape)
    low_rank = lax.psum(contract_last(rows_in, down_matrix), "tensor").astype(jnp.bfloat16)
    out_rows = (
        scale_factors * jnp.dot(low_rank, up_matrix, preferred_element_type=jnp.float32)
    ).astype(jnp.bfloat16)
    out_back = lax.all_to_all(
        out_rows.reshape(block_shape), "adapter", split_axis=0, concat_axis=0, tiled=True
    )
    cot_recv = lax.all_to_all(cot_send, "adapter", split_axis=0, concat_axis=0, tiled=True)
    weighted = (scale_factors * cot_recv.reshape(flat_shape)).astype(jnp.bfloat16)
    low_grad = lax.psum(contract_last(weighted, up_matrix), "tensor").astype(jnp.bfloat16)
    back_rows = jnp.dot(low_grad, down_matrix, preferred_element_type=jnp.float32).astype(
        jnp.bfloat16
    )
    grad_back = lax.all_to_all(
        back_rows.reshape(block_shape), "adapter", split_axis=0, concat_axis=0, tiled=True
    )
    branch_out = combine(onehot, out_back)
    input_grad = combine(onehot, grad_back)
    down_grad = (contract_first(low_grad, rows_in) / capacity).astype(jnp.bfloat16)[None]
    up_grad = (contract_first(low_rank, weighted) / capacity).astype(jnp.bfloat16)[None]
    return (branch_out, input_grad, down_grad, up_grad)


PLACES = 4


def on_line(pairs):
    return [(2 * a + side, 2 * b + side) for a, b in pairs for side in (0, 1)]


def xor_line(bit):
    return on_line([(a, a ^ bit) for a in range(PLACES)])


PARTNER = [(2 * a + side, 2 * a + 1 - side) for a in range(PLACES) for side in (0, 1)]
SWAP = [(0, 1), (1, 0)]
OWNERS = 2 * PLACES
FAR = xor_line(2) + [(OWNERS + a, OWNERS + b) for a, b in xor_line(3)]


def move(value, pairs):
    return lax.ppermute(value, "adapter", pairs)


def after(value, earlier):
    return lax.optimization_barrier((value, earlier))[0]


def narrow(value):
    return value.astype(jnp.bfloat16)


def add_up(*values):
    total = values[0]
    for value in values[1:]:
        total = total + value.astype(jnp.float32)
    return total


def partial_sums(weights, rows):
    parts = [jnp.dot(weight, rows, preferred_element_type=jnp.float32) for weight in weights]
    return lax.optimization_barrier((parts, [narrow(part) for part in parts[1:]]))


def both_cores(partial):
    return partial + lax.ppermute(partial, "tensor", SWAP)


def by_pairs(tokens, cotangent, down_adapter, up_adapter, token_lists, gating):
    me = lax.axis_index("adapter")
    first_group = lax.axis_index("groups") == 0
    tok_local = tokens.shape[0]
    capacity = gating.shape[1]
    down_matrix = down_adapter[0]
    up_matrix = up_adapter[0]
    rank = down_matrix.shape[0]

    far_down = lax.ppermute(down_matrix, ("groups", "adapter"), FAR)
    tokens2 = move(tokens, PARTNER)
    near_gate, down_later = lax.optimization_barrier((move(gating, xor_line(1)), down_matrix))
    near_down = move(down_later, xor_line(1))
    cot2 = move(cotangent, PARTNER)
    gates = jnp.concatenate([gating, near_gate])
    gates = jnp.concatenate([gates, move(gates, xor_line(2))])

    far_bit = jnp.where(first_group, 2, 3)
    experts = jnp.stack([me, me ^ 2, me ^ (2 * far_bit), me ^ (2 * (far_bit ^ 1))])
    lists = jnp.take(token_lists, experts, axis=0)
    crossed = jnp.concatenate([gates[:2], gates[3:], gates[2:3]])
    gate_rows = adapter_scale_factor * jnp.where(first_group, gates, crossed)
    token_ids = jnp.arange(tok_local, dtype=jnp.int32)
    ids = jnp.concatenate([me * tok_local + token_ids, (me ^ 1) * tok_local + token_ids])
    taken = lists[:, :, None] == ids[None, None, :]
    scale = jnp.sum(jnp.where(taken, gate_rows[:, :, None], 0.0), axis=1)

    up_later, tokens2, scale = lax.optimization_barrier((up_matrix, tokens2, scale))
    far_up = lax.ppermute(up_later, ("groups", "adapter"), FAR)
    near_up = move(up_later, xor_line(1))
    ready, near_down, scale = lax.optimization_barrier((far_down, near_down, scale))
    cross_down = lax.ppermute(ready, "groups", SWAP)
    tokens2 = jnp.concatenate([tokens, tokens2], axis=0)
    down_all = jnp.concatenate([down_matrix, near_down, far_down, cross_down], axis=0)

    def most_products(rows, *matrices):
        return both_cores(contract_last(jnp.concatenate(matrices), rows))

    def low_rank(most, rows, matrix):
        products = [most[k * rank : (k + 1) * rank] for k in range(3)]
        products.append(both_cores(contract_last(matrix, rows)))
        return [narrow(scale[k] * product) for k, product in enumerate(products)]

    def for_line(low):
        second = jnp.where(first_group, low[2], low[3])
        third = jnp.where(first_group, low[3], low[2])
        return low[0], low[1], second, third

    def outward_start(low, matrix):
        weights = jnp.concatenate([slot[:, tok_local:] for slot in low])
        return move(narrow(contract_first(weights, matrix)), PARTNER)

    def outward_end(low, matrix, back):
        weights = jnp.concatenate([slot[:, :tok_local] for slot in low])
        return narrow(contract_first(weights, matrix) + back.astype(jnp.float32))

    most = most_products(tokens2, down_matrix, near_down, far_down)
    low = low_rank(most, tokens2, cross_down)
    cot2, far_up, near_up, low = lax.optimization_barrier((cot2, far_up, near_up, low))
    cross_up = lax.ppermute(far_up, "groups", SWAP)
    cot2 = jnp.concatenate([cotangent, cot2], axis=0)
    (own, first, second, third), up_send = partial_sums(for_line(low), cot2)
    up_third = move(up_send[2], xor_line(1))
    most = most_products(cot2, up_matrix, near_up, far_up)
    most, up_next = lax.optimization_barrier((most, up_send[0]))
    up_first = move(up_next, xor_line(1))

    cross_up = after(cross_up, up_third)
    up_all = jnp.concatenate([up_matrix, near_up, far_up, cross_up], axis=0)
    low_back = low_rank(most, cot2, cross_up)
    (own_b, first_b, second_b, third_b), down_send = partial_sums(for_line(low_back), tokens2)
    down_third = move(down_send[2], xor_line(1))
    branch_back = outward_start(low, up_all)
    input_back = outward_start(low_back, down_all)
    up_far = move(narrow(add_up(second, up_third)), xor_line(2))
    down_sum = narrow(add_up(second_b, down_third))
    down_far = move(down_sum, xor_line(2))
    down_first = move(after(down_send[0], (up_first, down_sum)), xor_line(1))
    branch_out = outward_end(low, up_all, branch_back)
    up_grad = add_up(own, up_first, up_far)
    input_grad = outward_end(low_back, down_all, input_back)
    down_grad = add_up(own_b, down_first, down_far)
    down_grad = (down_grad / capacity).astype(jnp.bfloat16)[None]
    up_grad = (up_grad / capacity).astype(jnp.bfloat16)[None]
    return (branch_out, input_grad, down_grad, up_grad)


def local(*args):
    fits = lax.axis_size("adapter") == OWNERS and lax.axis_size("groups") == 2
    plan = by_pairs if fits else by_rows
    return plan(*args)


def solution(mesh):
    in_specs = (
        P(("groups", "adapter"), "tensor"),
        P(("groups", "adapter"), "tensor"),
        P("adapter", None, "tensor"),
        P("adapter", None, "tensor"),
        P("groups", None),
        P(("groups", "adapter"), None),
    )
    out_specs = (
        P(("groups", "adapter"), "tensor"),
        P(("groups", "adapter"), "tensor"),
        P(("groups", "adapter"), None, "tensor"),
        P(("groups", "adapter"), None, "tensor"),
    )
    return jax.shard_map(local, mesh=mesh, in_specs=in_specs, out_specs=out_specs, check_vma=False)
```

```python
import jax
import jax.numpy as jnp
from jax import lax
from jax.sharding import PartitionSpec as P

adapter_scale_factor = 2.0


def contract_last(left_op, right_op):
    return lax.dot_general(
        left_op, right_op, (((1,), (1,)), ((), ())), preferred_element_type=jnp.float32
    )


def contract_first(left_op, right_op):
    return lax.dot_general(
        left_op, right_op, (((0,), (0,)), ((), ())), preferred_element_type=jnp.float32
    )


def gather_rows(source_rows, local_index, live_slot):
    taken_rows = jnp.take(source_rows, local_index.reshape(-1), axis=0)
    taken_rows = taken_rows.reshape(local_index.shape + (source_rows.shape[1],))
    return jnp.where(live_slot[:, :, None], taken_rows, jnp.zeros_like(taken_rows))


def combine(onehot, returned):
    flat_rows = returned.reshape(-1, returned.shape[-1])
    return jnp.dot(onehot, flat_rows, preferred_element_type=jnp.float32).astype(jnp.bfloat16)


def by_rows(tokens, cotangent, down_adapter, up_adapter, token_lists, gating):
    owners = lax.axis_size("adapter")
    my_index = lax.axis_index("adapter")
    tok_local = tokens.shape[0]
    half_width = tokens.shape[1]
    capacity = gating.shape[1]
    slot_count = 3 * capacity // (2 * owners)
    slot_ids = jnp.arange(slot_count, dtype=jnp.int32)
    source = token_lists // tok_local
    sent_count = jnp.sum((source == my_index).astype(jnp.int32), axis=1)
    sent_start = jnp.sum((source < my_index).astype(jnp.int32), axis=1)
    live_send = slot_ids[None, :] < sent_count[:, None]
    position = jnp.minimum(sent_start[:, None] + slot_ids[None, :], capacity - 1)
    local_index = jnp.take_along_axis(token_lists, position, axis=1) - my_index * tok_local
    local_index = jnp.where(live_send, local_index, 0)
    outgoing_rows = gather_rows(tokens, local_index, live_send)
    cot_send = gather_rows(cotangent, local_index, live_send)
    token_ids = jnp.arange(tok_local, dtype=jnp.int32)
    onehot = ((token_ids[:, None] == local_index.reshape(1, -1)) & live_send.reshape(1, -1)).astype(
        jnp.bfloat16
    )
    own_list = lax.dynamic_slice_in_dim(token_lists, my_index, 1, 0)[0]
    own_source = own_list // tok_local
    peer_ids = jnp.arange(owners, dtype=jnp.int32)
    recv_count = jnp.sum((own_source[None, :] == peer_ids[:, None]).astype(jnp.int32), axis=1)
    received_offset = jnp.sum((own_source[None, :] < peer_ids[:, None]).astype(jnp.int32), axis=1)
    active_received = slot_ids[None, :] < recv_count[:, None]
    gate_pos = jnp.minimum(received_offset[:, None] + slot_ids[None, :], capacity - 1)
    gate_slot_values = jnp.take(gating[0], gate_pos.reshape(-1)).reshape(gate_pos.shape)
    scale_factors = (
        adapter_scale_factor * jnp.where(active_received, gate_slot_values, 0.0)
    ).reshape(-1, 1)
    down_matrix = down_adapter[0]
    up_matrix = up_adapter[0]
    flat_shape = (owners * slot_count, half_width)
    block_shape = (owners, slot_count, half_width)
    row_recv = lax.all_to_all(outgoing_rows, "adapter", split_axis=0, concat_axis=0, tiled=True)
    rows_in = row_recv.reshape(flat_shape)
    low_rank = lax.psum(contract_last(rows_in, down_matrix), "tensor").astype(jnp.bfloat16)
    out_rows = (
        scale_factors * jnp.dot(low_rank, up_matrix, preferred_element_type=jnp.float32)
    ).astype(jnp.bfloat16)
    out_back = lax.all_to_all(
        out_rows.reshape(block_shape), "adapter", split_axis=0, concat_axis=0, tiled=True
    )
    cot_recv = lax.all_to_all(cot_send, "adapter", split_axis=0, concat_axis=0, tiled=True)
    weighted = (scale_factors * cot_recv.reshape(flat_shape)).astype(jnp.bfloat16)
    low_grad = lax.psum(contract_last(weighted, up_matrix), "tensor").astype(jnp.bfloat16)
    back_rows = jnp.dot(low_grad, down_matrix, preferred_element_type=jnp.float32).astype(
        jnp.bfloat16
    )
    grad_back = lax.all_to_all(
        back_rows.reshape(block_shape), "adapter", split_axis=0, concat_axis=0, tiled=True
    )
    branch_out = combine(onehot, out_back)
    input_grad = combine(onehot, grad_back)
    down_grad = (contract_first(low_grad, rows_in) / capacity).astype(jnp.bfloat16)[None]
    up_grad = (contract_first(low_rank, weighted) / capacity).astype(jnp.bfloat16)[None]
    return (branch_out, input_grad, down_grad, up_grad)


PLACES = 4


def on_line(pairs):
    return [(2 * a + side, 2 * b + side) for a, b in pairs for side in (0, 1)]


def xor_line(bit):
    return on_line([(a, a ^ bit) for a in range(PLACES)])


PARTNER = [(2 * a + side, 2 * a + 1 - side) for a in range(PLACES) for side in (0, 1)]
SWAP = [(0, 1), (1, 0)]
OWNERS = 2 * PLACES
FAR = xor_line(2) + [(OWNERS + a, OWNERS + b) for a, b in xor_line(3)]


def move(value, pairs):
    return lax.ppermute(value, "adapter", pairs)


def after(value, earlier):
    return lax.optimization_barrier((value, earlier))[0]


def narrow(value):
    return value.astype(jnp.bfloat16)


def add_up(*values):
    total = values[0]
    for value in values[1:]:
        total = total + value.astype(jnp.float32)
    return total


def partial_sums(weights, rows):
    parts = [jnp.dot(weight, rows, preferred_element_type=jnp.float32) for weight in weights]
    return lax.optimization_barrier((parts, [narrow(part) for part in parts[1:]]))


def both_cores(partial):
    return partial + lax.ppermute(partial, "tensor", SWAP)


def by_pairs(tokens, cotangent, down_adapter, up_adapter, token_lists, gating):
    me = lax.axis_index("adapter")
    first_group = lax.axis_index("groups") == 0
    tok_local = tokens.shape[0]
    capacity = gating.shape[1]
    down_matrix = down_adapter[0]
    up_matrix = up_adapter[0]
    rank = down_matrix.shape[0]

    far_down = lax.ppermute(down_matrix, ("groups", "adapter"), FAR)
    tokens2 = move(tokens, PARTNER)
    near_gate, down_later, up_later = lax.optimization_barrier(
        (move(gating, xor_line(1)), down_matrix, up_matrix)
    )
    near_down, up_last = lax.optimization_barrier((move(down_later, xor_line(1)), up_matrix))
    near_up = move(up_last, xor_line(1))
    cot2 = move(cotangent, PARTNER)
    gates = jnp.concatenate([gating, near_gate])
    gates = jnp.concatenate([gates, move(gates, xor_line(2))])

    far_bit = jnp.where(first_group, 2, 3)
    experts = jnp.stack([me, me ^ 2, me ^ (2 * far_bit), me ^ (2 * (far_bit ^ 1))])
    lists = jnp.take(token_lists, experts, axis=0)
    crossed = jnp.concatenate([gates[:2], gates[3:], gates[2:3]])
    gate_rows = adapter_scale_factor * jnp.where(first_group, gates, crossed)
    token_ids = jnp.arange(tok_local, dtype=jnp.int32)
    ids = jnp.concatenate([me * tok_local + token_ids, (me ^ 1) * tok_local + token_ids])
    taken = lists[:, :, None] == ids[None, None, :]
    scale = jnp.sum(jnp.where(taken, gate_rows[:, :, None], 0.0), axis=1)

    far_up = lax.ppermute(up_later, ("groups", "adapter"), FAR)
    ready, scale = lax.optimization_barrier((far_down, scale))
    cross_down = lax.ppermute(ready, "groups", SWAP)
    tokens2 = jnp.concatenate([tokens, tokens2], axis=0)
    down_all = jnp.concatenate([down_matrix, near_down, far_down, cross_down], axis=0)

    def most_products(rows, *matrices):
        return both_cores(contract_last(jnp.concatenate(matrices), rows))

    def low_rank(most, rows, matrix):
        products = [most[k * rank : (k + 1) * rank] for k in range(3)]
        products.append(both_cores(contract_last(matrix, rows)))
        return [narrow(scale[k] * product) for k, product in enumerate(products)]

    def for_line(low):
        second = jnp.where(first_group, low[2], low[3])
        third = jnp.where(first_group, low[3], low[2])
        return low[0], low[1], second, third

    def outward_start(low, matrix):
        weights = jnp.concatenate([slot[:, tok_local:] for slot in low])
        return move(narrow(contract_first(weights, matrix)), PARTNER)

    def outward_end(low, matrix, back):
        weights = jnp.concatenate([slot[:, :tok_local] for slot in low])
        return narrow(contract_first(weights, matrix) + back.astype(jnp.float32))

    most = most_products(tokens2, down_matrix, near_down, far_down)
    most, tokens2 = lax.optimization_barrier((most, tokens2))
    low = low_rank(most, tokens2, cross_down)
    cot2, far_up, low = lax.optimization_barrier((cot2, far_up, low))
    cross_up = lax.ppermute(far_up, "groups", SWAP)
    cot2 = jnp.concatenate([cotangent, cot2], axis=0)
    (own, first, second, third), up_send = partial_sums(for_line(low), cot2)
    up_third = move(up_send[2], xor_line(1))
    most = most_products(cot2, up_matrix, near_up, far_up)
    most, up_next = lax.optimization_barrier((most, up_send[0]))
    up_first = move(up_next, xor_line(1))

    cross_up = after(cross_up, up_third)
    up_all = jnp.concatenate([up_matrix, near_up, far_up, cross_up], axis=0)
    low_back = low_rank(most, cot2, cross_up)
    (own_b, first_b, second_b, third_b), down_send = partial_sums(for_line(low_back), tokens2)
    down_third = move(down_send[2], xor_line(1))
    branch_back = outward_start(low, up_all)
    input_back = outward_start(low_back, down_all)
    up_far = move(narrow(add_up(second, up_third)), xor_line(2))
    down_sum = narrow(add_up(second_b, down_third))
    down_far = move(down_sum, xor_line(2))
    down_first = move(after(down_send[0], (up_first, down_sum)), xor_line(1))
    branch_out = outward_end(low, up_all, branch_back)
    up_grad = add_up(own, up_first, up_far)
    input_grad = outward_end(low_back, down_all, input_back)
    down_grad = add_up(own_b, down_first, down_far)
    down_grad = (down_grad / capacity).astype(jnp.bfloat16)[None]
    up_grad = (up_grad / capacity).astype(jnp.bfloat16)[None]
    return (branch_out, input_grad, down_grad, up_grad)


def local(*args):
    fits = lax.axis_size("adapter") == OWNERS and lax.axis_size("groups") == 2
    plan = by_pairs if fits else by_rows
    return plan(*args)


def solution(mesh):
    in_specs = (
        P(("groups", "adapter"), "tensor"),
        P(("groups", "adapter"), "tensor"),
        P("adapter", None, "tensor"),
        P("adapter", None, "tensor"),
        P("groups", None),
        P(("groups", "adapter"), None),
    )
    out_specs = (
        P(("groups", "adapter"), "tensor"),
        P(("groups", "adapter"), "tensor"),
        P(("groups", "adapter"), None, "tensor"),
        P(("groups", "adapter"), None, "tensor"),
    )
    return jax.shard_map(local, mesh=mesh, in_specs=in_specs, out_specs=out_specs, check_vma=False)
```

```python
import jax
import jax.numpy as jnp
from jax import lax
from jax.sharding import PartitionSpec as P

adapter_scale_factor = 2.0


def contract_last(left_op, right_op):
    return lax.dot_general(
        left_op, right_op, (((1,), (1,)), ((), ())), preferred_element_type=jnp.float32
    )


def contract_first(left_op, right_op):
    return lax.dot_general(
        left_op, right_op, (((0,), (0,)), ((), ())), preferred_element_type=jnp.float32
    )


def gather_rows(source_rows, local_index, live_slot):
    taken_rows = jnp.take(source_rows, local_index.reshape(-1), axis=0)
    taken_rows = taken_rows.reshape(local_index.shape + (source_rows.shape[1],))
    return jnp.where(live_slot[:, :, None], taken_rows, jnp.zeros_like(taken_rows))


def combine(onehot, returned):
    flat_rows = returned.reshape(-1, returned.shape[-1])
    return jnp.dot(onehot, flat_rows, preferred_element_type=jnp.float32).astype(jnp.bfloat16)


def by_rows(tokens, cotangent, down_adapter, up_adapter, token_lists, gating):
    owners = lax.axis_size("adapter")
    my_index = lax.axis_index("adapter")
    tok_local = tokens.shape[0]
    half_width = tokens.shape[1]
    capacity = gating.shape[1]
    slot_count = 3 * capacity // (2 * owners)
    slot_ids = jnp.arange(slot_count, dtype=jnp.int32)
    source = token_lists // tok_local
    sent_count = jnp.sum((source == my_index).astype(jnp.int32), axis=1)
    sent_start = jnp.sum((source < my_index).astype(jnp.int32), axis=1)
    live_send = slot_ids[None, :] < sent_count[:, None]
    position = jnp.minimum(sent_start[:, None] + slot_ids[None, :], capacity - 1)
    local_index = jnp.take_along_axis(token_lists, position, axis=1) - my_index * tok_local
    local_index = jnp.where(live_send, local_index, 0)
    outgoing_rows = gather_rows(tokens, local_index, live_send)
    cot_send = gather_rows(cotangent, local_index, live_send)
    token_ids = jnp.arange(tok_local, dtype=jnp.int32)
    onehot = ((token_ids[:, None] == local_index.reshape(1, -1)) & live_send.reshape(1, -1)).astype(
        jnp.bfloat16
    )
    own_list = lax.dynamic_slice_in_dim(token_lists, my_index, 1, 0)[0]
    own_source = own_list // tok_local
    peer_ids = jnp.arange(owners, dtype=jnp.int32)
    recv_count = jnp.sum((own_source[None, :] == peer_ids[:, None]).astype(jnp.int32), axis=1)
    received_offset = jnp.sum((own_source[None, :] < peer_ids[:, None]).astype(jnp.int32), axis=1)
    active_received = slot_ids[None, :] < recv_count[:, None]
    gate_pos = jnp.minimum(received_offset[:, None] + slot_ids[None, :], capacity - 1)
    gate_slot_values = jnp.take(gating[0], gate_pos.reshape(-1)).reshape(gate_pos.shape)
    scale_factors = (
        adapter_scale_factor * jnp.where(active_received, gate_slot_values, 0.0)
    ).reshape(-1, 1)
    down_matrix = down_adapter[0]
    up_matrix = up_adapter[0]
    flat_shape = (owners * slot_count, half_width)
    block_shape = (owners, slot_count, half_width)
    row_recv = lax.all_to_all(outgoing_rows, "adapter", split_axis=0, concat_axis=0, tiled=True)
    rows_in = row_recv.reshape(flat_shape)
    low_rank = lax.psum(contract_last(rows_in, down_matrix), "tensor").astype(jnp.bfloat16)
    out_rows = (
        scale_factors * jnp.dot(low_rank, up_matrix, preferred_element_type=jnp.float32)
    ).astype(jnp.bfloat16)
    out_back = lax.all_to_all(
        out_rows.reshape(block_shape), "adapter", split_axis=0, concat_axis=0, tiled=True
    )
    cot_recv = lax.all_to_all(cot_send, "adapter", split_axis=0, concat_axis=0, tiled=True)
    weighted = (scale_factors * cot_recv.reshape(flat_shape)).astype(jnp.bfloat16)
    low_grad = lax.psum(contract_last(weighted, up_matrix), "tensor").astype(jnp.bfloat16)
    back_rows = jnp.dot(low_grad, down_matrix, preferred_element_type=jnp.float32).astype(
        jnp.bfloat16
    )
    grad_back = lax.all_to_all(
        back_rows.reshape(block_shape), "adapter", split_axis=0, concat_axis=0, tiled=True
    )
    branch_out = combine(onehot, out_back)
    input_grad = combine(onehot, grad_back)
    down_grad = (contract_first(low_grad, rows_in) / capacity).astype(jnp.bfloat16)[None]
    up_grad = (contract_first(low_rank, weighted) / capacity).astype(jnp.bfloat16)[None]
    return (branch_out, input_grad, down_grad, up_grad)


PLACES = 4


def on_line(pairs):
    return [(2 * a + side, 2 * b + side) for a, b in pairs for side in (0, 1)]


def xor_line(bit):
    return on_line([(a, a ^ bit) for a in range(PLACES)])


PARTNER = [(2 * a + side, 2 * a + 1 - side) for a in range(PLACES) for side in (0, 1)]
SWAP = [(0, 1), (1, 0)]
OWNERS = 2 * PLACES
AROUND = on_line([(0, 1), (1, 3), (3, 2), (2, 0)])
DOWNWARD = on_line([(0, 3), (1, 0), (2, 1), (3, 2)])
FIRST_TURN = AROUND + [(OWNERS + a, OWNERS + b) for a, b in DOWNWARD]
SECOND_TURN = [(b, a) for a, b in FIRST_TURN]


def move(value, pairs):
    return lax.ppermute(value, "adapter", pairs)


def turn(value, pairs):
    return lax.ppermute(value, ("groups", "adapter"), pairs)


def after(value, earlier):
    return lax.optimization_barrier((value, earlier))[0]


def narrow(value):
    return value.astype(jnp.bfloat16)


def add_up(*values):
    total = values[0]
    for value in values[1:]:
        total = total + value.astype(jnp.float32)
    return total


def partial_sums(weights, rows):
    parts, sent = [], []
    for weight in weights[::-1]:
        part = jnp.dot(weight, rows, preferred_element_type=jnp.float32)
        part, send, rows = lax.optimization_barrier((part, narrow(part), rows))
        parts.append(part)
        sent.append(send)
    return parts[::-1], sent[::-1]


def both_cores(partial):
    return partial + lax.ppermute(partial, "tensor", SWAP)


def by_pairs(tokens, cotangent, down_adapter, up_adapter, token_lists, gating):
    me = lax.axis_index("adapter")
    first_group = lax.axis_index("groups") == 0
    tok_local = tokens.shape[0]
    capacity = gating.shape[1]
    down_matrix = down_adapter[0]
    up_matrix = up_adapter[0]
    rank = down_matrix.shape[0]

    near_gate, down_later = lax.optimization_barrier((move(gating, xor_line(1)), down_matrix))
    turn_down = turn(down_matrix, FIRST_TURN)
    tokens2 = move(tokens, PARTNER)
    cot2 = move(cotangent, PARTNER)
    back_down = turn(down_later, SECOND_TURN)

    place = me // 2
    near_first = jnp.where(first_group, (place == 1) | (place == 2), place % 2 == 0)
    far_bit = jnp.where(first_group, 2, 3)
    first_bit = jnp.where(near_first, 1, far_bit)
    bits = jnp.stack([jnp.zeros_like(me), first_bit, first_bit ^ far_bit ^ 1, far_bit ^ 1])
    gates = jnp.concatenate([gating, near_gate])
    gates = jnp.concatenate([gates, move(gates, xor_line(2))])
    gate_rows = adapter_scale_factor * jnp.take(gates, bits, axis=0)
    lists = jnp.take(token_lists, me ^ (2 * bits), axis=0)
    token_ids = jnp.arange(tok_local, dtype=jnp.int32)
    ids = jnp.concatenate([me * tok_local + token_ids, (me ^ 1) * tok_local + token_ids])
    taken = lists[:, :, None] == ids[None, None, :]
    scale = jnp.sum(jnp.where(taken, gate_rows[:, :, None], 0.0), axis=1)

    up_later, scale = lax.optimization_barrier((up_matrix, scale))
    turn_up = turn(up_later, FIRST_TURN)
    back_up = turn(up_later, SECOND_TURN)
    far_down, scale = lax.optimization_barrier((jnp.where(near_first, back_down, turn_down), scale))
    cross_down = lax.ppermute(far_down, "groups", SWAP)
    tokens2 = jnp.concatenate([tokens, tokens2], axis=0)
    down_all = jnp.concatenate([down_matrix, turn_down, back_down, cross_down], axis=0)

    def most_products(rows, *matrices):
        return both_cores(contract_last(jnp.concatenate(matrices), rows))

    def low_rank(most, rows, matrix):
        products = [most[k * rank : (k + 1) * rank] for k in range(3)]
        products.append(both_cores(contract_last(matrix, rows)))
        return [narrow(scale[k] * product) for k, product in enumerate(products)]

    def for_line(low):
        near = jnp.where(near_first, low[1], low[2])
        far = jnp.where(near_first, low[2], low[1])
        second = jnp.where(first_group, far, low[3])
        third = jnp.where(first_group, low[3], far)
        return low[0], near, second, third

    def theirs(low, matrix):
        weights = jnp.concatenate([slot[:, tok_local:] for slot in low])
        return narrow(contract_first(weights, matrix))

    def outward_end(low, matrix, back):
        weights = jnp.concatenate([slot[:, :tok_local] for slot in low])
        return narrow(contract_first(weights, matrix) + back.astype(jnp.float32))

    most = most_products(tokens2, down_matrix, turn_down, back_down)
    most, tokens2 = lax.optimization_barrier((most, tokens2))
    low = low_rank(most, tokens2, cross_down)
    cot2, turn_up, back_up, low = lax.optimization_barrier((cot2, turn_up, back_up, low))
    cross_up = lax.ppermute(jnp.where(near_first, back_up, turn_up), "groups", SWAP)
    cot2 = jnp.concatenate([cotangent, cot2], axis=0)
    (own, first, second, third), up_send = partial_sums(for_line(low), cot2)
    up_third = move(up_send[3], xor_line(1))
    most = most_products(cot2, up_matrix, turn_up, back_up)
    most, up_next = lax.optimization_barrier((most, up_send[1]))
    up_first = move(up_next, xor_line(1))

    cross_up = after(cross_up, up_third)
    up_all = jnp.concatenate([up_matrix, turn_up, back_up, cross_up], axis=0)
    low_back = low_rank(most, cot2, cross_up)
    (own_b, first_b, second_b, third_b), down_send = partial_sums(for_line(low_back), tokens2)
    down_third = move(down_send[3], xor_line(1))
    branch_back = move(theirs(low, up_all), PARTNER)
    input_theirs, up_sum = lax.optimization_barrier(
        (theirs(low_back, down_all), narrow(add_up(second, up_third)))
    )
    input_back = move(input_theirs, PARTNER)
    up_far = move(up_sum, xor_line(2))
    down_sum = narrow(add_up(second_b, down_third))
    down_far = move(down_sum, xor_line(2))
    down_first = move(after(down_send[1], (up_first, down_sum)), xor_line(1))
    branch_out = outward_end(low, up_all, branch_back)
    up_grad = add_up(own, up_first, up_far)
    input_grad = outward_end(low_back, down_all, input_back)
    down_grad = add_up(own_b, down_first, down_far)
    down_grad = (down_grad / capacity).astype(jnp.bfloat16)[None]
    up_grad = (up_grad / capacity).astype(jnp.bfloat16)[None]
    return (branch_out, input_grad, down_grad, up_grad)


def local(*args):
    fits = lax.axis_size("adapter") == OWNERS and lax.axis_size("groups") == 2
    plan = by_pairs if fits else by_rows
    return plan(*args)


def solution(mesh):
    in_specs = (
        P(("groups", "adapter"), "tensor"),
        P(("groups", "adapter"), "tensor"),
        P("adapter", None, "tensor"),
        P("adapter", None, "tensor"),
        P("groups", None),
        P(("groups", "adapter"), None),
    )
    out_specs = (
        P(("groups", "adapter"), "tensor"),
        P(("groups", "adapter"), "tensor"),
        P(("groups", "adapter"), None, "tensor"),
        P(("groups", "adapter"), None, "tensor"),
    )
    return jax.shard_map(local, mesh=mesh, in_specs=in_specs, out_specs=out_specs, check_vma=False)
```

```python
import jax
import jax.numpy as jnp
from jax import lax
from jax.sharding import PartitionSpec as P

adapter_scale_factor = 2.0


def contract_last(left_op, right_op):
    return lax.dot_general(
        left_op, right_op, (((1,), (1,)), ((), ())), preferred_element_type=jnp.float32
    )


def contract_first(left_op, right_op):
    return lax.dot_general(
        left_op, right_op, (((0,), (0,)), ((), ())), preferred_element_type=jnp.float32
    )


def gather_rows(source_rows, local_index, live_slot):
    taken_rows = jnp.take(source_rows, local_index.reshape(-1), axis=0)
    taken_rows = taken_rows.reshape(local_index.shape + (source_rows.shape[1],))
    return jnp.where(live_slot[:, :, None], taken_rows, jnp.zeros_like(taken_rows))


def combine(onehot, returned):
    flat_rows = returned.reshape(-1, returned.shape[-1])
    return jnp.dot(onehot, flat_rows, preferred_element_type=jnp.float32).astype(jnp.bfloat16)


def by_rows(tokens, cotangent, down_adapter, up_adapter, token_lists, gating):
    owners = lax.axis_size("adapter")
    my_index = lax.axis_index("adapter")
    tok_local = tokens.shape[0]
    half_width = tokens.shape[1]
    capacity = gating.shape[1]
    slot_count = 3 * capacity // (2 * owners)
    slot_ids = jnp.arange(slot_count, dtype=jnp.int32)
    source = token_lists // tok_local
    sent_count = jnp.sum((source == my_index).astype(jnp.int32), axis=1)
    sent_start = jnp.sum((source < my_index).astype(jnp.int32), axis=1)
    live_send = slot_ids[None, :] < sent_count[:, None]
    position = jnp.minimum(sent_start[:, None] + slot_ids[None, :], capacity - 1)
    local_index = jnp.take_along_axis(token_lists, position, axis=1) - my_index * tok_local
    local_index = jnp.where(live_send, local_index, 0)
    outgoing_rows = gather_rows(tokens, local_index, live_send)
    cot_send = gather_rows(cotangent, local_index, live_send)
    token_ids = jnp.arange(tok_local, dtype=jnp.int32)
    onehot = ((token_ids[:, None] == local_index.reshape(1, -1)) & live_send.reshape(1, -1)).astype(
        jnp.bfloat16
    )
    own_list = lax.dynamic_slice_in_dim(token_lists, my_index, 1, 0)[0]
    own_source = own_list // tok_local
    peer_ids = jnp.arange(owners, dtype=jnp.int32)
    recv_count = jnp.sum((own_source[None, :] == peer_ids[:, None]).astype(jnp.int32), axis=1)
    received_offset = jnp.sum((own_source[None, :] < peer_ids[:, None]).astype(jnp.int32), axis=1)
    active_received = slot_ids[None, :] < recv_count[:, None]
    gate_pos = jnp.minimum(received_offset[:, None] + slot_ids[None, :], capacity - 1)
    gate_slot_values = jnp.take(gating[0], gate_pos.reshape(-1)).reshape(gate_pos.shape)
    scale_factors = (
        adapter_scale_factor * jnp.where(active_received, gate_slot_values, 0.0)
    ).reshape(-1, 1)
    down_matrix = down_adapter[0]
    up_matrix = up_adapter[0]
    flat_shape = (owners * slot_count, half_width)
    block_shape = (owners, slot_count, half_width)
    row_recv = lax.all_to_all(outgoing_rows, "adapter", split_axis=0, concat_axis=0, tiled=True)
    rows_in = row_recv.reshape(flat_shape)
    low_rank = lax.psum(contract_last(rows_in, down_matrix), "tensor").astype(jnp.bfloat16)
    out_rows = (
        scale_factors * jnp.dot(low_rank, up_matrix, preferred_element_type=jnp.float32)
    ).astype(jnp.bfloat16)
    out_back = lax.all_to_all(
        out_rows.reshape(block_shape), "adapter", split_axis=0, concat_axis=0, tiled=True
    )
    cot_recv = lax.all_to_all(cot_send, "adapter", split_axis=0, concat_axis=0, tiled=True)
    weighted = (scale_factors * cot_recv.reshape(flat_shape)).astype(jnp.bfloat16)
    low_grad = lax.psum(contract_last(weighted, up_matrix), "tensor").astype(jnp.bfloat16)
    back_rows = jnp.dot(low_grad, down_matrix, preferred_element_type=jnp.float32).astype(
        jnp.bfloat16
    )
    grad_back = lax.all_to_all(
        back_rows.reshape(block_shape), "adapter", split_axis=0, concat_axis=0, tiled=True
    )
    branch_out = combine(onehot, out_back)
    input_grad = combine(onehot, grad_back)
    down_grad = (contract_first(low_grad, rows_in) / capacity).astype(jnp.bfloat16)[None]
    up_grad = (contract_first(low_rank, weighted) / capacity).astype(jnp.bfloat16)[None]
    return (branch_out, input_grad, down_grad, up_grad)


PLACES = 4


def on_line(pairs):
    return [(2 * a + side, 2 * b + side) for a, b in pairs for side in (0, 1)]


def xor_line(bit):
    return on_line([(a, a ^ bit) for a in range(PLACES)])


PARTNER = [(2 * a + side, 2 * a + 1 - side) for a in range(PLACES) for side in (0, 1)]
SWAP = [(0, 1), (1, 0)]
OWNERS = 2 * PLACES
AROUND = on_line([(0, 1), (1, 3), (3, 2), (2, 0)])
DOWNWARD = on_line([(0, 3), (1, 0), (2, 1), (3, 2)])
FIRST_TURN = AROUND + [(OWNERS + a, OWNERS + b) for a, b in DOWNWARD]
SECOND_TURN = [(b, a) for a, b in FIRST_TURN]


def move(value, pairs):
    return lax.ppermute(value, "adapter", pairs)


def turn(value, pairs):
    return lax.ppermute(value, ("groups", "adapter"), pairs)


def after(value, earlier):
    return lax.optimization_barrier((value, earlier))[0]


def narrow(value):
    return value.astype(jnp.bfloat16)


def add_up(*values):
    total = values[0]
    for value in values[1:]:
        total = total + value.astype(jnp.float32)
    return total


def partial_sums(weights, rows):
    parts, sent = [], []
    for weight in weights[::-1]:
        part = jnp.dot(weight, rows, preferred_element_type=jnp.float32)
        part, send, rows = lax.optimization_barrier((part, narrow(part), rows))
        parts.append(part)
        sent.append(send)
    return parts[::-1], sent[::-1]


def both_cores(partial):
    return partial + lax.ppermute(partial, "tensor", SWAP)


def by_pairs(tokens, cotangent, down_adapter, up_adapter, token_lists, gating):
    me = lax.axis_index("adapter")
    first_group = lax.axis_index("groups") == 0
    tok_local = tokens.shape[0]
    capacity = gating.shape[1]
    down_matrix = down_adapter[0]
    up_matrix = up_adapter[0]
    rank = down_matrix.shape[0]

    near_gate, down_later, cot_later = lax.optimization_barrier(
        (move(gating, xor_line(1)), down_matrix, cotangent)
    )
    turn_down = turn(down_matrix, FIRST_TURN)
    tokens2 = move(tokens, PARTNER)
    cot2 = move(cot_later, PARTNER)
    back_down = turn(down_later, SECOND_TURN)

    place = me // 2
    near_first = jnp.where(first_group, (place == 1) | (place == 2), place % 2 == 0)
    far_bit = jnp.where(first_group, 2, 3)
    first_bit = jnp.where(near_first, 1, far_bit)
    bits = jnp.stack([jnp.zeros_like(me), first_bit, first_bit ^ far_bit ^ 1, far_bit ^ 1])
    gates = jnp.concatenate([gating, near_gate])
    gates = jnp.concatenate([gates, move(gates, xor_line(2))])
    gate_rows = adapter_scale_factor * jnp.take(gates, bits, axis=0)
    lists = jnp.take(token_lists, me ^ (2 * bits), axis=0)
    token_ids = jnp.arange(tok_local, dtype=jnp.int32)
    ids = jnp.concatenate([me * tok_local + token_ids, (me ^ 1) * tok_local + token_ids])
    taken = lists[:, :, None] == ids[None, None, :]
    scale = jnp.sum(jnp.where(taken, gate_rows[:, :, None], 0.0), axis=1)

    up_later, scale = lax.optimization_barrier((up_matrix, scale))
    turn_up = turn(up_later, FIRST_TURN)
    back_up = turn(up_later, SECOND_TURN)
    far_down, scale = lax.optimization_barrier((jnp.where(near_first, back_down, turn_down), scale))
    cross_down = lax.ppermute(far_down, "groups", SWAP)
    tokens2 = jnp.concatenate([tokens, tokens2], axis=0)
    down_all = jnp.concatenate([down_matrix, turn_down, back_down, cross_down], axis=0)

    def most_products(rows, *matrices):
        return both_cores(contract_last(jnp.concatenate(matrices), rows))

    def low_rank(most, rows, matrix):
        products = [most[k * rank : (k + 1) * rank] for k in range(3)]
        products.append(both_cores(contract_last(matrix, rows)))
        return [narrow(scale[k] * product) for k, product in enumerate(products)]

    def for_line(low):
        near = jnp.where(near_first, low[1], low[2])
        far = jnp.where(near_first, low[2], low[1])
        second = jnp.where(first_group, far, low[3])
        third = jnp.where(first_group, low[3], far)
        return low[0], near, second, third

    def theirs(low, matrix):
        weights = jnp.concatenate([slot[:, tok_local:] for slot in low])
        return narrow(contract_first(weights, matrix))

    def outward_end(low, matrix, back):
        weights = jnp.concatenate([slot[:, :tok_local] for slot in low])
        return narrow(contract_first(weights, matrix) + back.astype(jnp.float32))

    most = most_products(tokens2, down_matrix, turn_down, back_down)
    most, tokens2 = lax.optimization_barrier((most, tokens2))
    low = low_rank(most, tokens2, cross_down)
    cot2, turn_up, back_up, low = lax.optimization_barrier((cot2, turn_up, back_up, low))
    cross_up = lax.ppermute(jnp.where(near_first, back_up, turn_up), "groups", SWAP)
    cot2 = jnp.concatenate([cotangent, cot2], axis=0)
    (own, first, second, third), up_send = partial_sums(for_line(low), cot2)
    up_third = move(up_send[3], xor_line(1))
    most = most_products(cot2, up_matrix, turn_up, back_up)
    most, up_next = lax.optimization_barrier((most, up_send[1]))
    up_first = move(up_next, xor_line(1))

    cross_up = after(cross_up, up_third)
    up_all = jnp.concatenate([up_matrix, turn_up, back_up, cross_up], axis=0)
    low_back = low_rank(most, cot2, cross_up)
    (own_b, first_b, second_b, third_b), down_send = partial_sums(for_line(low_back), tokens2)
    down_third = move(down_send[3], xor_line(1))
    branch_back = move(theirs(low, up_all), PARTNER)
    input_theirs, up_sum = lax.optimization_barrier(
        (theirs(low_back, down_all), narrow(add_up(second, up_third)))
    )
    input_back = move(input_theirs, PARTNER)
    up_far = move(up_sum, xor_line(2))
    down_sum = narrow(add_up(second_b, down_third))
    down_far = move(down_sum, xor_line(2))
    down_first = move(after(down_send[1], (up_first, down_sum)), xor_line(1))
    branch_out = outward_end(low, up_all, branch_back)
    up_grad = add_up(own, up_first, up_far)
    input_grad = outward_end(low_back, down_all, input_back)
    down_grad = add_up(own_b, down_first, down_far)
    down_grad = (down_grad / capacity).astype(jnp.bfloat16)[None]
    up_grad = (up_grad / capacity).astype(jnp.bfloat16)[None]
    return (branch_out, input_grad, down_grad, up_grad)


def local(*args):
    fits = lax.axis_size("adapter") == OWNERS and lax.axis_size("groups") == 2
    plan = by_pairs if fits else by_rows
    return plan(*args)


def solution(mesh):
    in_specs = (
        P(("groups", "adapter"), "tensor"),
        P(("groups", "adapter"), "tensor"),
        P("adapter", None, "tensor"),
        P("adapter", None, "tensor"),
        P("groups", None),
        P(("groups", "adapter"), None),
    )
    out_specs = (
        P(("groups", "adapter"), "tensor"),
        P(("groups", "adapter"), "tensor"),
        P(("groups", "adapter"), None, "tensor"),
        P(("groups", "adapter"), None, "tensor"),
    )
    return jax.shard_map(local, mesh=mesh, in_specs=in_specs, out_specs=out_specs, check_vma=False)
```

```python
import jax
import jax.numpy as jnp
from jax import lax
from jax.sharding import PartitionSpec as P

adapter_scale_factor = 2.0


def contract_last(left_op, right_op):
    return lax.dot_general(
        left_op, right_op, (((1,), (1,)), ((), ())), preferred_element_type=jnp.float32
    )


def contract_first(left_op, right_op):
    return lax.dot_general(
        left_op, right_op, (((0,), (0,)), ((), ())), preferred_element_type=jnp.float32
    )


def gather_rows(source_rows, local_index, live_slot):
    taken_rows = jnp.take(source_rows, local_index.reshape(-1), axis=0)
    taken_rows = taken_rows.reshape(local_index.shape + (source_rows.shape[1],))
    return jnp.where(live_slot[:, :, None], taken_rows, jnp.zeros_like(taken_rows))


def combine(onehot, returned):
    flat_rows = returned.reshape(-1, returned.shape[-1])
    return jnp.dot(onehot, flat_rows, preferred_element_type=jnp.float32).astype(jnp.bfloat16)


def by_rows(tokens, cotangent, down_adapter, up_adapter, token_lists, gating):
    owners = lax.axis_size("adapter")
    my_index = lax.axis_index("adapter")
    tok_local = tokens.shape[0]
    half_width = tokens.shape[1]
    capacity = gating.shape[1]
    slot_count = 3 * capacity // (2 * owners)
    slot_ids = jnp.arange(slot_count, dtype=jnp.int32)
    source = token_lists // tok_local
    sent_count = jnp.sum((source == my_index).astype(jnp.int32), axis=1)
    sent_start = jnp.sum((source < my_index).astype(jnp.int32), axis=1)
    live_send = slot_ids[None, :] < sent_count[:, None]
    position = jnp.minimum(sent_start[:, None] + slot_ids[None, :], capacity - 1)
    local_index = jnp.take_along_axis(token_lists, position, axis=1) - my_index * tok_local
    local_index = jnp.where(live_send, local_index, 0)
    outgoing_rows = gather_rows(tokens, local_index, live_send)
    cot_send = gather_rows(cotangent, local_index, live_send)
    token_ids = jnp.arange(tok_local, dtype=jnp.int32)
    onehot = ((token_ids[:, None] == local_index.reshape(1, -1)) & live_send.reshape(1, -1)).astype(
        jnp.bfloat16
    )
    own_list = lax.dynamic_slice_in_dim(token_lists, my_index, 1, 0)[0]
    own_source = own_list // tok_local
    peer_ids = jnp.arange(owners, dtype=jnp.int32)
    recv_count = jnp.sum((own_source[None, :] == peer_ids[:, None]).astype(jnp.int32), axis=1)
    received_offset = jnp.sum((own_source[None, :] < peer_ids[:, None]).astype(jnp.int32), axis=1)
    active_received = slot_ids[None, :] < recv_count[:, None]
    gate_pos = jnp.minimum(received_offset[:, None] + slot_ids[None, :], capacity - 1)
    gate_slot_values = jnp.take(gating[0], gate_pos.reshape(-1)).reshape(gate_pos.shape)
    scale_factors = (
        adapter_scale_factor * jnp.where(active_received, gate_slot_values, 0.0)
    ).reshape(-1, 1)
    down_matrix = down_adapter[0]
    up_matrix = up_adapter[0]
    flat_shape = (owners * slot_count, half_width)
    block_shape = (owners, slot_count, half_width)
    row_recv = lax.all_to_all(outgoing_rows, "adapter", split_axis=0, concat_axis=0, tiled=True)
    rows_in = row_recv.reshape(flat_shape)
    low_rank = lax.psum(contract_last(rows_in, down_matrix), "tensor").astype(jnp.bfloat16)
    out_rows = (
        scale_factors * jnp.dot(low_rank, up_matrix, preferred_element_type=jnp.float32)
    ).astype(jnp.bfloat16)
    out_back = lax.all_to_all(
        out_rows.reshape(block_shape), "adapter", split_axis=0, concat_axis=0, tiled=True
    )
    cot_recv = lax.all_to_all(cot_send, "adapter", split_axis=0, concat_axis=0, tiled=True)
    weighted = (scale_factors * cot_recv.reshape(flat_shape)).astype(jnp.bfloat16)
    low_grad = lax.psum(contract_last(weighted, up_matrix), "tensor").astype(jnp.bfloat16)
    back_rows = jnp.dot(low_grad, down_matrix, preferred_element_type=jnp.float32).astype(
        jnp.bfloat16
    )
    grad_back = lax.all_to_all(
        back_rows.reshape(block_shape), "adapter", split_axis=0, concat_axis=0, tiled=True
    )
    branch_out = combine(onehot, out_back)
    input_grad = combine(onehot, grad_back)
    down_grad = (contract_first(low_grad, rows_in) / capacity).astype(jnp.bfloat16)[None]
    up_grad = (contract_first(low_rank, weighted) / capacity).astype(jnp.bfloat16)[None]
    return (branch_out, input_grad, down_grad, up_grad)


PLACES = 4


def on_line(pairs):
    return [(2 * a + side, 2 * b + side) for a, b in pairs for side in (0, 1)]


def xor_line(bit):
    return on_line([(a, a ^ bit) for a in range(PLACES)])


PARTNER = [(2 * a + side, 2 * a + 1 - side) for a in range(PLACES) for side in (0, 1)]
SWAP = [(0, 1), (1, 0)]
OWNERS = 2 * PLACES
FAR = xor_line(2) + [(OWNERS + a, OWNERS + b) for a, b in xor_line(3)]


def move(value, pairs):
    return lax.ppermute(value, "adapter", pairs)


def after(value, earlier):
    return lax.optimization_barrier((value, earlier))[0]


def narrow(value):
    return value.astype(jnp.bfloat16)


def add_up(*values):
    total = values[0]
    for value in values[1:]:
        total = total + value.astype(jnp.float32)
    return total


def partial_sums(weights, rows):
    parts = [jnp.dot(weight, rows, preferred_element_type=jnp.float32) for weight in weights]
    return lax.optimization_barrier((parts, [narrow(part) for part in parts[1:]]))


def both_cores(partial):
    return partial + lax.ppermute(partial, "tensor", SWAP)


def by_pairs(tokens, cotangent, down_adapter, up_adapter, token_lists, gating):
    me = lax.axis_index("adapter")
    first_group = lax.axis_index("groups") == 0
    tok_local = tokens.shape[0]
    capacity = gating.shape[1]
    down_matrix = down_adapter[0]
    up_matrix = up_adapter[0]
    rank = down_matrix.shape[0]

    far_down = lax.ppermute(down_matrix, ("groups", "adapter"), FAR)
    tokens2 = move(tokens, PARTNER)
    near_gate, down_later, up_later = lax.optimization_barrier(
        (move(gating, xor_line(1)), down_matrix, up_matrix)
    )
    near_down, up_last = lax.optimization_barrier((move(down_later, xor_line(1)), up_matrix))
    near_up = move(up_last, xor_line(1))
    cot2 = move(cotangent, PARTNER)
    gates = jnp.concatenate([gating, near_gate])
    gates = jnp.concatenate([gates, move(gates, xor_line(2))])

    far_bit = jnp.where(first_group, 2, 3)
    experts = jnp.stack([me, me ^ 2, me ^ (2 * far_bit), me ^ (2 * (far_bit ^ 1))])
    lists = jnp.take(token_lists, experts, axis=0)
    crossed = jnp.concatenate([gates[:2], gates[3:], gates[2:3]])
    gate_rows = adapter_scale_factor * jnp.where(first_group, gates, crossed)
    token_ids = jnp.arange(tok_local, dtype=jnp.int32)
    ids = jnp.concatenate([me * tok_local + token_ids, (me ^ 1) * tok_local + token_ids])
    taken = lists[:, :, None] == ids[None, None, :]
    scale = jnp.sum(jnp.where(taken, gate_rows[:, :, None], 0.0), axis=1)

    far_up = lax.ppermute(up_later, ("groups", "adapter"), FAR)
    ready, scale = lax.optimization_barrier((far_down, scale))
    cross_down = lax.ppermute(ready, "groups", SWAP)
    tokens2 = jnp.concatenate([tokens, tokens2], axis=0)
    down_all = jnp.concatenate([down_matrix, near_down, far_down, cross_down], axis=0)

    def most_products(rows, *matrices):
        return both_cores(contract_last(jnp.concatenate(matrices), rows))

    def low_rank(most, rows, matrix):
        products = [most[k * rank : (k + 1) * rank] for k in range(3)]
        products.append(both_cores(contract_last(matrix, rows)))
        return [narrow(scale[k] * product) for k, product in enumerate(products)]

    def for_line(low):
        second = jnp.where(first_group, low[2], low[3])
        third = jnp.where(first_group, low[3], low[2])
        return low[0], low[1], second, third

    def outward_start(low, matrix):
        weights = jnp.concatenate([slot[:, tok_local:] for slot in low])
        return move(narrow(contract_first(weights, matrix)), PARTNER)

    def outward_end(low, matrix, back):
        weights = jnp.concatenate([slot[:, :tok_local] for slot in low])
        return narrow(contract_first(weights, matrix) + back.astype(jnp.float32))

    most = most_products(tokens2, down_matrix, near_down, far_down)
    most, tokens2 = lax.optimization_barrier((most, tokens2))
    low = low_rank(most, tokens2, cross_down)
    cot2, low = lax.optimization_barrier((cot2, low))
    cot2 = jnp.concatenate([cotangent, cot2], axis=0)
    (own, first, second, third), up_send = partial_sums(for_line(low), cot2)
    up_third = move(up_send[2], xor_line(1))
    far_up = after(far_up, up_send)
    cross_up = lax.ppermute(far_up, "groups", SWAP)
    most = most_products(cot2, up_matrix, near_up, far_up)
    most, up_next = lax.optimization_barrier((most, up_send[0]))
    up_first = move(up_next, xor_line(1))

    cross_up = after(cross_up, up_third)
    up_all = jnp.concatenate([up_matrix, near_up, far_up, cross_up], axis=0)
    low_back = low_rank(most, cot2, cross_up)
    (own_b, first_b, second_b, third_b), down_send = partial_sums(for_line(low_back), tokens2)
    down_third = move(down_send[2], xor_line(1))
    branch_back = outward_start(low, up_all)
    input_back = outward_start(low_back, down_all)
    up_far = move(narrow(add_up(second, up_third)), xor_line(2))
    down_sum = narrow(add_up(second_b, down_third))
    down_far = move(down_sum, xor_line(2))
    down_first = move(after(down_send[0], (up_first, down_sum)), xor_line(1))
    branch_out = outward_end(low, up_all, branch_back)
    up_grad = add_up(own, up_first, after(up_far, down_sum))
    input_grad = outward_end(low_back, down_all, input_back)
    input_grad, down_far = lax.optimization_barrier((input_grad, down_far))
    down_grad = add_up(own_b, down_first, down_far)
    down_grad = (down_grad / capacity).astype(jnp.bfloat16)[None]
    up_grad = (up_grad / capacity).astype(jnp.bfloat16)[None]
    return (branch_out, input_grad, down_grad, up_grad)


def local(*args):
    fits = lax.axis_size("adapter") == OWNERS and lax.axis_size("groups") == 2
    plan = by_pairs if fits else by_rows
    return plan(*args)


def solution(mesh):
    in_specs = (
        P(("groups", "adapter"), "tensor"),
        P(("groups", "adapter"), "tensor"),
        P("adapter", None, "tensor"),
        P("adapter", None, "tensor"),
        P("groups", None),
        P(("groups", "adapter"), None),
    )
    out_specs = (
        P(("groups", "adapter"), "tensor"),
        P(("groups", "adapter"), "tensor"),
        P(("groups", "adapter"), None, "tensor"),
        P(("groups", "adapter"), None, "tensor"),
    )
    return jax.shard_map(local, mesh=mesh, in_specs=in_specs, out_specs=out_specs, check_vma=False)
```

```python
import jax
import jax.numpy as jnp
from jax import lax
from jax.sharding import PartitionSpec as P

adapter_scale_factor = 2.0


def contract_last(left_op, right_op):
    return lax.dot_general(
        left_op, right_op, (((1,), (1,)), ((), ())), preferred_element_type=jnp.float32
    )


def contract_first(left_op, right_op):
    return lax.dot_general(
        left_op, right_op, (((0,), (0,)), ((), ())), preferred_element_type=jnp.float32
    )


def gather_rows(source_rows, local_index, live_slot):
    taken_rows = jnp.take(source_rows, local_index.reshape(-1), axis=0)
    taken_rows = taken_rows.reshape(local_index.shape + (source_rows.shape[1],))
    return jnp.where(live_slot[:, :, None], taken_rows, jnp.zeros_like(taken_rows))


def combine(onehot, returned):
    flat_rows = returned.reshape(-1, returned.shape[-1])
    return jnp.dot(onehot, flat_rows, preferred_element_type=jnp.float32).astype(jnp.bfloat16)


def by_rows(tokens, cotangent, down_adapter, up_adapter, token_lists, gating):
    owners = lax.axis_size("adapter")
    my_index = lax.axis_index("adapter")
    tok_local = tokens.shape[0]
    half_width = tokens.shape[1]
    capacity = gating.shape[1]
    slot_count = 3 * capacity // (2 * owners)
    slot_ids = jnp.arange(slot_count, dtype=jnp.int32)
    source = token_lists // tok_local
    sent_count = jnp.sum((source == my_index).astype(jnp.int32), axis=1)
    sent_start = jnp.sum((source < my_index).astype(jnp.int32), axis=1)
    live_send = slot_ids[None, :] < sent_count[:, None]
    position = jnp.minimum(sent_start[:, None] + slot_ids[None, :], capacity - 1)
    local_index = jnp.take_along_axis(token_lists, position, axis=1) - my_index * tok_local
    local_index = jnp.where(live_send, local_index, 0)
    outgoing_rows = gather_rows(tokens, local_index, live_send)
    cot_send = gather_rows(cotangent, local_index, live_send)
    token_ids = jnp.arange(tok_local, dtype=jnp.int32)
    onehot = ((token_ids[:, None] == local_index.reshape(1, -1)) & live_send.reshape(1, -1)).astype(
        jnp.bfloat16
    )
    own_list = lax.dynamic_slice_in_dim(token_lists, my_index, 1, 0)[0]
    own_source = own_list // tok_local
    peer_ids = jnp.arange(owners, dtype=jnp.int32)
    recv_count = jnp.sum((own_source[None, :] == peer_ids[:, None]).astype(jnp.int32), axis=1)
    received_offset = jnp.sum((own_source[None, :] < peer_ids[:, None]).astype(jnp.int32), axis=1)
    active_received = slot_ids[None, :] < recv_count[:, None]
    gate_pos = jnp.minimum(received_offset[:, None] + slot_ids[None, :], capacity - 1)
    gate_slot_values = jnp.take(gating[0], gate_pos.reshape(-1)).reshape(gate_pos.shape)
    scale_factors = (
        adapter_scale_factor * jnp.where(active_received, gate_slot_values, 0.0)
    ).reshape(-1, 1)
    down_matrix = down_adapter[0]
    up_matrix = up_adapter[0]
    flat_shape = (owners * slot_count, half_width)
    block_shape = (owners, slot_count, half_width)
    row_recv = lax.all_to_all(outgoing_rows, "adapter", split_axis=0, concat_axis=0, tiled=True)
    rows_in = row_recv.reshape(flat_shape)
    low_rank = lax.psum(contract_last(rows_in, down_matrix), "tensor").astype(jnp.bfloat16)
    out_rows = (
        scale_factors * jnp.dot(low_rank, up_matrix, preferred_element_type=jnp.float32)
    ).astype(jnp.bfloat16)
    out_back = lax.all_to_all(
        out_rows.reshape(block_shape), "adapter", split_axis=0, concat_axis=0, tiled=True
    )
    cot_recv = lax.all_to_all(cot_send, "adapter", split_axis=0, concat_axis=0, tiled=True)
    weighted = (scale_factors * cot_recv.reshape(flat_shape)).astype(jnp.bfloat16)
    low_grad = lax.psum(contract_last(weighted, up_matrix), "tensor").astype(jnp.bfloat16)
    back_rows = jnp.dot(low_grad, down_matrix, preferred_element_type=jnp.float32).astype(
        jnp.bfloat16
    )
    grad_back = lax.all_to_all(
        back_rows.reshape(block_shape), "adapter", split_axis=0, concat_axis=0, tiled=True
    )
    branch_out = combine(onehot, out_back)
    input_grad = combine(onehot, grad_back)
    down_grad = (contract_first(low_grad, rows_in) / capacity).astype(jnp.bfloat16)[None]
    up_grad = (contract_first(low_rank, weighted) / capacity).astype(jnp.bfloat16)[None]
    return (branch_out, input_grad, down_grad, up_grad)


PLACES = 4


def on_line(pairs):
    return [(2 * a + side, 2 * b + side) for a, b in pairs for side in (0, 1)]


def xor_line(bit):
    return on_line([(a, a ^ bit) for a in range(PLACES)])


PARTNER = [(2 * a + side, 2 * a + 1 - side) for a in range(PLACES) for side in (0, 1)]
SWAP = [(0, 1), (1, 0)]
OWNERS = 2 * PLACES
FAR = xor_line(2) + [(OWNERS + a, OWNERS + b) for a, b in xor_line(3)]


def move(value, pairs):
    return lax.ppermute(value, "adapter", pairs)


def after(value, earlier):
    return lax.optimization_barrier((value, earlier))[0]


def narrow(value):
    return value.astype(jnp.bfloat16)


def add_up(*values):
    total = values[0]
    for value in values[1:]:
        total = total + value.astype(jnp.float32)
    return total


def partial_sums(weights, rows):
    parts = [jnp.dot(weight, rows, preferred_element_type=jnp.float32) for weight in weights]
    return lax.optimization_barrier((parts, [narrow(part) for part in parts[1:]]))


def both_cores(partial):
    return partial + lax.ppermute(partial, "tensor", SWAP)


def by_pairs(tokens, cotangent, down_adapter, up_adapter, token_lists, gating):
    me = lax.axis_index("adapter")
    first_group = lax.axis_index("groups") == 0
    tok_local = tokens.shape[0]
    capacity = gating.shape[1]
    down_matrix = down_adapter[0]
    up_matrix = up_adapter[0]
    rank = down_matrix.shape[0]

    far_down = lax.ppermute(down_matrix, ("groups", "adapter"), FAR)
    tokens2 = move(tokens, PARTNER)
    near_gate, down_later, up_later = lax.optimization_barrier(
        (move(gating, xor_line(1)), down_matrix, up_matrix)
    )
    near_down, up_last = lax.optimization_barrier((move(down_later, xor_line(1)), up_matrix))
    far_up = lax.ppermute(up_last, ("groups", "adapter"), FAR)
    cot2 = move(cotangent, PARTNER)
    gates = jnp.concatenate([gating, near_gate])
    gates = jnp.concatenate([gates, move(gates, xor_line(2))])

    far_bit = jnp.where(first_group, 2, 3)
    experts = jnp.stack([me, me ^ 2, me ^ (2 * far_bit), me ^ (2 * (far_bit ^ 1))])
    lists = jnp.take(token_lists, experts, axis=0)
    crossed = jnp.concatenate([gates[:2], gates[3:], gates[2:3]])
    gate_rows = adapter_scale_factor * jnp.where(first_group, gates, crossed)
    token_ids = jnp.arange(tok_local, dtype=jnp.int32)
    ids = jnp.concatenate([me * tok_local + token_ids, (me ^ 1) * tok_local + token_ids])
    taken = lists[:, :, None] == ids[None, None, :]
    scale = jnp.sum(jnp.where(taken, gate_rows[:, :, None], 0.0), axis=1)

    up_later, scale = lax.optimization_barrier((up_later, scale))
    near_up = move(up_later, xor_line(1))
    ready, scale = lax.optimization_barrier((far_down, scale))
    cross_down = lax.ppermute(ready, "groups", SWAP)
    tokens2 = jnp.concatenate([tokens, tokens2], axis=0)
    down_all = jnp.concatenate([down_matrix, near_down, far_down, cross_down], axis=0)

    def most_products(rows, *matrices):
        return both_cores(contract_last(jnp.concatenate(matrices), rows))

    def low_rank(most, rows, matrix):
        products = [most[k * rank : (k + 1) * rank] for k in range(3)]
        products.append(both_cores(contract_last(matrix, rows)))
        return [narrow(scale[k] * product) for k, product in enumerate(products)]

    def for_line(low):
        second = jnp.where(first_group, low[2], low[3])
        third = jnp.where(first_group, low[3], low[2])
        return low[0], low[1], second, third

    def outward_start(low, matrix):
        weights = jnp.concatenate([slot[:, tok_local:] for slot in low])
        return move(narrow(contract_first(weights, matrix)), PARTNER)

    def outward_end(low, matrix, back):
        weights = jnp.concatenate([slot[:, :tok_local] for slot in low])
        return narrow(contract_first(weights, matrix) + back.astype(jnp.float32))

    most = most_products(tokens2, down_matrix, near_down, far_down)
    most, tokens2 = lax.optimization_barrier((most, tokens2))
    low = low_rank(most, tokens2, cross_down)
    cot2, low = lax.optimization_barrier((cot2, low))
    cot2 = jnp.concatenate([cotangent, cot2], axis=0)
    (own, first, second, third), up_send = partial_sums(for_line(low), cot2)
    up_third = move(up_send[2], xor_line(1))
    far_up = after(far_up, up_send)
    cross_up = lax.ppermute(far_up, "groups", SWAP)
    most = most_products(cot2, up_matrix, near_up, far_up)
    most, up_next = lax.optimization_barrier((most, up_send[0]))
    up_first = move(up_next, xor_line(1))

    cross_up = after(cross_up, up_third)
    up_all = jnp.concatenate([up_matrix, near_up, far_up, cross_up], axis=0)
    low_back = low_rank(most, cot2, cross_up)
    (own_b, first_b, second_b, third_b), down_send = partial_sums(for_line(low_back), tokens2)
    down_third = move(down_send[2], xor_line(1))
    branch_back = outward_start(low, up_all)
    input_back = outward_start(low_back, down_all)
    up_far = move(narrow(add_up(second, up_third)), xor_line(2))
    down_sum = narrow(add_up(second_b, down_third))
    down_far = move(down_sum, xor_line(2))
    down_first = move(after(down_send[0], (up_first, down_sum)), xor_line(1))
    branch_out = outward_end(low, up_all, branch_back)
    up_grad = add_up(own, up_first, after(up_far, down_sum))
    input_grad = outward_end(low_back, down_all, input_back)
    input_grad, down_far = lax.optimization_barrier((input_grad, down_far))
    down_grad = add_up(own_b, down_first, down_far)
    down_grad = (down_grad / capacity).astype(jnp.bfloat16)[None]
    up_grad = (up_grad / capacity).astype(jnp.bfloat16)[None]
    return (branch_out, input_grad, down_grad, up_grad)


def local(*args):
    fits = lax.axis_size("adapter") == OWNERS and lax.axis_size("groups") == 2
    plan = by_pairs if fits else by_rows
    return plan(*args)


def solution(mesh):
    in_specs = (
        P(("groups", "adapter"), "tensor"),
        P(("groups", "adapter"), "tensor"),
        P("adapter", None, "tensor"),
        P("adapter", None, "tensor"),
        P("groups", None),
        P(("groups", "adapter"), None),
    )
    out_specs = (
        P(("groups", "adapter"), "tensor"),
        P(("groups", "adapter"), "tensor"),
        P(("groups", "adapter"), None, "tensor"),
        P(("groups", "adapter"), None, "tensor"),
    )
    return jax.shard_map(local, mesh=mesh, in_specs=in_specs, out_specs=out_specs, check_vma=False)
```

```python
import jax
import jax.numpy as jnp
from jax import lax
from jax.sharding import PartitionSpec as P

adapter_scale_factor = 2.0


def contract_last(left_op, right_op):
    return lax.dot_general(
        left_op, right_op, (((1,), (1,)), ((), ())), preferred_element_type=jnp.float32
    )


def contract_first(left_op, right_op):
    return lax.dot_general(
        left_op, right_op, (((0,), (0,)), ((), ())), preferred_element_type=jnp.float32
    )


def gather_rows(source_rows, local_index, live_slot):
    taken_rows = jnp.take(source_rows, local_index.reshape(-1), axis=0)
    taken_rows = taken_rows.reshape(local_index.shape + (source_rows.shape[1],))
    return jnp.where(live_slot[:, :, None], taken_rows, jnp.zeros_like(taken_rows))


def combine(onehot, returned):
    flat_rows = returned.reshape(-1, returned.shape[-1])
    return jnp.dot(onehot, flat_rows, preferred_element_type=jnp.float32).astype(jnp.bfloat16)


def by_rows(tokens, cotangent, down_adapter, up_adapter, token_lists, gating):
    owners = lax.axis_size("adapter")
    my_index = lax.axis_index("adapter")
    tok_local = tokens.shape[0]
    half_width = tokens.shape[1]
    capacity = gating.shape[1]
    slot_count = 3 * capacity // (2 * owners)
    slot_ids = jnp.arange(slot_count, dtype=jnp.int32)
    source = token_lists // tok_local
    sent_count = jnp.sum((source == my_index).astype(jnp.int32), axis=1)
    sent_start = jnp.sum((source < my_index).astype(jnp.int32), axis=1)
    live_send = slot_ids[None, :] < sent_count[:, None]
    position = jnp.minimum(sent_start[:, None] + slot_ids[None, :], capacity - 1)
    local_index = jnp.take_along_axis(token_lists, position, axis=1) - my_index * tok_local
    local_index = jnp.where(live_send, local_index, 0)
    outgoing_rows = gather_rows(tokens, local_index, live_send)
    cot_send = gather_rows(cotangent, local_index, live_send)
    token_ids = jnp.arange(tok_local, dtype=jnp.int32)
    onehot = ((token_ids[:, None] == local_index.reshape(1, -1)) & live_send.reshape(1, -1)).astype(
        jnp.bfloat16
    )
    own_list = lax.dynamic_slice_in_dim(token_lists, my_index, 1, 0)[0]
    own_source = own_list // tok_local
    peer_ids = jnp.arange(owners, dtype=jnp.int32)
    recv_count = jnp.sum((own_source[None, :] == peer_ids[:, None]).astype(jnp.int32), axis=1)
    received_offset = jnp.sum((own_source[None, :] < peer_ids[:, None]).astype(jnp.int32), axis=1)
    active_received = slot_ids[None, :] < recv_count[:, None]
    gate_pos = jnp.minimum(received_offset[:, None] + slot_ids[None, :], capacity - 1)
    gate_slot_values = jnp.take(gating[0], gate_pos.reshape(-1)).reshape(gate_pos.shape)
    scale_factors = (
        adapter_scale_factor * jnp.where(active_received, gate_slot_values, 0.0)
    ).reshape(-1, 1)
    down_matrix = down_adapter[0]
    up_matrix = up_adapter[0]
    flat_shape = (owners * slot_count, half_width)
    block_shape = (owners, slot_count, half_width)
    row_recv = lax.all_to_all(outgoing_rows, "adapter", split_axis=0, concat_axis=0, tiled=True)
    rows_in = row_recv.reshape(flat_shape)
    low_rank = lax.psum(contract_last(rows_in, down_matrix), "tensor").astype(jnp.bfloat16)
    out_rows = (
        scale_factors * jnp.dot(low_rank, up_matrix, preferred_element_type=jnp.float32)
    ).astype(jnp.bfloat16)
    out_back = lax.all_to_all(
        out_rows.reshape(block_shape), "adapter", split_axis=0, concat_axis=0, tiled=True
    )
    cot_recv = lax.all_to_all(cot_send, "adapter", split_axis=0, concat_axis=0, tiled=True)
    weighted = (scale_factors * cot_recv.reshape(flat_shape)).astype(jnp.bfloat16)
    low_grad = lax.psum(contract_last(weighted, up_matrix), "tensor").astype(jnp.bfloat16)
    back_rows = jnp.dot(low_grad, down_matrix, preferred_element_type=jnp.float32).astype(
        jnp.bfloat16
    )
    grad_back = lax.all_to_all(
        back_rows.reshape(block_shape), "adapter", split_axis=0, concat_axis=0, tiled=True
    )
    branch_out = combine(onehot, out_back)
    input_grad = combine(onehot, grad_back)
    down_grad = (contract_first(low_grad, rows_in) / capacity).astype(jnp.bfloat16)[None]
    up_grad = (contract_first(low_rank, weighted) / capacity).astype(jnp.bfloat16)[None]
    return (branch_out, input_grad, down_grad, up_grad)


PLACES = 4


def on_line(pairs):
    return [(2 * a + side, 2 * b + side) for a, b in pairs for side in (0, 1)]


def xor_line(bit):
    return on_line([(a, a ^ bit) for a in range(PLACES)])


PARTNER = [(2 * a + side, 2 * a + 1 - side) for a in range(PLACES) for side in (0, 1)]
SWAP = [(0, 1), (1, 0)]
OWNERS = 2 * PLACES
FAR = xor_line(2) + [(OWNERS + a, OWNERS + b) for a, b in xor_line(3)]


def move(value, pairs):
    return lax.ppermute(value, "adapter", pairs)


def after(value, earlier):
    return lax.optimization_barrier((value, earlier))[0]


def narrow(value):
    return value.astype(jnp.bfloat16)


def add_up(*values):
    total = values[0]
    for value in values[1:]:
        total = total + value.astype(jnp.float32)
    return total


def partial_sums(weights, rows):
    parts = [jnp.dot(weight, rows, preferred_element_type=jnp.float32) for weight in weights]
    return lax.optimization_barrier((parts, [narrow(part) for part in parts[1:]]))


def both_cores(partial):
    return partial + lax.ppermute(partial, "tensor", SWAP)


def by_pairs(tokens, cotangent, down_adapter, up_adapter, token_lists, gating):
    me = lax.axis_index("adapter")
    first_group = lax.axis_index("groups") == 0
    tok_local = tokens.shape[0]
    capacity = gating.shape[1]
    down_matrix = down_adapter[0]
    up_matrix = up_adapter[0]
    rank = down_matrix.shape[0]

    far_down = lax.ppermute(down_matrix, ("groups", "adapter"), FAR)
    tokens2 = move(tokens, PARTNER)
    near_gate, down_later, up_later = lax.optimization_barrier(
        (move(gating, xor_line(1)), down_matrix, up_matrix)
    )
    near_down = move(down_later, xor_line(1))
    cot2 = move(cotangent, PARTNER)
    gates = jnp.concatenate([gating, near_gate])
    gates = jnp.concatenate([gates, move(gates, xor_line(2))])

    far_bit = jnp.where(first_group, 2, 3)
    experts = jnp.stack([me, me ^ 2, me ^ (2 * far_bit), me ^ (2 * (far_bit ^ 1))])
    lists = jnp.take(token_lists, experts, axis=0)
    crossed = jnp.concatenate([gates[:2], gates[3:], gates[2:3]])
    gate_rows = adapter_scale_factor * jnp.where(first_group, gates, crossed)
    token_ids = jnp.arange(tok_local, dtype=jnp.int32)
    ids = jnp.concatenate([me * tok_local + token_ids, (me ^ 1) * tok_local + token_ids])
    taken = lists[:, :, None] == ids[None, None, :]
    scale = jnp.sum(jnp.where(taken, gate_rows[:, :, None], 0.0), axis=1)

    far_up = lax.ppermute(up_later, ("groups", "adapter"), FAR)
    up_last, scale = lax.optimization_barrier((up_matrix, scale))
    near_up = move(up_last, xor_line(1))
    ready, scale = lax.optimization_barrier((far_down, scale))
    cross_down = lax.ppermute(ready, "groups", SWAP)
    tokens2 = jnp.concatenate([tokens, tokens2], axis=0)
    down_all = jnp.concatenate([down_matrix, near_down, far_down, cross_down], axis=0)

    def most_products(rows, *matrices):
        return both_cores(contract_last(jnp.concatenate(matrices), rows))

    def low_rank(most, rows, matrix):
        products = [most[k * rank : (k + 1) * rank] for k in range(3)]
        products.append(both_cores(contract_last(matrix, rows)))
        return [narrow(scale[k] * product) for k, product in enumerate(products)]

    def for_line(low):
        second = jnp.where(first_group, low[2], low[3])
        third = jnp.where(first_group, low[3], low[2])
        return low[0], low[1], second, third

    def outward_start(low, matrix):
        weights = jnp.concatenate([slot[:, tok_local:] for slot in low])
        return move(narrow(contract_first(weights, matrix)), PARTNER)

    def outward_end(low, matrix, back):
        weights = jnp.concatenate([slot[:, :tok_local] for slot in low])
        return narrow(contract_first(weights, matrix) + back.astype(jnp.float32))

    most = most_products(tokens2, down_matrix, near_down, far_down)
    most, tokens2 = lax.optimization_barrier((most, tokens2))
    low = low_rank(most, tokens2, cross_down)
    cot2, low = lax.optimization_barrier((cot2, low))
    cot2 = jnp.concatenate([cotangent, cot2], axis=0)
    (own, first, second, third), up_send = partial_sums(for_line(low), cot2)
    up_third = move(up_send[2], xor_line(1))
    far_up = after(far_up, up_send)
    cross_up = lax.ppermute(far_up, "groups", SWAP)
    most = most_products(cot2, up_matrix, near_up, far_up)
    most, up_next = lax.optimization_barrier((most, up_send[0]))
    up_first = move(up_next, xor_line(1))

    cross_up = after(cross_up, up_third)
    up_all = jnp.concatenate([up_matrix, near_up, far_up, cross_up], axis=0)
    low_back = low_rank(most, cot2, cross_up)
    (own_b, first_b, second_b, third_b), down_send = partial_sums(for_line(low_back), tokens2)
    down_third = move(down_send[2], xor_line(1))
    branch_back = outward_start(low, up_all)
    input_back = outward_start(low_back, down_all)
    up_far = move(narrow(add_up(second, up_third)), xor_line(2))
    down_sum = narrow(add_up(second_b, down_third))
    down_far = move(down_sum, xor_line(2))
    down_first = move(after(down_send[0], (up_first, down_sum)), xor_line(1))
    branch_out = outward_end(low, up_all, branch_back)
    up_grad = add_up(own, up_first, after(up_far, down_sum))
    input_grad = outward_end(low_back, down_all, input_back)
    input_grad, down_far = lax.optimization_barrier((input_grad, down_far))
    down_grad = add_up(own_b, down_first, down_far)
    down_grad = (down_grad / capacity).astype(jnp.bfloat16)[None]
    up_grad = (up_grad / capacity).astype(jnp.bfloat16)[None]
    return (branch_out, input_grad, down_grad, up_grad)


def local(*args):
    fits = lax.axis_size("adapter") == OWNERS and lax.axis_size("groups") == 2
    plan = by_pairs if fits else by_rows
    return plan(*args)


def solution(mesh):
    in_specs = (
        P(("groups", "adapter"), "tensor"),
        P(("groups", "adapter"), "tensor"),
        P("adapter", None, "tensor"),
        P("adapter", None, "tensor"),
        P("groups", None),
        P(("groups", "adapter"), None),
    )
    out_specs = (
        P(("groups", "adapter"), "tensor"),
        P(("groups", "adapter"), "tensor"),
        P(("groups", "adapter"), None, "tensor"),
        P(("groups", "adapter"), None, "tensor"),
    )
    return jax.shard_map(local, mesh=mesh, in_specs=in_specs, out_specs=out_specs, check_vma=False)
```

```python
import jax
import jax.numpy as jnp
from jax import lax
from jax.sharding import PartitionSpec as P

adapter_scale_factor = 2.0


def contract_last(left_op, right_op):
    return lax.dot_general(
        left_op, right_op, (((1,), (1,)), ((), ())), preferred_element_type=jnp.float32
    )


def contract_first(left_op, right_op):
    return lax.dot_general(
        left_op, right_op, (((0,), (0,)), ((), ())), preferred_element_type=jnp.float32
    )


def gather_rows(source_rows, local_index, live_slot):
    taken_rows = jnp.take(source_rows, local_index.reshape(-1), axis=0)
    taken_rows = taken_rows.reshape(local_index.shape + (source_rows.shape[1],))
    return jnp.where(live_slot[:, :, None], taken_rows, jnp.zeros_like(taken_rows))


def combine(onehot, returned):
    flat_rows = returned.reshape(-1, returned.shape[-1])
    return jnp.dot(onehot, flat_rows, preferred_element_type=jnp.float32).astype(jnp.bfloat16)


def by_rows(tokens, cotangent, down_adapter, up_adapter, token_lists, gating):
    owners = lax.axis_size("adapter")
    my_index = lax.axis_index("adapter")
    tok_local = tokens.shape[0]
    half_width = tokens.shape[1]
    capacity = gating.shape[1]
    slot_count = 3 * capacity // (2 * owners)
    slot_ids = jnp.arange(slot_count, dtype=jnp.int32)
    source = token_lists // tok_local
    sent_count = jnp.sum((source == my_index).astype(jnp.int32), axis=1)
    sent_start = jnp.sum((source < my_index).astype(jnp.int32), axis=1)
    live_send = slot_ids[None, :] < sent_count[:, None]
    position = jnp.minimum(sent_start[:, None] + slot_ids[None, :], capacity - 1)
    local_index = jnp.take_along_axis(token_lists, position, axis=1) - my_index * tok_local
    local_index = jnp.where(live_send, local_index, 0)
    outgoing_rows = gather_rows(tokens, local_index, live_send)
    cot_send = gather_rows(cotangent, local_index, live_send)
    token_ids = jnp.arange(tok_local, dtype=jnp.int32)
    onehot = ((token_ids[:, None] == local_index.reshape(1, -1)) & live_send.reshape(1, -1)).astype(
        jnp.bfloat16
    )
    own_list = lax.dynamic_slice_in_dim(token_lists, my_index, 1, 0)[0]
    own_source = own_list // tok_local
    peer_ids = jnp.arange(owners, dtype=jnp.int32)
    recv_count = jnp.sum((own_source[None, :] == peer_ids[:, None]).astype(jnp.int32), axis=1)
    received_offset = jnp.sum((own_source[None, :] < peer_ids[:, None]).astype(jnp.int32), axis=1)
    active_received = slot_ids[None, :] < recv_count[:, None]
    gate_pos = jnp.minimum(received_offset[:, None] + slot_ids[None, :], capacity - 1)
    gate_slot_values = jnp.take(gating[0], gate_pos.reshape(-1)).reshape(gate_pos.shape)
    scale_factors = (
        adapter_scale_factor * jnp.where(active_received, gate_slot_values, 0.0)
    ).reshape(-1, 1)
    down_matrix = down_adapter[0]
    up_matrix = up_adapter[0]
    flat_shape = (owners * slot_count, half_width)
    block_shape = (owners, slot_count, half_width)
    row_recv = lax.all_to_all(outgoing_rows, "adapter", split_axis=0, concat_axis=0, tiled=True)
    rows_in = row_recv.reshape(flat_shape)
    low_rank = lax.psum(contract_last(rows_in, down_matrix), "tensor").astype(jnp.bfloat16)
    out_rows = (
        scale_factors * jnp.dot(low_rank, up_matrix, preferred_element_type=jnp.float32)
    ).astype(jnp.bfloat16)
    out_back = lax.all_to_all(
        out_rows.reshape(block_shape), "adapter", split_axis=0, concat_axis=0, tiled=True
    )
    cot_recv = lax.all_to_all(cot_send, "adapter", split_axis=0, concat_axis=0, tiled=True)
    weighted = (scale_factors * cot_recv.reshape(flat_shape)).astype(jnp.bfloat16)
    low_grad = lax.psum(contract_last(weighted, up_matrix), "tensor").astype(jnp.bfloat16)
    back_rows = jnp.dot(low_grad, down_matrix, preferred_element_type=jnp.float32).astype(
        jnp.bfloat16
    )
    grad_back = lax.all_to_all(
        back_rows.reshape(block_shape), "adapter", split_axis=0, concat_axis=0, tiled=True
    )
    branch_out = combine(onehot, out_back)
    input_grad = combine(onehot, grad_back)
    down_grad = (contract_first(low_grad, rows_in) / capacity).astype(jnp.bfloat16)[None]
    up_grad = (contract_first(low_rank, weighted) / capacity).astype(jnp.bfloat16)[None]
    return (branch_out, input_grad, down_grad, up_grad)


PLACES = 4


def on_line(pairs):
    return [(2 * a + side, 2 * b + side) for a, b in pairs for side in (0, 1)]


def xor_line(bit):
    return on_line([(a, a ^ bit) for a in range(PLACES)])


PARTNER = [(2 * a + side, 2 * a + 1 - side) for a in range(PLACES) for side in (0, 1)]
SWAP = [(0, 1), (1, 0)]
OWNERS = 2 * PLACES
FAR = xor_line(2) + [(OWNERS + a, OWNERS + b) for a, b in xor_line(3)]


def move(value, pairs):
    return lax.ppermute(value, "adapter", pairs)


def after(value, earlier):
    return lax.optimization_barrier((value, earlier))[0]


def narrow(value):
    return value.astype(jnp.bfloat16)


def add_up(*values):
    total = values[0]
    for value in values[1:]:
        total = total + value.astype(jnp.float32)
    return total


def partial_sums(weights, rows):
    parts = [jnp.dot(weight, rows, preferred_element_type=jnp.float32) for weight in weights]
    return lax.optimization_barrier((parts, [narrow(part) for part in parts[1:]]))


def both_cores(partial):
    return partial + lax.ppermute(partial, "tensor", SWAP)


def by_pairs(tokens, cotangent, down_adapter, up_adapter, token_lists, gating):
    me = lax.axis_index("adapter")
    first_group = lax.axis_index("groups") == 0
    tok_local = tokens.shape[0]
    capacity = gating.shape[1]
    down_matrix = down_adapter[0]
    up_matrix = up_adapter[0]
    rank = down_matrix.shape[0]

    far_down = lax.ppermute(down_matrix, ("groups", "adapter"), FAR)
    tokens2 = move(tokens, PARTNER)
    near_gate, down_later, up_later = lax.optimization_barrier(
        (move(gating, xor_line(1)), down_matrix, up_matrix)
    )
    near_down = move(down_later, xor_line(1))
    cot2 = move(cotangent, PARTNER)
    gates = jnp.concatenate([gating, near_gate])
    gates = jnp.concatenate([gates, move(gates, xor_line(2))])

    far_bit = jnp.where(first_group, 2, 3)
    experts = jnp.stack([me, me ^ 2, me ^ (2 * far_bit), me ^ (2 * (far_bit ^ 1))])
    lists = jnp.take(token_lists, experts, axis=0)
    crossed = jnp.concatenate([gates[:2], gates[3:], gates[2:3]])
    gate_rows = adapter_scale_factor * jnp.where(first_group, gates, crossed)
    token_ids = jnp.arange(tok_local, dtype=jnp.int32)
    ids = jnp.concatenate([me * tok_local + token_ids, (me ^ 1) * tok_local + token_ids])
    taken = lists[:, :, None] == ids[None, None, :]
    scale = jnp.sum(jnp.where(taken, gate_rows[:, :, None], 0.0), axis=1)

    far_up = lax.ppermute(up_later, ("groups", "adapter"), FAR)
    up_last, scale = lax.optimization_barrier((up_matrix, scale))
    near_up = move(up_last, xor_line(1))
    ready, scale = lax.optimization_barrier((far_down, scale))
    cross_down = lax.ppermute(ready, "groups", SWAP)
    tokens2 = jnp.concatenate([tokens, tokens2], axis=0)
    down_all = jnp.concatenate([down_matrix, near_down, far_down, cross_down], axis=0)

    def most_products(rows, *matrices):
        return both_cores(contract_last(jnp.concatenate(matrices), rows))

    def low_rank(most, rows, matrix):
        products = [most[k * rank : (k + 1) * rank] for k in range(3)]
        products.append(both_cores(contract_last(matrix, rows)))
        return [narrow(scale[k] * product) for k, product in enumerate(products)]

    def for_line(low):
        second = jnp.where(first_group, low[2], low[3])
        third = jnp.where(first_group, low[3], low[2])
        return low[0], low[1], second, third

    def outward_start(low, matrix):
        weights = jnp.concatenate([slot[:, tok_local:] for slot in low])
        return move(narrow(contract_first(weights, matrix)), PARTNER)

    def outward_end(low, matrix, back):
        weights = jnp.concatenate([slot[:, :tok_local] for slot in low])
        return narrow(contract_first(weights, matrix) + back.astype(jnp.float32))

    most = most_products(tokens2, down_matrix, near_down, far_down)
    most, tokens2 = lax.optimization_barrier((most, tokens2))
    low = low_rank(most, tokens2, cross_down)
    cot2, low = lax.optimization_barrier((cot2, low))
    cot2 = jnp.concatenate([cotangent, cot2], axis=0)
    *others, for_third = for_line(low)
    up_send_third = narrow(jnp.dot(for_third, cot2, preferred_element_type=jnp.float32))
    up_third = move(up_send_third, xor_line(1))
    far_up = after(far_up, up_send_third)
    cross_up = lax.ppermute(far_up, "groups", SWAP)
    most = most_products(cot2, up_matrix, near_up, far_up)
    most, rows_later = lax.optimization_barrier((most, cot2))
    (own, first, second), up_send = partial_sums(others, rows_later)
    up_first = move(up_send[0], xor_line(1))

    cross_up, up_sum = lax.optimization_barrier((cross_up, narrow(add_up(second, up_third))))
    up_far = move(up_sum, xor_line(2))
    up_all = jnp.concatenate([up_matrix, near_up, far_up, cross_up], axis=0)
    low_back = low_rank(most, cot2, cross_up)
    (own_b, first_b, second_b, third_b), down_send = partial_sums(for_line(low_back), tokens2)
    down_third = move(down_send[2], xor_line(1))
    branch_back = outward_start(low, up_all)
    input_back = outward_start(low_back, down_all)
    down_sum = narrow(add_up(second_b, down_third))
    down_far = move(down_sum, xor_line(2))
    down_first = move(after(down_send[0], (up_first, down_sum)), xor_line(1))
    branch_out = outward_end(low, up_all, branch_back)
    up_grad = add_up(own, up_first, after(up_far, down_sum))
    input_grad = outward_end(low_back, down_all, input_back)
    input_grad, down_far = lax.optimization_barrier((input_grad, down_far))
    down_grad = add_up(own_b, down_first, down_far)
    down_grad = (down_grad / capacity).astype(jnp.bfloat16)[None]
    up_grad = (up_grad / capacity).astype(jnp.bfloat16)[None]
    return (branch_out, input_grad, down_grad, up_grad)


def local(*args):
    fits = lax.axis_size("adapter") == OWNERS and lax.axis_size("groups") == 2
    plan = by_pairs if fits else by_rows
    return plan(*args)


def solution(mesh):
    in_specs = (
        P(("groups", "adapter"), "tensor"),
        P(("groups", "adapter"), "tensor"),
        P("adapter", None, "tensor"),
        P("adapter", None, "tensor"),
        P("groups", None),
        P(("groups", "adapter"), None),
    )
    out_specs = (
        P(("groups", "adapter"), "tensor"),
        P(("groups", "adapter"), "tensor"),
        P(("groups", "adapter"), None, "tensor"),
        P(("groups", "adapter"), None, "tensor"),
    )
    return jax.shard_map(local, mesh=mesh, in_specs=in_specs, out_specs=out_specs, check_vma=False)
```

```python
import jax
import jax.numpy as jnp
from jax import lax
from jax.sharding import PartitionSpec as P

adapter_scale_factor = 2.0


def contract_last(left_op, right_op):
    return lax.dot_general(
        left_op, right_op, (((1,), (1,)), ((), ())), preferred_element_type=jnp.float32
    )


def contract_first(left_op, right_op):
    return lax.dot_general(
        left_op, right_op, (((0,), (0,)), ((), ())), preferred_element_type=jnp.float32
    )


def gather_rows(source_rows, local_index, live_slot):
    taken_rows = jnp.take(source_rows, local_index.reshape(-1), axis=0)
    taken_rows = taken_rows.reshape(local_index.shape + (source_rows.shape[1],))
    return jnp.where(live_slot[:, :, None], taken_rows, jnp.zeros_like(taken_rows))


def combine(onehot, returned):
    flat_rows = returned.reshape(-1, returned.shape[-1])
    return jnp.dot(onehot, flat_rows, preferred_element_type=jnp.float32).astype(jnp.bfloat16)


def by_rows(tokens, cotangent, down_adapter, up_adapter, token_lists, gating):
    owners = lax.axis_size("adapter")
    my_index = lax.axis_index("adapter")
    tok_local = tokens.shape[0]
    half_width = tokens.shape[1]
    capacity = gating.shape[1]
    slot_count = 3 * capacity // (2 * owners)
    slot_ids = jnp.arange(slot_count, dtype=jnp.int32)
    source = token_lists // tok_local
    sent_count = jnp.sum((source == my_index).astype(jnp.int32), axis=1)
    sent_start = jnp.sum((source < my_index).astype(jnp.int32), axis=1)
    live_send = slot_ids[None, :] < sent_count[:, None]
    position = jnp.minimum(sent_start[:, None] + slot_ids[None, :], capacity - 1)
    local_index = jnp.take_along_axis(token_lists, position, axis=1) - my_index * tok_local
    local_index = jnp.where(live_send, local_index, 0)
    outgoing_rows = gather_rows(tokens, local_index, live_send)
    cot_send = gather_rows(cotangent, local_index, live_send)
    token_ids = jnp.arange(tok_local, dtype=jnp.int32)
    onehot = ((token_ids[:, None] == local_index.reshape(1, -1)) & live_send.reshape(1, -1)).astype(
        jnp.bfloat16
    )
    own_list = lax.dynamic_slice_in_dim(token_lists, my_index, 1, 0)[0]
    own_source = own_list // tok_local
    peer_ids = jnp.arange(owners, dtype=jnp.int32)
    recv_count = jnp.sum((own_source[None, :] == peer_ids[:, None]).astype(jnp.int32), axis=1)
    received_offset = jnp.sum((own_source[None, :] < peer_ids[:, None]).astype(jnp.int32), axis=1)
    active_received = slot_ids[None, :] < recv_count[:, None]
    gate_pos = jnp.minimum(received_offset[:, None] + slot_ids[None, :], capacity - 1)
    gate_slot_values = jnp.take(gating[0], gate_pos.reshape(-1)).reshape(gate_pos.shape)
    scale_factors = (
        adapter_scale_factor * jnp.where(active_received, gate_slot_values, 0.0)
    ).reshape(-1, 1)
    down_matrix = down_adapter[0]
    up_matrix = up_adapter[0]
    flat_shape = (owners * slot_count, half_width)
    block_shape = (owners, slot_count, half_width)
    row_recv = lax.all_to_all(outgoing_rows, "adapter", split_axis=0, concat_axis=0, tiled=True)
    rows_in = row_recv.reshape(flat_shape)
    low_rank = lax.psum(contract_last(rows_in, down_matrix), "tensor").astype(jnp.bfloat16)
    out_rows = (
        scale_factors * jnp.dot(low_rank, up_matrix, preferred_element_type=jnp.float32)
    ).astype(jnp.bfloat16)
    out_back = lax.all_to_all(
        out_rows.reshape(block_shape), "adapter", split_axis=0, concat_axis=0, tiled=True
    )
    cot_recv = lax.all_to_all(cot_send, "adapter", split_axis=0, concat_axis=0, tiled=True)
    weighted = (scale_factors * cot_recv.reshape(flat_shape)).astype(jnp.bfloat16)
    low_grad = lax.psum(contract_last(weighted, up_matrix), "tensor").astype(jnp.bfloat16)
    back_rows = jnp.dot(low_grad, down_matrix, preferred_element_type=jnp.float32).astype(
        jnp.bfloat16
    )
    grad_back = lax.all_to_all(
        back_rows.reshape(block_shape), "adapter", split_axis=0, concat_axis=0, tiled=True
    )
    branch_out = combine(onehot, out_back)
    input_grad = combine(onehot, grad_back)
    down_grad = (contract_first(low_grad, rows_in) / capacity).astype(jnp.bfloat16)[None]
    up_grad = (contract_first(low_rank, weighted) / capacity).astype(jnp.bfloat16)[None]
    return (branch_out, input_grad, down_grad, up_grad)


PLACES = 4


def on_line(pairs):
    return [(2 * a + side, 2 * b + side) for a, b in pairs for side in (0, 1)]


def xor_line(bit):
    return on_line([(a, a ^ bit) for a in range(PLACES)])


PARTNER = [(2 * a + side, 2 * a + 1 - side) for a in range(PLACES) for side in (0, 1)]
SWAP = [(0, 1), (1, 0)]
OWNERS = 2 * PLACES
FAR = xor_line(2) + [(OWNERS + a, OWNERS + b) for a, b in xor_line(3)]


def move(value, pairs):
    return lax.ppermute(value, "adapter", pairs)


def after(value, earlier):
    return lax.optimization_barrier((value, earlier))[0]


def narrow(value):
    return value.astype(jnp.bfloat16)


def add_up(*values):
    total = values[0]
    for value in values[1:]:
        total = total + value.astype(jnp.float32)
    return total


def partial_sums(weights, rows):
    parts = [jnp.dot(weight, rows, preferred_element_type=jnp.float32) for weight in weights]
    return lax.optimization_barrier((parts, [narrow(part) for part in parts[1:]]))


def both_cores(partial):
    return partial + lax.ppermute(partial, "tensor", SWAP)


def by_pairs(tokens, cotangent, down_adapter, up_adapter, token_lists, gating):
    me = lax.axis_index("adapter")
    first_group = lax.axis_index("groups") == 0
    tok_local = tokens.shape[0]
    capacity = gating.shape[1]
    down_matrix = down_adapter[0]
    up_matrix = up_adapter[0]
    rank = down_matrix.shape[0]

    far_down = lax.ppermute(down_matrix, ("groups", "adapter"), FAR)
    tokens2 = move(tokens, PARTNER)
    near_gate, down_later, up_later = lax.optimization_barrier(
        (move(gating, xor_line(1)), down_matrix, up_matrix)
    )
    near_down = move(down_later, xor_line(1))
    cot2 = move(cotangent, PARTNER)
    gates = jnp.concatenate([gating, near_gate])
    gates = jnp.concatenate([gates, move(gates, xor_line(2))])

    far_bit = jnp.where(first_group, 2, 3)
    experts = jnp.stack([me, me ^ 2, me ^ (2 * far_bit), me ^ (2 * (far_bit ^ 1))])
    lists = jnp.take(token_lists, experts, axis=0)
    crossed = jnp.concatenate([gates[:2], gates[3:], gates[2:3]])
    gate_rows = adapter_scale_factor * jnp.where(first_group, gates, crossed)
    token_ids = jnp.arange(tok_local, dtype=jnp.int32)
    ids = jnp.concatenate([me * tok_local + token_ids, (me ^ 1) * tok_local + token_ids])
    taken = lists[:, :, None] == ids[None, None, :]
    scale = jnp.sum(jnp.where(taken, gate_rows[:, :, None], 0.0), axis=1)

    far_up = lax.ppermute(up_later, ("groups", "adapter"), FAR)
    up_last, scale = lax.optimization_barrier((up_matrix, scale))
    near_up = move(up_last, xor_line(1))
    ready, scale = lax.optimization_barrier((far_down, scale))
    cross_down = lax.ppermute(ready, "groups", SWAP)
    tokens2 = jnp.concatenate([tokens, tokens2], axis=0)
    down_all = jnp.concatenate([down_matrix, near_down, far_down, cross_down], axis=0)

    def most_products(rows, *matrices):
        return both_cores(contract_last(jnp.concatenate(matrices), rows))

    def low_rank(most, rows, matrix):
        products = [most[k * rank : (k + 1) * rank] for k in range(3)]
        products.append(both_cores(contract_last(matrix, rows)))
        return [narrow(scale[k] * product) for k, product in enumerate(products)]

    def for_line(low):
        second = jnp.where(first_group, low[2], low[3])
        third = jnp.where(first_group, low[3], low[2])
        return low[0], low[1], second, third

    def outward_start(low, matrix):
        weights = jnp.concatenate([slot[:, tok_local:] for slot in low])
        return move(narrow(contract_first(weights, matrix)), PARTNER)

    def outward_end(low, matrix, back):
        weights = jnp.concatenate([slot[:, :tok_local] for slot in low])
        return narrow(contract_first(weights, matrix) + back.astype(jnp.float32))

    most = most_products(tokens2, down_matrix, near_down, far_down)
    most, tokens2 = lax.optimization_barrier((most, tokens2))
    low = low_rank(most, tokens2, cross_down)
    low, far_up = lax.optimization_barrier((low, far_up))
    *others, for_third = for_line(low)
    part = jnp.dot(for_third[:, :tok_local], cotangent, preferred_element_type=jnp.float32)
    theirs, for_third, part = lax.optimization_barrier((cot2, for_third[:, tok_local:], part))
    part = part + jnp.dot(for_third, theirs, preferred_element_type=jnp.float32)
    up_send_third = narrow(part)
    up_third = move(up_send_third, xor_line(1))
    theirs = after(theirs, up_send_third)
    cot2 = jnp.concatenate([cotangent, theirs], axis=0)
    far_up = after(far_up, up_send_third)
    cross_up = lax.ppermute(far_up, "groups", SWAP)
    most = most_products(cot2, up_matrix, near_up, far_up)
    most, rows_later = lax.optimization_barrier((most, cot2))
    (own, first, second), up_send = partial_sums(others, rows_later)
    up_first = move(up_send[0], xor_line(1))

    cross_up, up_sum = lax.optimization_barrier((cross_up, narrow(add_up(second, up_third))))
    up_far = move(up_sum, xor_line(2))
    up_all = jnp.concatenate([up_matrix, near_up, far_up, cross_up], axis=0)
    low_back = low_rank(most, cot2, cross_up)
    (own_b, first_b, second_b, third_b), down_send = partial_sums(for_line(low_back), tokens2)
    down_third = move(down_send[2], xor_line(1))
    branch_back = outward_start(low, up_all)
    input_back = outward_start(low_back, down_all)
    down_sum = narrow(add_up(second_b, down_third))
    down_far = move(down_sum, xor_line(2))
    down_first = move(after(down_send[0], (up_first, down_sum)), xor_line(1))
    branch_out = outward_end(low, up_all, branch_back)
    up_grad = add_up(own, up_first, after(up_far, down_sum))
    input_grad = outward_end(low_back, down_all, input_back)
    input_grad, down_far = lax.optimization_barrier((input_grad, down_far))
    down_grad = add_up(own_b, down_first, down_far)
    down_grad = (down_grad / capacity).astype(jnp.bfloat16)[None]
    up_grad = (up_grad / capacity).astype(jnp.bfloat16)[None]
    return (branch_out, input_grad, down_grad, up_grad)


def local(*args):
    fits = lax.axis_size("adapter") == OWNERS and lax.axis_size("groups") == 2
    plan = by_pairs if fits else by_rows
    return plan(*args)


def solution(mesh):
    in_specs = (
        P(("groups", "adapter"), "tensor"),
        P(("groups", "adapter"), "tensor"),
        P("adapter", None, "tensor"),
        P("adapter", None, "tensor"),
        P("groups", None),
        P(("groups", "adapter"), None),
    )
    out_specs = (
        P(("groups", "adapter"), "tensor"),
        P(("groups", "adapter"), "tensor"),
        P(("groups", "adapter"), None, "tensor"),
        P(("groups", "adapter"), None, "tensor"),
    )
    return jax.shard_map(local, mesh=mesh, in_specs=in_specs, out_specs=out_specs, check_vma=False)
```

```python
import jax
import jax.numpy as jnp
from jax import lax
from jax.sharding import PartitionSpec as P

adapter_scale_factor = 2.0


def contract_last(left_op, right_op):
    return lax.dot_general(
        left_op, right_op, (((1,), (1,)), ((), ())), preferred_element_type=jnp.float32
    )


def contract_first(left_op, right_op):
    return lax.dot_general(
        left_op, right_op, (((0,), (0,)), ((), ())), preferred_element_type=jnp.float32
    )


def gather_rows(source_rows, local_index, live_slot):
    taken_rows = jnp.take(source_rows, local_index.reshape(-1), axis=0)
    taken_rows = taken_rows.reshape(local_index.shape + (source_rows.shape[1],))
    return jnp.where(live_slot[:, :, None], taken_rows, jnp.zeros_like(taken_rows))


def combine(onehot, returned):
    flat_rows = returned.reshape(-1, returned.shape[-1])
    return jnp.dot(onehot, flat_rows, preferred_element_type=jnp.float32).astype(jnp.bfloat16)


def by_rows(tokens, cotangent, down_adapter, up_adapter, token_lists, gating):
    owners = lax.axis_size("adapter")
    my_index = lax.axis_index("adapter")
    tok_local = tokens.shape[0]
    half_width = tokens.shape[1]
    capacity = gating.shape[1]
    slot_count = 3 * capacity // (2 * owners)
    slot_ids = jnp.arange(slot_count, dtype=jnp.int32)
    source = token_lists // tok_local
    sent_count = jnp.sum((source == my_index).astype(jnp.int32), axis=1)
    sent_start = jnp.sum((source < my_index).astype(jnp.int32), axis=1)
    live_send = slot_ids[None, :] < sent_count[:, None]
    position = jnp.minimum(sent_start[:, None] + slot_ids[None, :], capacity - 1)
    local_index = jnp.take_along_axis(token_lists, position, axis=1) - my_index * tok_local
    local_index = jnp.where(live_send, local_index, 0)
    outgoing_rows = gather_rows(tokens, local_index, live_send)
    cot_send = gather_rows(cotangent, local_index, live_send)
    token_ids = jnp.arange(tok_local, dtype=jnp.int32)
    onehot = ((token_ids[:, None] == local_index.reshape(1, -1)) & live_send.reshape(1, -1)).astype(
        jnp.bfloat16
    )
    own_list = lax.dynamic_slice_in_dim(token_lists, my_index, 1, 0)[0]
    own_source = own_list // tok_local
    peer_ids = jnp.arange(owners, dtype=jnp.int32)
    recv_count = jnp.sum((own_source[None, :] == peer_ids[:, None]).astype(jnp.int32), axis=1)
    received_offset = jnp.sum((own_source[None, :] < peer_ids[:, None]).astype(jnp.int32), axis=1)
    active_received = slot_ids[None, :] < recv_count[:, None]
    gate_pos = jnp.minimum(received_offset[:, None] + slot_ids[None, :], capacity - 1)
    gate_slot_values = jnp.take(gating[0], gate_pos.reshape(-1)).reshape(gate_pos.shape)
    scale_factors = (
        adapter_scale_factor * jnp.where(active_received, gate_slot_values, 0.0)
    ).reshape(-1, 1)
    down_matrix = down_adapter[0]
    up_matrix = up_adapter[0]
    flat_shape = (owners * slot_count, half_width)
    block_shape = (owners, slot_count, half_width)
    row_recv = lax.all_to_all(outgoing_rows, "adapter", split_axis=0, concat_axis=0, tiled=True)
    rows_in = row_recv.reshape(flat_shape)
    low_rank = lax.psum(contract_last(rows_in, down_matrix), "tensor").astype(jnp.bfloat16)
    out_rows = (
        scale_factors * jnp.dot(low_rank, up_matrix, preferred_element_type=jnp.float32)
    ).astype(jnp.bfloat16)
    out_back = lax.all_to_all(
        out_rows.reshape(block_shape), "adapter", split_axis=0, concat_axis=0, tiled=True
    )
    cot_recv = lax.all_to_all(cot_send, "adapter", split_axis=0, concat_axis=0, tiled=True)
    weighted = (scale_factors * cot_recv.reshape(flat_shape)).astype(jnp.bfloat16)
    low_grad = lax.psum(contract_last(weighted, up_matrix), "tensor").astype(jnp.bfloat16)
    back_rows = jnp.dot(low_grad, down_matrix, preferred_element_type=jnp.float32).astype(
        jnp.bfloat16
    )
    grad_back = lax.all_to_all(
        back_rows.reshape(block_shape), "adapter", split_axis=0, concat_axis=0, tiled=True
    )
    branch_out = combine(onehot, out_back)
    input_grad = combine(onehot, grad_back)
    down_grad = (contract_first(low_grad, rows_in) / capacity).astype(jnp.bfloat16)[None]
    up_grad = (contract_first(low_rank, weighted) / capacity).astype(jnp.bfloat16)[None]
    return (branch_out, input_grad, down_grad, up_grad)


PLACES = 4


def on_line(pairs):
    return [(2 * a + side, 2 * b + side) for a, b in pairs for side in (0, 1)]


def xor_line(bit):
    return on_line([(a, a ^ bit) for a in range(PLACES)])


PARTNER = [(2 * a + side, 2 * a + 1 - side) for a in range(PLACES) for side in (0, 1)]
SWAP = [(0, 1), (1, 0)]
OWNERS = 2 * PLACES
FAR = xor_line(2) + [(OWNERS + a, OWNERS + b) for a, b in xor_line(3)]


def move(value, pairs):
    return lax.ppermute(value, "adapter", pairs)


def after(value, earlier):
    return lax.optimization_barrier((value, earlier))[0]


def narrow(value):
    return value.astype(jnp.bfloat16)


def add_up(*values):
    total = values[0]
    for value in values[1:]:
        total = total + value.astype(jnp.float32)
    return total


def partial_sums(weights, rows):
    parts = [jnp.dot(weight, rows, preferred_element_type=jnp.float32) for weight in weights]
    return lax.optimization_barrier((parts, [narrow(part) for part in parts[1:]]))


def both_cores(partial):
    return partial + lax.ppermute(partial, "tensor", SWAP)


def by_pairs(tokens, cotangent, down_adapter, up_adapter, token_lists, gating):
    me = lax.axis_index("adapter")
    first_group = lax.axis_index("groups") == 0
    tok_local = tokens.shape[0]
    capacity = gating.shape[1]
    down_matrix = down_adapter[0]
    up_matrix = up_adapter[0]
    rank = down_matrix.shape[0]

    far_down = lax.ppermute(down_matrix, ("groups", "adapter"), FAR)
    tokens2 = move(tokens, PARTNER)
    near_gate, down_later, up_later = lax.optimization_barrier(
        (move(gating, xor_line(1)), down_matrix, up_matrix)
    )
    near_down = move(down_later, xor_line(1))
    cot2 = move(cotangent, PARTNER)
    gates = jnp.concatenate([gating, near_gate])
    gates = jnp.concatenate([gates, move(gates, xor_line(2))])

    far_bit = jnp.where(first_group, 2, 3)
    experts = jnp.stack([me, me ^ 2, me ^ (2 * far_bit), me ^ (2 * (far_bit ^ 1))])
    lists = jnp.take(token_lists, experts, axis=0)
    crossed = jnp.concatenate([gates[:2], gates[3:], gates[2:3]])
    gate_rows = adapter_scale_factor * jnp.where(first_group, gates, crossed)
    token_ids = jnp.arange(tok_local, dtype=jnp.int32)
    ids = jnp.concatenate([me * tok_local + token_ids, (me ^ 1) * tok_local + token_ids])
    taken = lists[:, :, None] == ids[None, None, :]
    scale = jnp.sum(jnp.where(taken, gate_rows[:, :, None], 0.0), axis=1)

    far_up = lax.ppermute(up_later, ("groups", "adapter"), FAR)
    up_last, scale = lax.optimization_barrier((up_matrix, scale))
    near_up = move(up_last, xor_line(1))
    ready, scale = lax.optimization_barrier((far_down, scale))
    cross_down = lax.ppermute(ready, "groups", SWAP)
    tokens2 = jnp.concatenate([tokens, tokens2], axis=0)
    down_all = jnp.concatenate([down_matrix, near_down, far_down, cross_down], axis=0)

    def most_products(rows, *matrices):
        return both_cores(contract_last(jnp.concatenate(matrices), rows))

    def low_rank(most, rows, matrix):
        products = [most[k * rank : (k + 1) * rank] for k in range(3)]
        products.append(both_cores(contract_last(matrix, rows)))
        return [narrow(scale[k] * product) for k, product in enumerate(products)]

    def for_line(low):
        second = jnp.where(first_group, low[2], low[3])
        third = jnp.where(first_group, low[3], low[2])
        return low[0], low[1], second, third

    def outward_start(low, matrix):
        weights = jnp.concatenate([slot[:, tok_local:] for slot in low])
        return move(narrow(contract_first(weights, matrix)), PARTNER)

    def outward_end(low, matrix, back):
        weights = jnp.concatenate([slot[:, :tok_local] for slot in low])
        return narrow(contract_first(weights, matrix) + back.astype(jnp.float32))

    most = most_products(tokens2, down_matrix, near_down, far_down)
    most, tokens2 = lax.optimization_barrier((most, tokens2))
    low = low_rank(most, tokens2, cross_down)
    cot2, low = lax.optimization_barrier((cot2, low))
    cot2 = jnp.concatenate([cotangent, cot2], axis=0)
    *others, for_third = for_line(low)
    up_send_third = narrow(jnp.dot(for_third, cot2, preferred_element_type=jnp.float32))
    up_third = move(up_send_third, xor_line(1))
    far_up = after(far_up, up_send_third)
    cross_up = lax.ppermute(far_up, "groups", SWAP)
    most = most_products(cot2, up_matrix, near_up, far_up)
    most, rows_later = lax.optimization_barrier((most, cot2))
    (own, first, second), up_send = partial_sums(others, rows_later)

    cross_up, up_sum = lax.optimization_barrier((cross_up, narrow(add_up(second, up_third))))
    up_far = move(up_sum, xor_line(2))
    up_all = jnp.concatenate([up_matrix, near_up, far_up, cross_up], axis=0)
    low_back = low_rank(most, cot2, cross_up)
    (own_b, first_b, second_b, third_b), down_send = partial_sums(for_line(low_back), tokens2)
    down_third = move(down_send[2], xor_line(1))
    up_later, down_send = lax.optimization_barrier((up_send[0], down_send))
    up_first = move(up_later, xor_line(1))
    branch_back = outward_start(low, up_all)
    input_back = outward_start(low_back, down_all)
    down_sum = narrow(add_up(second_b, down_third))
    down_far = move(down_sum, xor_line(2))
    down_first = move(after(down_send[0], down_sum), xor_line(1))
    branch_out = outward_end(low, up_all, branch_back)
    up_grad = add_up(own, up_first, after(up_far, down_sum))
    input_grad = outward_end(low_back, down_all, input_back)
    input_grad, down_far = lax.optimization_barrier((input_grad, down_far))
    down_grad = add_up(own_b, down_first, down_far)
    down_grad = (down_grad / capacity).astype(jnp.bfloat16)[None]
    up_grad = (up_grad / capacity).astype(jnp.bfloat16)[None]
    return (branch_out, input_grad, down_grad, up_grad)


def local(*args):
    fits = lax.axis_size("adapter") == OWNERS and lax.axis_size("groups") == 2
    plan = by_pairs if fits else by_rows
    return plan(*args)


def solution(mesh):
    in_specs = (
        P(("groups", "adapter"), "tensor"),
        P(("groups", "adapter"), "tensor"),
        P("adapter", None, "tensor"),
        P("adapter", None, "tensor"),
        P("groups", None),
        P(("groups", "adapter"), None),
    )
    out_specs = (
        P(("groups", "adapter"), "tensor"),
        P(("groups", "adapter"), "tensor"),
        P(("groups", "adapter"), None, "tensor"),
        P(("groups", "adapter"), None, "tensor"),
    )
    return jax.shard_map(local, mesh=mesh, in_specs=in_specs, out_specs=out_specs, check_vma=False)
```

```python
import jax
import jax.numpy as jnp
from jax import lax
from jax.sharding import PartitionSpec as P

adapter_scale_factor = 2.0


def contract_last(left_op, right_op):
    return lax.dot_general(
        left_op, right_op, (((1,), (1,)), ((), ())), preferred_element_type=jnp.float32
    )


def contract_first(left_op, right_op):
    return lax.dot_general(
        left_op, right_op, (((0,), (0,)), ((), ())), preferred_element_type=jnp.float32
    )


def gather_rows(source_rows, local_index, live_slot):
    taken_rows = jnp.take(source_rows, local_index.reshape(-1), axis=0)
    taken_rows = taken_rows.reshape(local_index.shape + (source_rows.shape[1],))
    return jnp.where(live_slot[:, :, None], taken_rows, jnp.zeros_like(taken_rows))


def combine(onehot, returned):
    flat_rows = returned.reshape(-1, returned.shape[-1])
    return jnp.dot(onehot, flat_rows, preferred_element_type=jnp.float32).astype(jnp.bfloat16)


def by_rows(tokens, cotangent, down_adapter, up_adapter, token_lists, gating):
    owners = lax.axis_size("adapter")
    my_index = lax.axis_index("adapter")
    tok_local = tokens.shape[0]
    half_width = tokens.shape[1]
    capacity = gating.shape[1]
    slot_count = 3 * capacity // (2 * owners)
    slot_ids = jnp.arange(slot_count, dtype=jnp.int32)
    source = token_lists // tok_local
    sent_count = jnp.sum((source == my_index).astype(jnp.int32), axis=1)
    sent_start = jnp.sum((source < my_index).astype(jnp.int32), axis=1)
    live_send = slot_ids[None, :] < sent_count[:, None]
    position = jnp.minimum(sent_start[:, None] + slot_ids[None, :], capacity - 1)
    local_index = jnp.take_along_axis(token_lists, position, axis=1) - my_index * tok_local
    local_index = jnp.where(live_send, local_index, 0)
    outgoing_rows = gather_rows(tokens, local_index, live_send)
    cot_send = gather_rows(cotangent, local_index, live_send)
    token_ids = jnp.arange(tok_local, dtype=jnp.int32)
    onehot = ((token_ids[:, None] == local_index.reshape(1, -1)) & live_send.reshape(1, -1)).astype(
        jnp.bfloat16
    )
    own_list = lax.dynamic_slice_in_dim(token_lists, my_index, 1, 0)[0]
    own_source = own_list // tok_local
    peer_ids = jnp.arange(owners, dtype=jnp.int32)
    recv_count = jnp.sum((own_source[None, :] == peer_ids[:, None]).astype(jnp.int32), axis=1)
    received_offset = jnp.sum((own_source[None, :] < peer_ids[:, None]).astype(jnp.int32), axis=1)
    active_received = slot_ids[None, :] < recv_count[:, None]
    gate_pos = jnp.minimum(received_offset[:, None] + slot_ids[None, :], capacity - 1)
    gate_slot_values = jnp.take(gating[0], gate_pos.reshape(-1)).reshape(gate_pos.shape)
    scale_factors = (
        adapter_scale_factor * jnp.where(active_received, gate_slot_values, 0.0)
    ).reshape(-1, 1)
    down_matrix = down_adapter[0]
    up_matrix = up_adapter[0]
    flat_shape = (owners * slot_count, half_width)
    block_shape = (owners, slot_count, half_width)
    row_recv = lax.all_to_all(outgoing_rows, "adapter", split_axis=0, concat_axis=0, tiled=True)
    rows_in = row_recv.reshape(flat_shape)
    low_rank = lax.psum(contract_last(rows_in, down_matrix), "tensor").astype(jnp.bfloat16)
    out_rows = (
        scale_factors * jnp.dot(low_rank, up_matrix, preferred_element_type=jnp.float32)
    ).astype(jnp.bfloat16)
    out_back = lax.all_to_all(
        out_rows.reshape(block_shape), "adapter", split_axis=0, concat_axis=0, tiled=True
    )
    cot_recv = lax.all_to_all(cot_send, "adapter", split_axis=0, concat_axis=0, tiled=True)
    weighted = (scale_factors * cot_recv.reshape(flat_shape)).astype(jnp.bfloat16)
    low_grad = lax.psum(contract_last(weighted, up_matrix), "tensor").astype(jnp.bfloat16)
    back_rows = jnp.dot(low_grad, down_matrix, preferred_element_type=jnp.float32).astype(
        jnp.bfloat16
    )
    grad_back = lax.all_to_all(
        back_rows.reshape(block_shape), "adapter", split_axis=0, concat_axis=0, tiled=True
    )
    branch_out = combine(onehot, out_back)
    input_grad = combine(onehot, grad_back)
    down_grad = (contract_first(low_grad, rows_in) / capacity).astype(jnp.bfloat16)[None]
    up_grad = (contract_first(low_rank, weighted) / capacity).astype(jnp.bfloat16)[None]
    return (branch_out, input_grad, down_grad, up_grad)


PLACES = 4


def on_line(pairs):
    return [(2 * a + side, 2 * b + side) for a, b in pairs for side in (0, 1)]


def xor_line(bit):
    return on_line([(a, a ^ bit) for a in range(PLACES)])


PARTNER = [(2 * a + side, 2 * a + 1 - side) for a in range(PLACES) for side in (0, 1)]
SWAP = [(0, 1), (1, 0)]
OWNERS = 2 * PLACES
FAR = xor_line(2) + [(OWNERS + a, OWNERS + b) for a, b in xor_line(3)]


def move(value, pairs):
    return lax.ppermute(value, "adapter", pairs)


def after(value, earlier):
    return lax.optimization_barrier((value, earlier))[0]


def narrow(value):
    return value.astype(jnp.bfloat16)


def add_up(*values):
    total = values[0]
    for value in values[1:]:
        total = total + value.astype(jnp.float32)
    return total


def partial_sums(weights, rows):
    parts = [jnp.dot(weight, rows, preferred_element_type=jnp.float32) for weight in weights]
    return lax.optimization_barrier((parts, [narrow(part) for part in parts[1:]]))


def both_cores(partial):
    return partial + lax.ppermute(partial, "tensor", SWAP)


def by_pairs(tokens, cotangent, down_adapter, up_adapter, token_lists, gating):
    me = lax.axis_index("adapter")
    first_group = lax.axis_index("groups") == 0
    tok_local = tokens.shape[0]
    capacity = gating.shape[1]
    down_matrix = down_adapter[0]
    up_matrix = up_adapter[0]
    rank = down_matrix.shape[0]

    tokens2 = move(tokens, PARTNER)
    near_gate, down_later, up_later = lax.optimization_barrier(
        (move(gating, xor_line(1)), down_matrix, up_matrix)
    )
    far_down = lax.ppermute(down_later, ("groups", "adapter"), FAR)
    near_down = move(down_later, xor_line(1))
    cot2 = move(cotangent, PARTNER)
    gates = jnp.concatenate([gating, near_gate])
    gates = jnp.concatenate([gates, move(gates, xor_line(2))])

    far_bit = jnp.where(first_group, 2, 3)
    experts = jnp.stack([me, me ^ 2, me ^ (2 * far_bit), me ^ (2 * (far_bit ^ 1))])
    lists = jnp.take(token_lists, experts, axis=0)
    crossed = jnp.concatenate([gates[:2], gates[3:], gates[2:3]])
    gate_rows = adapter_scale_factor * jnp.where(first_group, gates, crossed)
    token_ids = jnp.arange(tok_local, dtype=jnp.int32)
    ids = jnp.concatenate([me * tok_local + token_ids, (me ^ 1) * tok_local + token_ids])
    taken = lists[:, :, None] == ids[None, None, :]
    scale = jnp.sum(jnp.where(taken, gate_rows[:, :, None], 0.0), axis=1)

    far_up = lax.ppermute(up_later, ("groups", "adapter"), FAR)
    up_last, scale = lax.optimization_barrier((up_matrix, scale))
    near_up = move(up_last, xor_line(1))
    ready, scale = lax.optimization_barrier((far_down, scale))
    cross_down = lax.ppermute(ready, "groups", SWAP)
    tokens2 = jnp.concatenate([tokens, tokens2], axis=0)
    down_all = jnp.concatenate([down_matrix, near_down, far_down, cross_down], axis=0)

    def most_products(rows, *matrices):
        return both_cores(contract_last(jnp.concatenate(matrices), rows))

    def low_rank(most, rows, matrix):
        products = [most[k * rank : (k + 1) * rank] for k in range(3)]
        products.append(both_cores(contract_last(matrix, rows)))
        return [narrow(scale[k] * product) for k, product in enumerate(products)]

    def for_line(low):
        second = jnp.where(first_group, low[2], low[3])
        third = jnp.where(first_group, low[3], low[2])
        return low[0], low[1], second, third

    def outward_start(low, matrix):
        weights = jnp.concatenate([slot[:, tok_local:] for slot in low])
        return move(narrow(contract_first(weights, matrix)), PARTNER)

    def outward_end(low, matrix, back):
        weights = jnp.concatenate([slot[:, :tok_local] for slot in low])
        return narrow(contract_first(weights, matrix) + back.astype(jnp.float32))

    most = most_products(tokens2, down_matrix, near_down, far_down)
    most, tokens2 = lax.optimization_barrier((most, tokens2))
    low = low_rank(most, tokens2, cross_down)
    cot2, low = lax.optimization_barrier((cot2, low))
    cot2 = jnp.concatenate([cotangent, cot2], axis=0)
    *others, for_third = for_line(low)
    up_send_third = narrow(jnp.dot(for_third, cot2, preferred_element_type=jnp.float32))
    up_third = move(up_send_third, xor_line(1))
    far_up = after(far_up, up_send_third)
    cross_up = lax.ppermute(far_up, "groups", SWAP)
    most = most_products(cot2, up_matrix, near_up, far_up)
    most, rows_later = lax.optimization_barrier((most, cot2))
    (own, first, second), up_send = partial_sums(others, rows_later)
    up_first = move(up_send[0], xor_line(1))

    cross_up, up_sum = lax.optimization_barrier((cross_up, narrow(add_up(second, up_third))))
    up_far = move(up_sum, xor_line(2))
    up_all = jnp.concatenate([up_matrix, near_up, far_up, cross_up], axis=0)
    low_back = low_rank(most, cot2, cross_up)
    (own_b, first_b, second_b, third_b), down_send = partial_sums(for_line(low_back), tokens2)
    down_third = move(down_send[2], xor_line(1))
    branch_back = outward_start(low, up_all)
    input_back = outward_start(low_back, down_all)
    down_sum = narrow(add_up(second_b, down_third))
    down_far = move(down_sum, xor_line(2))
    down_first = move(after(down_send[0], (up_first, down_sum)), xor_line(1))
    branch_out = outward_end(low, up_all, branch_back)
    up_grad = add_up(own, up_first, after(up_far, down_sum))
    input_grad = outward_end(low_back, down_all, input_back)
    input_grad, down_far = lax.optimization_barrier((input_grad, down_far))
    down_grad = add_up(own_b, down_first, down_far)
    down_grad = (down_grad / capacity).astype(jnp.bfloat16)[None]
    up_grad = (up_grad / capacity).astype(jnp.bfloat16)[None]
    return (branch_out, input_grad, down_grad, up_grad)


def local(*args):
    fits = lax.axis_size("adapter") == OWNERS and lax.axis_size("groups") == 2
    plan = by_pairs if fits else by_rows
    return plan(*args)


def solution(mesh):
    in_specs = (
        P(("groups", "adapter"), "tensor"),
        P(("groups", "adapter"), "tensor"),
        P("adapter", None, "tensor"),
        P("adapter", None, "tensor"),
        P("groups", None),
        P(("groups", "adapter"), None),
    )
    out_specs = (
        P(("groups", "adapter"), "tensor"),
        P(("groups", "adapter"), "tensor"),
        P(("groups", "adapter"), None, "tensor"),
        P(("groups", "adapter"), None, "tensor"),
    )
    return jax.shard_map(local, mesh=mesh, in_specs=in_specs, out_specs=out_specs, check_vma=False)
```
